32 devices in a mesh: dp: 8 (over z, y), tensor: 4 (over x, core).
Axes of the slice: x: 2, y: 2, z: 4, core: 2. Of those that a mesh axis runs over, the one named last changes fastest.
Arguments:
- tokens: bfloat16 [16384, 1280], P(('dp', 'tensor')), may hold values from -6 to 6
- cotangent: bfloat16 [16384, 1280], P(('dp', 'tensor')), may hold values from -6 to 6
- lengths: int32 [16], P('dp'), may hold values from 256 to 1024, as said below
- key_mask: int32 [16, 1024], P('dp'), may hold values 0 or 1
- qkv_weight: float32 [1280, 3, 1280], P('dp', None, 'tensor'), may hold values from -0.15625 to 0.15625
- out_weight: float32 [1280, 1280], P(('tensor', 'dp')), may hold values from -4 to 4
- up_weight: float32 [1280, 5120], P('dp', 'tensor'), may hold values from -0.15625 to 0.15625
- down_weight: float32 [5120, 1280], P(('tensor', 'dp')), may hold values from -0.078125 to 0.078125
- norm_params: float32 [4, 1280], P(None, 'dp')
- qkv_first: float32 [1280, 3, 1280], P('dp', None, 'tensor'), may hold values from -0.001953125 to 0.001953125
- qkv_second: float32 [1280, 3, 1280], P('dp', None, 'tensor'), may hold values from 5.493164e-08 to 9.155273e-07
- out_first: float32 [1280, 1280], P(('tensor', 'dp')), may hold values from -0.00010681152 to 0.00010681152
- out_second: float32 [1280, 1280], P(('tensor', 'dp')), may hold values from 1.4038086e-10 to 2.2583009e-09
- up_first: float32 [1280, 5120], P('dp', 'tensor'), may hold values from -0.00024414062 to 0.00024414062
- up_second: float32 [1280, 5120], P('dp', 'tensor'), may hold values from 1.1596679e-09 to 4.577637e-09
- down_first: float32 [5120, 1280], P(('tensor', 'dp')), may hold values from -0.0004272461 to 0.0004272461
- down_second: float32 [5120, 1280], P(('tensor', 'dp')), may hold values from 3.2958984e-09 to 1.3183594e-08
- norm_first: float32 [4, 1280], P(None, 'dp'), may hold values from -0.0029296875 to 0.0029296875
- norm_second: float32 [4, 1280], P(None, 'dp'), may hold values from 1.2207032e-07 to 2.0141601e-06
Outputs:
- layer_out: bfloat16 [16384, 1280], P(('dp', 'tensor'))
- input_grad: bfloat16 [16384, 1280], P(('dp', 'tensor'))
- grad_norm: float32 [], replicated
- qkv_new: float32 [1280, 3, 1280], P('dp', None, 'tensor')
- qkv_first_new: float32 [1280, 3, 1280], P('dp', None, 'tensor')
- qkv_second_new: float32 [1280, 3, 1280], P('dp', None, 'tensor')
- out_new: float32 [1280, 1280], P(('tensor', 'dp'))
- out_first_new: float32 [1280, 1280], P(('tensor', 'dp'))
- out_second_new: float32 [1280, 1280], P(('tensor', 'dp'))
- up_new: float32 [1280, 5120], P('dp', 'tensor')
- up_first_new: float32 [1280, 5120], P('dp', 'tensor')
- up_second_new: float32 [1280, 5120], P('dp', 'tensor')
- down_new: float32 [5120, 1280], P(('tensor', 'dp'))
- down_first_new: float32 [5120, 1280], P(('tensor', 'dp'))
- down_second_new: float32 [5120, 1280], P(('tensor', 'dp'))
- norm_new: float32 [4, 1280], P(None, 'dp')
- norm_first_new: float32 [4, 1280], P(None, 'dp')
- norm_second_new: float32 [4, 1280], P(None, 'dp')
- shift_grad: float32 [1280], P('dp')
The draws below stay inside these ranges and needn't reach their ends.
Inputs may be any that keep to these rules, and one draw needn't show every extreme that they name: `lengths`: tokens that count in each cell, from its first position; some cell has all 1024 in every draw.
All inputs are finite; a program needn't handle non-finite values. No bound on the sum of `key_mask` on one device may be relied on, other than what follows from the above.
Results may differ from the reference program's by a relative error of at most 0.02.
Values may be sent and summed in bfloat16 or wider, within the bound.
No kernel may reach another device: no remote copies, remote signals or barrier semaphores. Data moves between devices by JAX's collectives and lax.ppermute only.
A program may use at most 192 MiB of HBM per device.

```python
import math
import jax
import jax.numpy as jnp
from jax import lax

D = 1280
H = 20
FF = 5120
HD = 64
L = 1024
STEP = 5
CELLS = 16
TOKENS = 16384
N_TENSOR = 4


def draw_lengths(key, part):
    key = jax.random.fold_in(key, 11)
    key_draw, key_pick = jax.random.split(key)
    sampled = jax.random.randint(key_draw, (CELLS,), L // 4, L + 1)
    longest = jax.random.randint(key_pick, (), 0, CELLS)
    return jnp.where(jnp.arange(CELLS) == longest, L, sampled).astype(jnp.int32)


def draw_norm_params(key, part):
    key = jax.random.fold_in(key, 23)
    key_gain, key_shift = jax.random.split(key)
    column = jnp.arange(D, dtype=jnp.float32) / D
    rising = 0.6 + 1.2 * column
    factor = jax.random.uniform(key_gain, (2, D), jnp.float32, 0.8, 1.2)
    shifts = 0.3 * jax.random.normal(key_shift, (2, D), jnp.float32)
    gain_rows = rising[None, :] * factor
    return jnp.stack([gain_rows[0], shifts[0], gain_rows[1], shifts[1]]).astype(jnp.float32)


def place_ends(array, own_key, low, top_value):
    extent = array.shape
    place = [jax.random.randint(jax.random.fold_in(own_key, axis), (), 0, extent[axis]) for axis in range(len(extent))]
    array = array.at[tuple(place)].set(low)
    longest = extent.index(max(extent))
    place[longest] = (place[longest] + 1) % extent[longest]
    return array.at[tuple(place)].set(top_value)


def block_scale(stream_key, extent, cuts, smallest, top_value):
    def one(axis_at, parts):
        heights = jax.random.uniform(jax.random.fold_in(jax.random.fold_in(stream_key, 6), axis_at), (parts,), jnp.float32, smallest / len(cuts), top_value / len(cuts))
        return jnp.repeat(jnp.exp(heights), extent[axis_at] // parts).reshape((-1,) + (1,) * (len(extent) - axis_at - 1))

    factor_of = one(*cuts[0])
    for cut in cuts[1:]:
        factor_of = factor_of * one(*cut)
    return factor_of


def gaussian(key, shape, spread, most, cuts=(), held_as=jnp.bfloat16):
    entries = spread * jax.random.normal(key, shape, jnp.float32)
    if cuts:
        entries = entries * block_scale(key, shape, cuts, -0.22, 0.18)
    return jnp.clip(entries, -most, most).astype(held_as)


def setup_inputs(seed: int = 0) -> dict:
    key_of = jax.random.split(jax.random.key(seed), 20)
    return {
        "tokens": gaussian(key_of[0], (TOKENS, D), 1.0, 6.0, ((0, 32),)),
        "cotangent": gaussian(key_of[1], (TOKENS, D), 1.0, 6.0, ((0, 32),)),
        "lengths": draw_lengths(jax.random.fold_in(key_of[19], 71), 0),
        "key_mask": place_ends((jax.random.randint(key_of[3], (CELLS, L), 0, 8) < 7).astype(jnp.int32), jax.random.fold_in(key_of[3], 1), 0, 1),
        "qkv_weight": gaussian(key_of[4], (D, 3, D), D ** -0.5, 0.15625, ((0, 8), (2, 4)), jnp.float32),
        "out_weight": gaussian(key_of[5], (D, D), (max(1, 2 * D // L)) ** -0.5, 4.0, ((0, 32),), jnp.float32),
        "up_weight": gaussian(key_of[6], (D, FF), D ** -0.5, 0.15625, ((0, 8), (1, 4)), jnp.float32),
        "down_weight": gaussian(key_of[7], (FF, D), FF ** -0.5, 0.078125, ((0, 32),), jnp.float32),
        "norm_params": draw_norm_params(jax.random.fold_in(key_of[19], 71), 0),
        "qkv_first": gaussian(key_of[9], (D, 3, D), (0.43 * D ** -1), 0.001953125, ((0, 8), (2, 4)), jnp.float32),
        "qkv_second": jnp.clip(jnp.exp(math.log(9.155273232863692e-07) - 2.8134107 * jax.random.uniform(key_of[10], (D, 3, D), jnp.float32) ** block_scale(key_of[10], (D, 3, D), ((0, 8), (2, 4)), -0.2, 0.2)), 5.493163968139925e-08, 9.155273232863692e-07),
        "out_first": gaussian(key_of[11], (D, D), (0.022 * D ** -1), 0.00010681152, ((0, 32),), jnp.float32),
        "out_second": jnp.clip(jnp.exp(math.log(2.258300879631747e-09) - 2.778009 * jax.random.uniform(key_of[12], (D, D), jnp.float32) ** block_scale(key_of[12], (D, D), ((0, 32),), -0.2, 0.2)), 1.403808597144618e-10, 2.258300879631747e-09),
        "up_first": gaussian(key_of[13], (D, FF), (0.056 * D ** -1), 0.00024414062, ((0, 8), (1, 4)), jnp.float32),
        "up_second": jnp.clip(jnp.exp(math.log(4.577636936176077e-09) - 1.3730492 * jax.random.uniform(key_of[14], (D, FF), jnp.float32) ** block_scale(key_of[14], (D, FF), ((0, 8), (1, 4)), -0.2, 0.2)), 1.1596679172498625e-09, 4.577636936176077e-09),
        "down_first": gaussian(key_of[15], (FF, D), (0.095 * D ** -1), 0.0004272461, ((0, 32),), jnp.float32),
        "down_second": jnp.clip(jnp.exp(math.log(1.3183593772225777e-08) - 1.3862944 * jax.random.uniform(key_of[16], (FF, D), jnp.float32) ** block_scale(key_of[16], (FF, D), ((0, 32),), -0.2, 0.2)), 3.295898443056444e-09, 1.3183593772225777e-08),
        "norm_first": gaussian(key_of[17], (4, D), (0.65 * D ** -1), 0.0029296875, ((1, 8),), jnp.float32),
        "norm_second": jnp.clip(jnp.exp(math.log(2.0141601453360636e-06) - 2.8033603 * jax.random.uniform(key_of[18], (4, D), jnp.float32) ** block_scale(key_of[18], (4, D), ((1, 8),), -0.2, 0.2)), 1.2207031829802872e-07, 2.0141601453360636e-06),
    }


@jax.custom_vjp
def low(v):
    return lax.optimization_barrier(v.astype(jnp.bfloat16)).astype(jnp.float32)

@jax.custom_vjp
def low_back(v):
    return v

def low_keep(v):
    return (low(v), None)

def low_pass(kept, grad):
    return (grad,)

def back_keep(v):
    return (v, None)

def back_low(kept, grad):
    return (low(grad),)
low.defvjp(low_keep, low_pass)
low_back.defvjp(back_keep, back_low)
PRECISE = lax.Precision.HIGHEST
NORM_EPS = 1e-05
CLIP_LIMIT = 1.0
BETA_FIRST = 0.5
BETA_SECOND = 0.5
ADAM_EPS = 1e-08
DECAY_RATE = 0.01
RATE_QKV = 0.03
RATE_OUT = 0.5
RATE_UP = 0.03
RATE_DOWN = 0.015
RATE_NORM = 0.2

def layer_norm(values, gain_row, shift_row):
    centered = values - lax.optimization_barrier(jnp.mean(values, axis=-1, keepdims=True))
    inverse = lax.rsqrt(lax.optimization_barrier(jnp.mean(centered * centered, axis=-1, keepdims=True)) + NORM_EPS)
    return centered * inverse * gain_row + shift_row

def cell_attention(packed):
    qkv_cell, valid_cell = packed
    queries = qkv_cell[:, 0]
    key_rows = qkv_cell[:, 1]
    values = qkv_cell[:, 2]
    scores = low_back(jnp.einsum('qhe,khe->hqk', queries, key_rows, precision=PRECISE) * HD ** (-0.5))
    masked = jnp.where(valid_cell[None, None, :], scores, -1e+30)
    row_max = lax.optimization_barrier(jnp.max(masked, axis=-1, keepdims=True))
    log_total = row_max + jnp.log(lax.optimization_barrier(jnp.sum(jnp.exp(masked - row_max), axis=-1, keepdims=True)))
    weights = low(jnp.exp(masked - log_total))
    return jnp.einsum('hqk,khe->qhe', weights, values, precision=PRECISE)

def grouped_sum(left, right):
    inner = left.shape[1] // N_TENSOR
    total = jnp.zeros((left.shape[0], right.shape[1]), jnp.float32)
    for group in range(N_TENSOR):
        piece = jnp.dot(left[:, group * inner:(group + 1) * inner], right[group * inner:(group + 1) * inner], precision=PRECISE)
        total = total + low(piece)
    return total

def grouped_columns(normed, weight_low):
    width = weight_low.shape[-1] // N_TENSOR
    pieces = []
    for group in range(N_TENSOR):
        copied = low_back(normed)
        pieces.append(jnp.tensordot(copied, weight_low[..., group * width:(group + 1) * width], axes=1, precision=PRECISE))
    return jnp.concatenate(pieces, axis=-1)

def layer_forward(stream_in, qkv_master, out_master, up_master, down_master, norm_master, key_valid):
    qkv_low = low(qkv_master)
    out_low = low(out_master)
    up_low = low(up_master)
    down_low = low(down_master)
    norm_low = low(norm_master)
    normed_one = low(layer_norm(stream_in, norm_low[0], norm_low[1]))
    projected = low_back(low(grouped_columns(normed_one, qkv_low)))
    projected = projected.reshape(CELLS, L, 3, H, HD)
    context = lax.map(jax.checkpoint(cell_attention), (projected, key_valid))
    context = low_back(low(context.reshape(TOKENS, D)))
    residual = stream_in + low_back(grouped_sum(context, out_low))
    normed_two = low(layer_norm(residual, norm_low[2], norm_low[3]))
    hidden_pre = low_back(grouped_columns(normed_two, up_low))
    hidden = low(jax.nn.gelu(hidden_pre, approximate=False))
    return residual + low_back(grouped_sum(hidden, down_low))

def adam_update(master, grad_sum, moment_one, moment_two, step_rate, clip_factor):
    clipped = grad_sum * clip_factor
    one_new = BETA_FIRST * moment_one + (1.0 - BETA_FIRST) * clipped
    two_new = BETA_SECOND * moment_two + (1.0 - BETA_SECOND) * clipped * clipped
    one_hat = one_new / (1.0 - BETA_FIRST ** STEP)
    two_hat = two_new / (1.0 - BETA_SECOND ** STEP)
    master_new = master - step_rate * (one_hat / (jnp.sqrt(two_hat) + ADAM_EPS) + DECAY_RATE * master)
    return (master_new, one_new, two_new)

def reference(tokens, cotangent, lengths, key_mask, qkv_weight, out_weight, up_weight, down_weight, norm_params, qkv_first, qkv_second, out_first, out_second, up_first, up_second, down_first, down_second, norm_first, norm_second):
    positions = jnp.arange(L, dtype=jnp.int32)
    key_valid = (positions[None, :] < lengths[:, None]) & ((key_mask == 1) | (positions[None, :] == 0))

    def wrapped(stream_in, qkv_master, out_master, up_master, down_master, norm_master):
        return layer_forward(stream_in, qkv_master, out_master, up_master, down_master, norm_master, key_valid)
    layer_out, pullback = jax.vjp(wrapped, tokens.astype(jnp.float32), qkv_weight, out_weight, up_weight, down_weight, norm_params)
    grad_input, grad_qkv, grad_out, grad_up, grad_down, grad_norm_params = pullback(cotangent.astype(jnp.float32))
    squares_total = jnp.sum(grad_qkv * grad_qkv) + jnp.sum(grad_out * grad_out) + jnp.sum(grad_up * grad_up) + jnp.sum(grad_down * grad_down) + jnp.sum(grad_norm_params * grad_norm_params)
    grad_norm = jnp.sqrt(squares_total)
    clip_factor = jnp.minimum(1.0, CLIP_LIMIT / grad_norm)
    qkv_new, qkv_one, qkv_two = adam_update(qkv_weight, grad_qkv, qkv_first, qkv_second, RATE_QKV, clip_factor)
    out_new, out_one, out_two = adam_update(out_weight, grad_out, out_first, out_second, RATE_OUT, clip_factor)
    up_new, up_one, up_two = adam_update(up_weight, grad_up, up_first, up_second, RATE_UP, clip_factor)
    down_new, down_one, down_two = adam_update(down_weight, grad_down, down_first, down_second, RATE_DOWN, clip_factor)
    norm_new, norm_one, norm_two = adam_update(norm_params, grad_norm_params, norm_first, norm_second, RATE_NORM, clip_factor)
    shift_grad = clip_factor * grad_norm_params[3]
    return (layer_out.astype(jnp.bfloat16), grad_input.astype(jnp.bfloat16), grad_norm, qkv_new, qkv_one, qkv_two, out_new, out_one, out_two, up_new, up_one, up_two, down_new, down_one, down_two, norm_new, norm_one, norm_two, shift_grad)
```

```python
import functools

import jax
import jax.numpy as jnp
from jax import lax
from jax.experimental import pallas as pl
from jax.experimental.pallas import tpu as pltpu
from jax.sharding import PartitionSpec as P

HD = 64
STEP = 5

NORM_EPS = 1e-05
CLIP_LIMIT = 1.0
BETA_FIRST = 0.5
BETA_SECOND = 0.5
ADAM_EPS = 1e-08
DECAY_RATE = 0.01
RATE_QKV = 0.03
RATE_OUT = 0.5
RATE_UP = 0.03
RATE_DOWN = 0.015
RATE_NORM = 0.2

F32 = jnp.float32
BF16 = jnp.bfloat16
NN = (((1,), (0,)), ((), ()))
NT = (((1,), (1,)), ((), ()))
TN = (((0,), (0,)), ((), ()))
VMEM = pl.BlockSpec(memory_space=pltpu.VMEM)


def dot(left, right, dims=NN):
    return lax.dot_general(left, right, dims, preferred_element_type=F32)


def widen(block, columns, lane):
    rows = block.shape[0]
    wide = jnp.concatenate([block.astype(F32), jnp.zeros((rows, HD), F32)], axis=1)
    for n, column in enumerate(columns):
        wide = jnp.where(lane == HD + n, column, wide)
    return wide.astype(BF16)


def minus_parts(column):
    high = column.astype(BF16).astype(F32)
    rest = column - high
    middle = rest.astype(BF16).astype(F32)
    return [-high, -middle, middle - rest]


def attend_kernel(heads, step, qkv_ref, bias_ref, ctx_ref, lse_ref, keys):
    tokens = qkv_ref.shape[0]
    width = heads * HD
    lane = lax.broadcasted_iota(jnp.int32, (1, 2 * HD), 1)
    for h in range(heads):
        keys[h] = widen(qkv_ref[:, width + h * HD : width + (h + 1) * HD], [bias_ref[...]], lane)

    def block(n, _):
        rows = pl.ds(pl.multiple_of(n * step, step), step)
        outs = []
        stat = jnp.zeros((step, 2 * HD), F32)
        for h in range(heads):
            query = qkv_ref[rows, h * HD : (h + 1) * HD].astype(F32) * HD ** (-0.5)
            scores = dot(widen(query, [jnp.ones((step, 1), F32)], lane), keys[h], NT)
            top = jnp.max(scores, axis=1, keepdims=True)
            weights = jnp.exp(scores - top)
            total = jnp.sum(weights, axis=1, keepdims=True)
            values = qkv_ref[:, 2 * width + h * HD : 2 * width + (h + 1) * HD]
            outs.append((dot(weights.astype(BF16), values) / total).astype(BF16))
            stat = jnp.where(lane == h, top + jnp.log(total), stat)
        ctx_ref[rows, :] = jnp.concatenate(outs, axis=1)
        lse_ref[rows, :] = stat
        return 0

    lax.fori_loop(0, tokens // step, block, 0)


def attend(qkv, bias, heads, step=512):
    tokens = qkv.shape[0]
    return pl.pallas_call(
        functools.partial(attend_kernel, heads, step),
        out_shape=(
            jax.ShapeDtypeStruct((tokens, heads * HD), BF16),
            jax.ShapeDtypeStruct((tokens, 2 * HD), F32),
        ),
        in_specs=[VMEM] * 2,
        out_specs=[VMEM] * 2,
        scratch_shapes=[pltpu.VMEM((heads, tokens, 2 * HD), BF16)],
        compiler_params=pltpu.CompilerParams(vmem_limit_bytes=48 * 2**20),
        cost_estimate=pl.CostEstimate(
            flops=16 * heads * tokens * tokens * HD,
            bytes_accessed=10 * tokens * heads * HD,
            transcendentals=heads * tokens * tokens,
        ),
        name="attend",
    )(qkv, bias)


def attend_back_kernel(
    heads, step, qkv_ref, bias_ref, ctx_ref, lse_ref, grad_ref, out_ref, keys, values, dk, dv
):
    tokens = qkv_ref.shape[0]
    width = heads * HD
    scale = HD ** (-0.5)
    lane = lax.broadcasted_iota(jnp.int32, (1, 2 * HD), 1)
    one = jnp.ones((tokens, 1), F32)
    for h in range(heads):
        key = qkv_ref[:, width + h * HD : width + (h + 1) * HD]
        value = qkv_ref[:, 2 * width + h * HD : 2 * width + (h + 1) * HD]
        keys[h] = widen(key, [bias_ref[...], one, one, one], lane)
        values[h] = widen(value, [one, one, one], lane)
    dk[...] = jnp.zeros_like(dk)
    dv[...] = jnp.zeros_like(dv)

    def block(n, _):
        rows = pl.ds(pl.multiple_of(n * step, step), step)
        outs = []
        ones = jnp.ones((step, 1), F32)
        for h in range(heads):
            cols = slice(h * HD, (h + 1) * HD)
            query = qkv_ref[rows, cols].astype(F32) * scale
            grad = grad_ref[rows, cols].astype(F32)
            delta = jnp.sum(grad * ctx_ref[rows, cols].astype(F32), axis=1, keepdims=True)
            lse = lse_ref[rows, h : h + 1]
            weights = jnp.exp(dot(widen(query, [ones] + minus_parts(lse), lane), keys[h], NT))
            slopes = dot(widen(grad, minus_parts(delta), lane), values[h], NT)
            slopes = (weights * slopes).astype(BF16)
            weights = weights.astype(BF16)
            key = qkv_ref[:, width + h * HD : width + (h + 1) * HD]
            outs.append((dot(slopes, key) * scale).astype(BF16))
            dk[h] += dot(query.T.astype(BF16), slopes)
            dv[h] += dot(grad.T.astype(BF16), weights)
        out_ref[rows, :width] = jnp.concatenate(outs, axis=1)
        return 0

    lax.fori_loop(0, tokens // step, block, 0)
    for place, total in ((1, dk), (2, dv)):
        turned = jnp.concatenate([total[h].T for h in range(heads)], axis=1)
        out_ref[:, place * width : (place + 1) * width] = turned.astype(BF16)


def attend_back(qkv, bias, ctx, lse, grad, heads, step=256):
    tokens = qkv.shape[0]
    return pl.pallas_call(
        functools.partial(attend_back_kernel, heads, step),
        out_shape=jax.ShapeDtypeStruct((tokens, 3 * heads * HD), BF16),
        in_specs=[VMEM] * 5,
        out_specs=VMEM,
        scratch_shapes=[pltpu.VMEM((heads, tokens, 2 * HD), BF16)] * 2
        + [pltpu.VMEM((heads, HD, tokens), F32)] * 2,
        compiler_params=pltpu.CompilerParams(vmem_limit_bytes=48 * 2**20),
        cost_estimate=pl.CostEstimate(
            flops=40 * heads * tokens * tokens * HD,
            bytes_accessed=20 * tokens * heads * HD,
            transcendentals=heads * tokens * tokens,
        ),
        name="attend_back",
    )(qkv, bias, ctx, lse, grad)


def swap(value, axis, bits):
    size = lax.axis_size(axis)
    return lax.ppermute(value, axis, [(i, i ^ bits) for i in range(size)])


def core_swap(value):
    return swap(value, "tensor", 1)


def side_swap(value):
    return swap(value, "tensor", 2)


def dp_split(size):
    fast = 2 if size < 16 else 4
    return size // fast, fast


def gather_rows(shard):
    slow, fast = dp_split(lax.axis_size("dp"))
    blocks = []
    for k in range(slow):
        block = swap(shard, "dp", k * fast) if k else shard
        blocks.append([swap(block, "dp", j) if j else block for j in range(fast)])
    return assemble(blocks, slow, fast)


def assemble(blocks, slow, fast):
    rows, columns = blocks[0][0].shape
    index = lax.axis_index("dp")
    place = jnp.stack([index // fast, index % fast]).astype(jnp.int32)
    flat = [b for line in blocks for b in line]

    def kernel(place_ref, *refs):
        ins, out, sems = refs[: slow * fast], refs[-2], refs[-1]
        copies = []
        for n, source in enumerate(ins):
            k, j = n // fast, n % fast
            target = (place_ref[0] ^ k) * fast + (place_ref[1] ^ j)
            copies.append(pltpu.make_async_copy(source, out.at[target], sems.at[n]))
        for copy in copies:
            copy.start()
        for copy in copies:
            copy.wait()

    out = pl.pallas_call(
        kernel,
        out_shape=jax.ShapeDtypeStruct((slow * fast, rows, columns), shard_type(flat[0])),
        in_specs=[pl.BlockSpec(memory_space=pltpu.SMEM)] + [pl.BlockSpec(memory_space=pl.ANY)] * len(flat),
        out_specs=pl.BlockSpec(memory_space=pl.ANY),
        scratch_shapes=[pltpu.SemaphoreType.DMA((slow * fast,))],
        name="assemble",
    )(place, *flat)
    return out.reshape(slow * fast * rows, columns)


def shard_type(value):
    return value.dtype


def scatter_rows(total):
    slow, fast = dp_split(lax.axis_size("dp"))
    rows = total.shape[0] // (slow * fast)
    index = lax.axis_index("dp")
    high, low = index // fast, index % fast

    def part(k, j):
        start = ((high ^ k) * fast + (low ^ j)) * rows
        return lax.dynamic_slice_in_dim(total, start, rows, 0)

    result = None
    for k in list(range(1, slow)) + [0]:
        line = part(k, 0).astype(F32)
        for j in range(1, fast):
            line = line + swap(part(k, j), "dp", j).astype(F32)
        if k:
            line = swap(line.astype(BF16), "dp", k * fast).astype(F32)
        result = line if result is None else result + line
    return result


def gather_tokens(own):
    near = jnp.concatenate([own, core_swap(own)])
    side = side_swap(own)
    far = jnp.concatenate([side, core_swap(side)])
    return near, far


def half_sum(partial):
    half = partial.shape[0] // 2
    return partial[:half].astype(F32) + core_swap(partial[half:]).astype(F32)


def send_far(partial):
    return side_swap(half_sum(partial).astype(BF16)).astype(F32)


def sum_all(value):
    for axis in ("tensor", "dp"):
        bits = 1
        while bits < lax.axis_size(axis):
            value = value + swap(value, axis, bits)
            bits *= 2
    return value


def layer_norm_parts(values, gain_row, shift_row):
    centered = values - jnp.mean(values, axis=-1, keepdims=True)
    inverse = lax.rsqrt(jnp.mean(centered * centered, axis=-1, keepdims=True) + NORM_EPS)
    normed = centered * inverse
    return (normed * gain_row + shift_row, normed, inverse)


def layer_norm_back(grad_normed, normed, inverse, gain_row):
    scaled = grad_normed * gain_row
    return inverse * (
        scaled
        - jnp.mean(scaled, axis=-1, keepdims=True)
        - normed * jnp.mean(scaled * normed, axis=-1, keepdims=True)
    )


def adam_update(master, grad_sum, moment_one, moment_two, step_rate, clip_factor):
    clipped = grad_sum * clip_factor
    one_new = BETA_FIRST * moment_one + (1.0 - BETA_FIRST) * clipped
    two_new = BETA_SECOND * moment_two + (1.0 - BETA_SECOND) * clipped * clipped
    one_hat = one_new / (1.0 - BETA_FIRST**STEP)
    two_hat = two_new / (1.0 - BETA_SECOND**STEP)
    master_new = master - step_rate * (
        one_hat / (jnp.sqrt(two_hat) + ADAM_EPS) + DECAY_RATE * master
    )
    return (master_new, one_new, two_new)


def gelu_parts(value):
    share = 0.5 * lax.erfc(value * -(0.5**0.5))
    slope = share + value * jnp.exp(-0.5 * value * value) * (0.5 / jnp.pi) ** 0.5
    return (value * share).astype(BF16), slope.astype(BF16)


def on_device(
    tokens,
    cotangent,
    lengths,
    key_mask,
    qkv_weight,
    out_weight,
    up_weight,
    down_weight,
    norm_params,
    qkv_first,
    qkv_second,
    out_first,
    out_second,
    up_first,
    up_second,
    down_first,
    down_second,
    norm_first,
    norm_second,
):
    own, width = tokens.shape
    cell = 2 * own
    heads = qkv_weight.shape[2] // HD
    dp, tensor = lax.axis_index("dp"), lax.axis_index("tensor")
    side, core = tensor // 2, tensor % 2

    norm_rows = norm_params.shape[1]
    norm_low = lax.all_gather(norm_params.astype(BF16), "dp", axis=1, tiled=True)
    norm_values = norm_low.astype(F32)

    positions = jnp.arange(cell, dtype=jnp.int32)
    key_valid = (positions[None, :] < lengths[:, None]) & (
        (key_mask == 1) | (positions[None, :] == 0)
    )
    bias = jnp.where(key_valid, 0.0, -1e30).astype(F32)
    bias = jnp.where(side == 0, bias, bias[::-1])
    bias = jnp.where(core == 0, bias, jnp.roll(bias, own, axis=1))
    bias_near, bias_far = bias[0][:, None], bias[1][:, None]

    qkv_full = gather_rows(qkv_weight.astype(BF16).reshape(qkv_weight.shape[0], -1))
    out_full = gather_rows(out_weight.astype(BF16))
    up_full = gather_rows(up_weight.astype(BF16))
    down_full = gather_rows(down_weight.astype(BF16))

    stream_in = tokens.astype(F32)
    ln_one, normed_one, inverse_one = layer_norm_parts(stream_in, norm_values[0], norm_values[1])
    one_near, one_far = gather_tokens(ln_one.astype(BF16))
    qkv_far = dot(one_far, qkv_full).astype(BF16)
    ctx_far, lse_far = attend(qkv_far, bias_far, heads)
    out_far = send_far(dot(ctx_far, out_full).astype(BF16))
    qkv_near = dot(one_near, qkv_full).astype(BF16)
    ctx_near, lse_near = attend(qkv_near, bias_near, heads)
    out_near = half_sum(dot(ctx_near, out_full).astype(BF16))
    residual = stream_in + (out_near + out_far)

    ln_two, normed_two, inverse_two = layer_norm_parts(residual, norm_values[2], norm_values[3])
    two_near, two_far = gather_tokens(ln_two.astype(BF16))
    grad_near, grad_far = gather_tokens(cotangent)
    hid_near, slope_near = gelu_parts(dot(two_near, up_full))
    hid_far, slope_far = gelu_parts(dot(two_far, up_full))
    pre_far = (dot(grad_far, down_full, NT) * slope_far.astype(F32)).astype(BF16)
    back_far = send_far(dot(pre_far, up_full, NT).astype(BF16))
    pre_near = (dot(grad_near, down_full, NT) * slope_near.astype(F32)).astype(BF16)
    back_near = half_sum(dot(pre_near, up_full, NT).astype(BF16))
    grad_ln_two = back_near + back_far

    hid = jnp.concatenate([hid_near, hid_far])
    grad_group = jnp.concatenate([grad_near, grad_far])
    two_group = jnp.concatenate([two_near, two_far])
    pre = jnp.concatenate([pre_near, pre_far])
    grad_down = dot(hid, grad_group, TN).astype(BF16)
    summed_down = scatter_rows(grad_down)
    grad_up = dot(two_group, pre, TN).astype(BF16)
    summed_up = scatter_rows(grad_up)

    last_far = send_far(dot(hid_far, down_full).astype(BF16))
    last_near = half_sum(dot(hid_near, down_full).astype(BF16))
    layer_out = (residual + (last_near + last_far)).astype(BF16)

    grad_residual = cotangent.astype(F32) + layer_norm_back(
        grad_ln_two, normed_two, inverse_two, norm_values[2]
    )
    gain_two = jnp.sum(grad_ln_two * normed_two, axis=0)
    shift_two = jnp.sum(grad_ln_two, axis=0)

    res_near, res_far = gather_tokens(grad_residual.astype(BF16))
    dctx_near = dot(res_near, out_full, NT).astype(BF16)
    dqkv_near = attend_back(qkv_near, bias_near, ctx_near, lse_near, dctx_near, heads)
    dctx_far = dot(res_far, out_full, NT).astype(BF16)
    dqkv_far = attend_back(qkv_far, bias_far, ctx_far, lse_far, dctx_far, heads)
    first_far = send_far(dot(dqkv_far, qkv_full, NT).astype(BF16))
    first_near = half_sum(dot(dqkv_near, qkv_full, NT).astype(BF16))
    one_group = jnp.concatenate([one_near, one_far])
    dqkv = jnp.concatenate([dqkv_near, dqkv_far])
    grad_qkv = dot(one_group, dqkv, TN).astype(BF16)
    summed_qkv = scatter_rows(grad_qkv)
    res_group = jnp.concatenate([res_near, res_far])
    ctx = jnp.concatenate([ctx_near, ctx_far])
    grad_out = dot(ctx, res_group, TN).astype(BF16)
    summed_out = scatter_rows(grad_out)

    grad_ln_one = first_near + first_far
    input_grad = (
        grad_residual + layer_norm_back(grad_ln_one, normed_one, inverse_one, norm_values[0])
    ).astype(BF16)
    gain_one = jnp.sum(grad_ln_one * normed_one, axis=0)
    shift_one = jnp.sum(grad_ln_one, axis=0)

    local_squares = (
        jnp.sum(summed_qkv * summed_qkv)
        + jnp.sum(summed_out * summed_out)
        + jnp.sum(summed_up * summed_up)
        + jnp.sum(summed_down * summed_down)
    )
    rows = jnp.stack([gain_one, shift_one, gain_two, shift_two])
    packed = jnp.concatenate([rows, jnp.full((4, 128), local_squares, F32)], axis=1)
    packed = sum_all(packed)
    norm_grad = packed[:, :width]
    squares_total = packed[0, width] + jnp.sum(norm_grad * norm_grad)
    summed_norm = lax.dynamic_slice_in_dim(norm_grad, dp * norm_rows, norm_rows, 1)
    grad_norm = jnp.sqrt(squares_total)
    clip_factor = jnp.minimum(1.0, CLIP_LIMIT / grad_norm)

    qkv_new, qkv_one, qkv_two = adam_update(
        qkv_weight,
        summed_qkv.reshape(qkv_weight.shape),
        qkv_first,
        qkv_second,
        RATE_QKV,
        clip_factor,
    )
    out_new, out_one, out_two = adam_update(
        out_weight, summed_out, out_first, out_second, RATE_OUT, clip_factor
    )
    up_new, up_one, up_two = adam_update(
        up_weight, summed_up, up_first, up_second, RATE_UP, clip_factor
    )
    down_new, down_one, down_two = adam_update(
        down_weight, summed_down, down_first, down_second, RATE_DOWN, clip_factor
    )
    norm_new, norm_one, norm_two = adam_update(
        norm_params, summed_norm, norm_first, norm_second, RATE_NORM, clip_factor
    )
    shift_grad = clip_factor * summed_norm[3]
    return (
        layer_out,
        input_grad,
        grad_norm,
        qkv_new,
        qkv_one,
        qkv_two,
        out_new,
        out_one,
        out_two,
        up_new,
        up_one,
        up_two,
        down_new,
        down_one,
        down_two,
        norm_new,
        norm_one,
        norm_two,
        shift_grad,
    )


def solution(mesh):
    tokens = P(("dp", "tensor"), None)
    columns = P("dp", None, "tensor")
    rows = P(("tensor", "dp"), None)
    both = P("dp", "tensor")
    norms = P(None, "dp")
    return jax.shard_map(
        on_device,
        mesh=mesh,
        in_specs=(tokens, tokens, P("dp"), P("dp", None), columns, rows, both, rows, norms)
        + (columns,) * 2
        + (rows,) * 2
        + (both,) * 2
        + (rows,) * 2
        + (norms,) * 2,
        out_specs=(tokens, tokens, P())
        + (columns,) * 3
        + (rows,) * 3
        + (both,) * 3
        + (rows,) * 3
        + (norms,) * 3
        + (P("dp"),),
        check_vma=False,
    )
```

```python
import functools

import jax
import jax.numpy as jnp
from jax import lax
from jax.experimental import pallas as pl
from jax.experimental.pallas import tpu as pltpu
from jax.sharding import PartitionSpec as P

HD = 64
STEP = 5

NORM_EPS = 1e-05
CLIP_LIMIT = 1.0
BETA_FIRST = 0.5
BETA_SECOND = 0.5
ADAM_EPS = 1e-08
DECAY_RATE = 0.01
RATE_QKV = 0.03
RATE_OUT = 0.5
RATE_UP = 0.03
RATE_DOWN = 0.015
RATE_NORM = 0.2

F32 = jnp.float32
BF16 = jnp.bfloat16
NN = (((1,), (0,)), ((), ()))
NT = (((1,), (1,)), ((), ()))
TN = (((0,), (0,)), ((), ()))
VMEM = pl.BlockSpec(memory_space=pltpu.VMEM)


def dot(left, right, dims=NN):
    return lax.dot_general(left, right, dims, preferred_element_type=F32)


def widen(block, columns, lane):
    rows = block.shape[0]
    wide = jnp.concatenate([block.astype(F32), jnp.zeros((rows, HD), F32)], axis=1)
    for n, column in enumerate(columns):
        wide = jnp.where(lane == HD + n, column, wide)
    return wide.astype(BF16)


def minus_parts(column):
    high = column.astype(BF16).astype(F32)
    rest = column - high
    middle = rest.astype(BF16).astype(F32)
    return [-high, -middle, middle - rest]


def attend_kernel(heads, step, qkv_ref, bias_ref, ctx_ref, lse_ref, keys):
    tokens = qkv_ref.shape[0]
    width = heads * HD
    lane = lax.broadcasted_iota(jnp.int32, (1, 2 * HD), 1)
    for h in range(heads):
        keys[h] = widen(qkv_ref[:, width + h * HD : width + (h + 1) * HD], [bias_ref[...]], lane)

    def block(n, _):
        rows = pl.ds(pl.multiple_of(n * step, step), step)
        outs = []
        stat = jnp.zeros((step, 2 * HD), F32)
        for h in range(heads):
            query = qkv_ref[rows, h * HD : (h + 1) * HD].astype(F32) * HD ** (-0.5)
            scores = dot(widen(query, [jnp.ones((step, 1), F32)], lane), keys[h], NT)
            top = jnp.max(scores, axis=1, keepdims=True)
            weights = jnp.exp(scores - top)
            total = jnp.sum(weights, axis=1, keepdims=True)
            values = qkv_ref[:, 2 * width + h * HD : 2 * width + (h + 1) * HD]
            outs.append((dot(weights.astype(BF16), values) / total).astype(BF16))
            stat = jnp.where(lane == h, top + jnp.log(total), stat)
        ctx_ref[rows, :] = jnp.concatenate(outs, axis=1)
        lse_ref[rows, :] = stat
        return 0

    lax.fori_loop(0, tokens // step, block, 0)


def attend(qkv, bias, heads, step=512):
    tokens = qkv.shape[0]
    return pl.pallas_call(
        functools.partial(attend_kernel, heads, step),
        out_shape=(
            jax.ShapeDtypeStruct((tokens, heads * HD), BF16),
            jax.ShapeDtypeStruct((tokens, 2 * HD), F32),
        ),
        in_specs=[VMEM] * 2,
        out_specs=[VMEM] * 2,
        scratch_shapes=[pltpu.VMEM((heads, tokens, 2 * HD), BF16)],
        compiler_params=pltpu.CompilerParams(vmem_limit_bytes=48 * 2**20),
        cost_estimate=pl.CostEstimate(flops=0, bytes_accessed=1, transcendentals=0),
        name="attend",
    )(qkv, bias)


def attend_back_kernel(
    heads, step, qkv_ref, bias_ref, ctx_ref, lse_ref, grad_ref, out_ref, keys, values, dk, dv
):
    tokens = qkv_ref.shape[0]
    width = heads * HD
    scale = HD ** (-0.5)
    lane = lax.broadcasted_iota(jnp.int32, (1, 2 * HD), 1)
    one = jnp.ones((tokens, 1), F32)
    for h in range(heads):
        key = qkv_ref[:, width + h * HD : width + (h + 1) * HD]
        value = qkv_ref[:, 2 * width + h * HD : 2 * width + (h + 1) * HD]
        keys[h] = widen(key, [bias_ref[...], one, one, one], lane)
        values[h] = widen(value, [one, one, one], lane)
    dk[...] = jnp.zeros_like(dk)
    dv[...] = jnp.zeros_like(dv)

    def block(n, _):
        rows = pl.ds(pl.multiple_of(n * step, step), step)
        outs = []
        ones = jnp.ones((step, 1), F32)
        for h in range(heads):
            cols = slice(h * HD, (h + 1) * HD)
            query = qkv_ref[rows, cols].astype(F32) * scale
            grad = grad_ref[rows, cols].astype(F32)
            delta = jnp.sum(grad * ctx_ref[rows, cols].astype(F32), axis=1, keepdims=True)
            lse = lse_ref[rows, h : h + 1]
            weights = jnp.exp(dot(widen(query, [ones] + minus_parts(lse), lane), keys[h], NT))
            slopes = dot(widen(grad, minus_parts(delta), lane), values[h], NT)
            slopes = (weights * slopes).astype(BF16)
            weights = weights.astype(BF16)
            key = qkv_ref[:, width + h * HD : width + (h + 1) * HD]
            outs.append((dot(slopes, key) * scale).astype(BF16))
            dk[h] += dot(query.T.astype(BF16), slopes)
            dv[h] += dot(grad.T.astype(BF16), weights)
        out_ref[rows, :width] = jnp.concatenate(outs, axis=1)
        return 0

    lax.fori_loop(0, tokens // step, block, 0)
    for place, total in ((1, dk), (2, dv)):
        turned = jnp.concatenate([total[h].T for h in range(heads)], axis=1)
        out_ref[:, place * width : (place + 1) * width] = turned.astype(BF16)


def attend_back(qkv, bias, ctx, lse, grad, heads, step=256):
    tokens = qkv.shape[0]
    return pl.pallas_call(
        functools.partial(attend_back_kernel, heads, step),
        out_shape=jax.ShapeDtypeStruct((tokens, 3 * heads * HD), BF16),
        in_specs=[VMEM] * 5,
        out_specs=VMEM,
        scratch_shapes=[pltpu.VMEM((heads, tokens, 2 * HD), BF16)] * 2
        + [pltpu.VMEM((heads, HD, tokens), F32)] * 2,
        compiler_params=pltpu.CompilerParams(vmem_limit_bytes=48 * 2**20),
        cost_estimate=pl.CostEstimate(flops=0, bytes_accessed=1, transcendentals=0),
        name="attend_back",
    )(qkv, bias, ctx, lse, grad)


def swap(value, axis, bits):
    size = lax.axis_size(axis)
    return lax.ppermute(value, axis, [(i, i ^ bits) for i in range(size)])


def core_swap(value):
    return swap(value, "tensor", 1)


def side_swap(value):
    return swap(value, "tensor", 2)


def tie(*values):
    return lax.optimization_barrier(values)


def dp_split(size):
    fast = 2 if size < 16 else 4
    return size // fast, fast


def high_swap(value, k):
    return swap(value, "dp", k * dp_split(lax.axis_size("dp"))[1])


def gather_small(shard):
    slow, fast = dp_split(lax.axis_size("dp"))
    index = lax.axis_index("dp")
    lines = jnp.stack([shard] + [high_swap(shard, k) for k in range(1, slow)])
    blocks = jnp.stack([lines] + [swap(lines, "dp", j) for j in range(1, fast)])
    high, low = index // fast, index % fast
    order = [(low ^ j, high ^ k) for k in range(slow) for j in range(fast)]
    return jnp.stack([blocks[j, k] for j, k in order])


def gather_first(shard):
    slow, fast = dp_split(lax.axis_size("dp"))
    lines = {k: [high_swap(shard, k)] for k in range(1, slow, 2)}
    lines[0] = [shard] + [swap(shard, "dp", j) for j in range(1, fast)]
    return lines


def spread(line):
    fast = dp_split(lax.axis_size("dp"))[1]
    return line[:1] + [swap(line[0], "dp", j) for j in range(1, fast)]


def gather_second(shard, lines):
    slow, _ = dp_split(lax.axis_size("dp"))
    even = {k: [high_swap(shard, k)] for k in range(2, slow, 2)}
    return even, {k: spread(v) if k else v for k, v in lines.items()}


def gather_third(even, lines):
    lines = {**lines, **{k: spread(line) for k, line in even.items()}}
    return [lines[k] for k in range(len(lines))]


def assemble(blocks, cuts):
    slow, fast = len(blocks), len(blocks[0])
    flat = [b for line in blocks for b in line]
    rows, columns = flat[0].shape
    index = lax.axis_index("dp")
    place = jnp.stack([index // fast, index % fast]).astype(jnp.int32)

    def kernel(place_ref, *refs):
        ins, outs = refs[: slow * fast], refs[slow * fast : -2]
        whole, sems = refs[-2:]
        whole = outs[0] if len(cuts) == 1 else whole
        copies = []
        for n, source in enumerate(ins):
            target = (place_ref[0] ^ (n // fast)) * fast + (place_ref[1] ^ (n % fast))
            copies.append(pltpu.make_async_copy(source, whole.at[target], sems.at[n]))
        for copy in copies:
            copy.start()
        for copy in copies:
            copy.wait()
        if len(cuts) > 1:
            start = 0
            for out, cut in zip(outs, cuts, strict=True):
                out[...] = whole[:, :, start : start + cut]
                start += cut

    full = (slow * fast, rows, columns)
    outs = pl.pallas_call(
        kernel,
        out_shape=[jax.ShapeDtypeStruct((*full[:2], cut), flat[0].dtype) for cut in cuts],
        in_specs=[pl.BlockSpec(memory_space=pltpu.SMEM)]
        + [pl.BlockSpec(memory_space=pl.ANY)] * len(flat),
        out_specs=[VMEM] * len(cuts),
        scratch_shapes=[
            pltpu.VMEM(full if len(cuts) > 1 else (8, 16, 128), flat[0].dtype),
            pltpu.SemaphoreType.DMA((slow * fast,)),
        ],
        compiler_params=pltpu.CompilerParams(vmem_limit_bytes=24 * 2**20),
        cost_estimate=pl.CostEstimate(flops=0, bytes_accessed=1, transcendentals=0),
        name="assemble",
    )(place, *flat)
    return [out.reshape(slow * fast * rows, -1) for out in outs]


def pick(total, k, j):
    slow, fast = dp_split(lax.axis_size("dp"))
    rows = total.shape[0] // (slow * fast)
    index = lax.axis_index("dp")
    start = (((index // fast) ^ k) * fast + ((index % fast) ^ j)) * rows
    return lax.dynamic_slice_in_dim(total, start, rows, 0)


def scatter_first(total, ks):
    _, fast = dp_split(lax.axis_size("dp"))
    lines = {}
    for k in ks:
        line = pick(total, k, 0).astype(F32)
        for j in range(1, fast):
            line = line + swap(pick(total, k, j), "dp", j).astype(F32)
        lines[k] = line.astype(BF16) if k else line
    return lines


def scatter_second(lines):
    return [high_swap(line, k).astype(F32) if k else line for k, line in lines.items()]


def scatter_order():
    slow, _ = dp_split(lax.axis_size("dp"))
    return list(range(2, slow, 2)), list(range(1, slow, 2)), [0]


def scatter_rows(total):
    parts = []
    for ks in scatter_order():
        parts += scatter_second(scatter_first(total, ks))
    return functools.reduce(jnp.add, parts)


def half_sum(partial):
    half = partial.shape[0] // 2
    return partial[:half].astype(F32) + core_swap(partial[half:]).astype(F32)


def sum_all(value):
    for axis in ("tensor", "dp"):
        bits = 1
        while bits < lax.axis_size(axis):
            value = value + swap(value, axis, bits)
            bits *= 2
    return value


def layer_norm_parts(values, gain_row, shift_row):
    centered = values - jnp.mean(values, axis=-1, keepdims=True)
    inverse = lax.rsqrt(jnp.mean(centered * centered, axis=-1, keepdims=True) + NORM_EPS)
    normed = centered * inverse
    return (normed * gain_row + shift_row, normed, inverse)


def layer_norm_back(grad_normed, normed, inverse, gain_row):
    scaled = grad_normed * gain_row
    return inverse * (
        scaled
        - jnp.mean(scaled, axis=-1, keepdims=True)
        - normed * jnp.mean(scaled * normed, axis=-1, keepdims=True)
    )


def adam_update(master, grad_sum, moment_one, moment_two, step_rate, clip_factor):
    clipped = grad_sum * clip_factor
    one_new = BETA_FIRST * moment_one + (1.0 - BETA_FIRST) * clipped
    two_new = BETA_SECOND * moment_two + (1.0 - BETA_SECOND) * clipped * clipped
    one_hat = one_new / (1.0 - BETA_FIRST**STEP)
    two_hat = two_new / (1.0 - BETA_SECOND**STEP)
    master_new = master - step_rate * (
        one_hat / (jnp.sqrt(two_hat) + ADAM_EPS) + DECAY_RATE * master
    )
    return (master_new, one_new, two_new)


def gelu_parts(value):
    share = 0.5 + 0.5 * lax.erf(value * 0.5**0.5)
    slope = share + value * jnp.exp(-0.5 * value * value) * (0.5 / jnp.pi) ** 0.5
    return (value * share).astype(BF16), slope.astype(BF16)


def on_device(
    tokens,
    cotangent,
    lengths,
    key_mask,
    qkv_weight,
    out_weight,
    up_weight,
    down_weight,
    norm_params,
    qkv_first,
    qkv_second,
    out_first,
    out_second,
    up_first,
    up_second,
    down_first,
    down_second,
    norm_first,
    norm_second,
):
    own, width = tokens.shape
    cell = 2 * own
    heads = qkv_weight.shape[2] // HD
    dp, tensor = lax.axis_index("dp"), lax.axis_index("tensor")
    side, core = tensor // 2, tensor % 2

    norm_rows = norm_params.shape[1]

    positions = jnp.arange(cell, dtype=jnp.int32)
    key_valid = (positions[None, :] < lengths[:, None]) & (
        (key_mask == 1) | (positions[None, :] == 0)
    )
    bias = jnp.where(key_valid, 0.0, -1e30).astype(F32)
    bias = jnp.where(side == 0, bias, bias[::-1])
    bias = jnp.where(core == 0, bias, jnp.roll(bias, own, axis=1))
    bias_near, bias_far = bias[0][:, None], bias[1][:, None]

    shard_rows = qkv_weight.shape[0]
    qkv_width = 3 * heads * HD
    half = own // 2
    first_low = jnp.concatenate(
        [
            qkv_weight.astype(BF16).reshape(shard_rows, -1),
            out_weight.astype(BF16).reshape(shard_rows, -1),
        ],
        axis=1,
    )
    first_lines = gather_first(first_low)
    side_top = side_swap(tokens[:half])
    mate_tokens = core_swap(tokens)
    first_low, first_lines, mate_tokens, side_top, norm_low, tokens, up_low, down_low = tie(
        first_low,
        first_lines,
        mate_tokens,
        side_top,
        norm_params.astype(BF16),
        tokens,
        up_weight.astype(BF16),
        down_weight.astype(BF16),
    )

    first_even, first_lines = gather_second(first_low, first_lines)
    side_rest = side_swap(tokens[half:])
    norm_low = gather_small(norm_low)
    norm_values = jnp.moveaxis(norm_low, 0, 1).reshape(4, width).astype(F32)
    stream_in = tokens.astype(F32)
    _, normed_one, inverse_one = layer_norm_parts(stream_in, norm_values[0], norm_values[1])

    def first_norm(rows):
        return layer_norm_parts(rows.astype(F32), norm_values[0], norm_values[1])[0].astype(BF16)

    one_near = first_norm(jnp.concatenate([tokens, mate_tokens]))
    first_even, first_lines, one_near, up_low = tie(first_even, first_lines, one_near, up_low)
    up_lines = gather_first(up_low)
    first_blocks = gather_third(first_even, first_lines)
    side_tokens = jnp.concatenate([side_top, side_rest])
    one_far = first_norm(jnp.concatenate([side_tokens, core_swap(side_tokens)]))
    first_blocks, one_far = tie(first_blocks, one_far)

    qkv_full, out_full = assemble(first_blocks, (qkv_width, heads * HD))
    out_full = out_full.reshape(-1, width)
    qkv_far = dot(one_far, qkv_full).astype(BF16)
    ctx_far, lse_far = attend(qkv_far, bias_far, heads)
    ctx_far, up_low, up_lines, down_low = tie(ctx_far, up_low, up_lines, down_low)
    up_even, up_lines = gather_second(up_low, up_lines)
    far_sum = half_sum(dot(ctx_far, out_full).astype(BF16)).astype(BF16)
    far_sum, one_near, qkv_full = tie(far_sum, one_near, qkv_full)
    out_far = side_swap(far_sum)
    qkv_near = dot(one_near, qkv_full).astype(BF16)
    ctx_near, lse_near = attend(qkv_near, bias_near, heads)
    ctx_near, up_even, up_lines, down_low = tie(ctx_near, up_even, up_lines, down_low)
    up_blocks = gather_third(up_even, up_lines)
    down_lines = gather_first(down_low)
    out_near = half_sum(dot(ctx_near, out_full).astype(BF16))
    out_near, up_blocks, out_far, down_low, down_lines, cotangent = tie(
        out_near, up_blocks, out_far, down_low, down_lines, cotangent
    )
    down_even, down_lines = gather_second(down_low, down_lines)
    (up_full,) = assemble(up_blocks, (width,))
    residual = stream_in + (out_near + out_far.astype(F32))

    ln_two, normed_two, inverse_two = layer_norm_parts(residual, norm_values[2], norm_values[3])
    ln_two = ln_two.astype(BF16)
    two_near = jnp.concatenate([ln_two, core_swap(ln_two)])
    two_near, ln_two, up_full = tie(two_near, ln_two, up_full)
    two_side = side_swap(ln_two)
    hid_near, slope_near = gelu_parts(dot(two_near, up_full))
    hid_near, slope_near, down_even, down_lines, two_side, cotangent = tie(
        hid_near, slope_near, down_even, down_lines, two_side, cotangent
    )
    down_blocks = gather_third(down_even, down_lines)
    cot_side = side_swap(cotangent)
    grad_near = jnp.concatenate([cotangent, core_swap(cotangent)])
    two_far = jnp.concatenate([two_side, core_swap(two_side)])
    hid_far, slope_far = gelu_parts(dot(two_far, up_full))
    hid_far, slope_far, down_blocks, grad_near = tie(hid_far, slope_far, down_blocks, grad_near)
    (down_full,) = assemble(down_blocks, (width,))

    pre_near = (dot(grad_near, down_full, NT) * slope_near.astype(F32)).astype(BF16)
    pre_near, cot_side = tie(pre_near, cot_side)
    grad_far = jnp.concatenate([cot_side, core_swap(cot_side)])
    pre_far = (dot(grad_far, down_full, NT) * slope_far.astype(F32)).astype(BF16)
    far_sum = half_sum(dot(pre_far, up_full, NT).astype(BF16)).astype(BF16)
    far_sum, pre_near = tie(far_sum, pre_near)
    back_far = side_swap(far_sum)
    back_near = half_sum(dot(pre_near, up_full, NT).astype(BF16))

    hid = jnp.concatenate([hid_near, hid_far])
    grad_group = jnp.concatenate([grad_near, grad_far])
    two_group = jnp.concatenate([two_near, two_far])
    pre = jnp.concatenate([pre_near, pre_far])
    hid, back_near = tie(hid, back_near)
    evens, odds, rest = scatter_order()
    grad_down = dot(hid, grad_group, TN).astype(BF16)
    down_first_lines = scatter_first(grad_down, evens)
    grad_down, pre, down_first_lines = tie(grad_down, pre, down_first_lines)
    down_parts = scatter_second(down_first_lines)
    down_first_lines = scatter_first(grad_down, odds + rest)
    grad_up = dot(two_group, pre, TN).astype(BF16)
    grad_up, back_far, down_first_lines, down_parts = tie(
        grad_up, back_far, down_first_lines, down_parts
    )
    down_parts = down_parts + scatter_second(down_first_lines)
    up_first_lines = scatter_first(grad_up, evens)

    grad_ln_two = back_near + back_far.astype(F32)
    grad_residual = cotangent.astype(F32) + layer_norm_back(
        grad_ln_two, normed_two, inverse_two, norm_values[2]
    )
    gain_two = jnp.sum(grad_ln_two * normed_two, axis=0)
    shift_two = jnp.sum(grad_ln_two, axis=0)

    res_low = grad_residual.astype(BF16)
    res_near = jnp.concatenate([res_low, core_swap(res_low)])
    res_near, res_low, hid_far = tie(res_near, res_low, hid_far)
    res_side = side_swap(res_low)
    last_far = half_sum(dot(hid_far, down_full).astype(BF16)).astype(BF16)
    last_near = half_sum(dot(hid_near, down_full).astype(BF16))
    res_near, last_near, last_far, down_parts, up_first_lines = tie(
        res_near, last_near, last_far, down_parts, up_first_lines
    )
    up_parts = scatter_second(up_first_lines)
    up_first_lines = scatter_first(grad_up, odds + rest)
    dctx_near = dot(res_near, out_full, NT).astype(BF16)
    dqkv_near = attend_back(qkv_near, bias_near, ctx_near, lse_near, dctx_near, heads)
    dqkv_near, res_side, up_parts, up_first_lines, last_far = tie(
        dqkv_near, res_side, up_parts, up_first_lines, last_far
    )
    up_parts = up_parts + scatter_second(up_first_lines)
    last_side = side_swap(last_far)
    res_far = jnp.concatenate([res_side, core_swap(res_side)])
    res_group = jnp.concatenate([res_near, res_far])
    ctx = jnp.concatenate([ctx_near, ctx_far])
    grad_out = dot(ctx, res_group, TN).astype(BF16)
    dctx_far = dot(res_far, out_full, NT).astype(BF16)
    first_near = half_sum(dot(dqkv_near, qkv_full, NT).astype(BF16))
    dctx_far, grad_out, first_near = tie(dctx_far, grad_out, first_near)
    out_first_lines = scatter_first(grad_out, evens + odds + rest)
    dqkv_far = attend_back(qkv_far, bias_far, ctx_far, lse_far, dctx_far, heads)
    dqkv_far, out_first_lines, up_parts, last_side = tie(
        dqkv_far, out_first_lines, up_parts, last_side
    )
    out_parts = scatter_second(out_first_lines)
    one_group = jnp.concatenate([one_near, one_far])
    dqkv = jnp.concatenate([dqkv_near, dqkv_far])
    grad_qkv = dot(one_group, dqkv, TN).astype(BF16)
    qkv_first_lines = scatter_first(grad_qkv, evens)
    far_sum = half_sum(dot(dqkv_far, qkv_full, NT).astype(BF16)).astype(BF16)
    far_sum, grad_qkv, qkv_first_lines, out_parts, down_parts = tie(
        far_sum, grad_qkv, qkv_first_lines, out_parts, down_parts
    )
    first_far = side_swap(far_sum)
    qkv_parts = scatter_second(qkv_first_lines)
    qkv_first_lines = scatter_first(grad_qkv, odds + rest)

    def total(parts):
        return functools.reduce(jnp.add, parts)

    summed_down, summed_up, summed_out = total(down_parts), total(up_parts), total(out_parts)
    layer_out = (residual + (last_near + last_side.astype(F32))).astype(BF16)
    early_squares = (
        jnp.sum(summed_out * summed_out)
        + jnp.sum(summed_up * summed_up)
        + jnp.sum(summed_down * summed_down)
    )
    qkv_parts, qkv_first_lines, layer_out, early_squares = tie(
        qkv_parts, qkv_first_lines, layer_out, early_squares
    )
    qkv_parts = qkv_parts + scatter_second(qkv_first_lines)
    grad_ln_one = first_near + first_far.astype(F32)
    input_grad = (
        grad_residual + layer_norm_back(grad_ln_one, normed_one, inverse_one, norm_values[0])
    ).astype(BF16)
    gain_one = jnp.sum(grad_ln_one * normed_one, axis=0)
    shift_one = jnp.sum(grad_ln_one, axis=0)
    rows = jnp.stack([gain_one, shift_one, gain_two, shift_two])
    qkv_parts, rows, input_grad = tie(qkv_parts, rows, input_grad)
    summed_qkv = total(qkv_parts)

    local_squares = early_squares + jnp.sum(summed_qkv * summed_qkv)
    packed = jnp.concatenate([rows, jnp.full((4, 128), local_squares, F32)], axis=1)
    packed = sum_all(packed)
    norm_grad = packed[:, :width]
    squares_total = packed[0, width] + jnp.sum(norm_grad * norm_grad)
    summed_norm = lax.dynamic_slice_in_dim(norm_grad, dp * norm_rows, norm_rows, 1)
    grad_norm = jnp.sqrt(squares_total)
    clip_factor = jnp.minimum(1.0, CLIP_LIMIT / grad_norm)

    qkv_new, qkv_one, qkv_two = adam_update(
        qkv_weight,
        summed_qkv.reshape(qkv_weight.shape),
        qkv_first,
        qkv_second,
        RATE_QKV,
        clip_factor,
    )
    out_new, out_one, out_two = adam_update(
        out_weight, summed_out, out_first, out_second, RATE_OUT, clip_factor
    )
    up_new, up_one, up_two = adam_update(
        up_weight, summed_up, up_first, up_second, RATE_UP, clip_factor
    )
    down_new, down_one, down_two = adam_update(
        down_weight, summed_down, down_first, down_second, RATE_DOWN, clip_factor
    )
    norm_new, norm_one, norm_two = adam_update(
        norm_params, summed_norm, norm_first, norm_second, RATE_NORM, clip_factor
    )
    shift_grad = clip_factor * summed_norm[3]
    return (
        layer_out,
        input_grad,
        grad_norm,
        qkv_new,
        qkv_one,
        qkv_two,
        out_new,
        out_one,
        out_two,
        up_new,
        up_one,
        up_two,
        down_new,
        down_one,
        down_two,
        norm_new,
        norm_one,
        norm_two,
        shift_grad,
    )


def solution(mesh):
    tokens = P(("dp", "tensor"), None)
    columns = P("dp", None, "tensor")
    rows = P(("tensor", "dp"), None)
    both = P("dp", "tensor")
    norms = P(None, "dp")
    return jax.shard_map(
        on_device,
        mesh=mesh,
        in_specs=(tokens, tokens, P("dp"), P("dp", None), columns, rows, both, rows, norms)
        + (columns,) * 2
        + (rows,) * 2
        + (both,) * 2
        + (rows,) * 2
        + (norms,) * 2,
        out_specs=(tokens, tokens, P())
        + (columns,) * 3
        + (rows,) * 3
        + (both,) * 3
        + (rows,) * 3
        + (norms,) * 3
        + (P("dp"),),
        check_vma=False,
    )
```

```python
import functools

import jax
import jax.numpy as jnp
from jax import lax
from jax.experimental import pallas as pl
from jax.experimental.layout import Layout, with_layout_constraint
from jax.experimental.pallas import tpu as pltpu
from jax.sharding import PartitionSpec as P

HD = 64
STEP = 5

NORM_EPS = 1e-05
CLIP_LIMIT = 1.0
BETA_FIRST = 0.5
BETA_SECOND = 0.5
ADAM_EPS = 1e-08
DECAY_RATE = 0.01
RATE_QKV = 0.03
RATE_OUT = 0.5
RATE_UP = 0.03
RATE_DOWN = 0.015
RATE_NORM = 0.2

F32 = jnp.float32
BF16 = jnp.bfloat16
NN = (((1,), (0,)), ((), ()))
NT = (((1,), (1,)), ((), ()))
TN = (((0,), (0,)), ((), ()))
VMEM = pl.BlockSpec(memory_space=pltpu.VMEM)


def dot(left, right, dims=NN):
    return lax.dot_general(left, right, dims, preferred_element_type=F32)


def widen(block, columns, lane):
    rows = block.shape[0]
    wide = jnp.concatenate([block.astype(F32), jnp.zeros((rows, HD), F32)], axis=1)
    for n, column in enumerate(columns):
        wide = jnp.where(lane == HD + n, column, wide)
    return wide.astype(BF16)


def minus_parts(column):
    high = column.astype(BF16).astype(F32)
    rest = column - high
    middle = rest.astype(BF16).astype(F32)
    return [-high, -middle, middle - rest]


def attend_kernel(heads, step, qkv_ref, bias_ref, ctx_ref, lse_ref, keys):
    tokens = qkv_ref.shape[0]
    width = heads * HD
    lane = lax.broadcasted_iota(jnp.int32, (1, 2 * HD), 1)
    for h in range(heads):
        keys[h] = widen(qkv_ref[:, width + h * HD : width + (h + 1) * HD], [bias_ref[...]], lane)

    def block(n, _):
        rows = pl.ds(pl.multiple_of(n * step, step), step)
        outs = []
        stat = jnp.zeros((step, 2 * HD), F32)
        for h in range(heads):
            query = qkv_ref[rows, h * HD : (h + 1) * HD].astype(F32) * HD ** (-0.5)
            scores = dot(widen(query, [jnp.ones((step, 1), F32)], lane), keys[h], NT)
            top = jnp.max(scores, axis=1, keepdims=True)
            weights = jnp.exp(scores - top)
            total = jnp.sum(weights, axis=1, keepdims=True)
            values = qkv_ref[:, 2 * width + h * HD : 2 * width + (h + 1) * HD]
            outs.append((dot(weights.astype(BF16), values) / total).astype(BF16))
            stat = jnp.where(lane == h, top + jnp.log(total), stat)
        ctx_ref[rows, :] = jnp.concatenate(outs, axis=1)
        lse_ref[rows, :] = stat
        return 0

    lax.fori_loop(0, tokens // step, block, 0)


def attend(qkv, bias, heads, step=512):
    tokens = qkv.shape[0]
    return pl.pallas_call(
        functools.partial(attend_kernel, heads, step),
        out_shape=(
            jax.ShapeDtypeStruct((tokens, heads * HD), BF16),
            jax.ShapeDtypeStruct((tokens, 2 * HD), F32),
        ),
        in_specs=[VMEM] * 2,
        out_specs=[VMEM] * 2,
        scratch_shapes=[pltpu.VMEM((heads, tokens, 2 * HD), BF16)],
        compiler_params=pltpu.CompilerParams(vmem_limit_bytes=48 * 2**20),
        cost_estimate=pl.CostEstimate(flops=0, bytes_accessed=1, transcendentals=0),
        name="attend",
    )(qkv, bias)


def attend_back_kernel(
    heads, step, qkv_ref, bias_ref, ctx_ref, lse_ref, grad_ref, out_ref, keys, values, dk, dv
):
    tokens = qkv_ref.shape[0]
    width = heads * HD
    scale = HD ** (-0.5)
    lane = lax.broadcasted_iota(jnp.int32, (1, 2 * HD), 1)
    one = jnp.ones((tokens, 1), F32)
    for h in range(heads):
        key = qkv_ref[:, width + h * HD : width + (h + 1) * HD]
        value = qkv_ref[:, 2 * width + h * HD : 2 * width + (h + 1) * HD]
        keys[h] = widen(key, [bias_ref[...], one, one, one], lane)
        values[h] = widen(value, [one, one, one], lane)
    dk[...] = jnp.zeros_like(dk)
    dv[...] = jnp.zeros_like(dv)

    def block(n, _):
        rows = pl.ds(pl.multiple_of(n * step, step), step)
        outs = []
        ones = jnp.ones((step, 1), F32)
        for h in range(heads):
            cols = slice(h * HD, (h + 1) * HD)
            query = qkv_ref[rows, cols].astype(F32) * scale
            grad = grad_ref[rows, cols].astype(F32)
            delta = jnp.sum(grad * ctx_ref[rows, cols].astype(F32), axis=1, keepdims=True)
            lse = lse_ref[rows, h : h + 1]
            weights = jnp.exp(dot(widen(query, [ones] + minus_parts(lse), lane), keys[h], NT))
            slopes = dot(widen(grad, minus_parts(delta), lane), values[h], NT)
            slopes = (weights * slopes).astype(BF16)
            weights = weights.astype(BF16)
            key = qkv_ref[:, width + h * HD : width + (h + 1) * HD]
            outs.append((dot(slopes, key) * scale).astype(BF16))
            dk[h] += dot(query.T.astype(BF16), slopes)
            dv[h] += dot(grad.T.astype(BF16), weights)
        out_ref[rows, :width] = jnp.concatenate(outs, axis=1)
        return 0

    lax.fori_loop(0, tokens // step, block, 0)
    for place, total in ((1, dk), (2, dv)):
        turned = jnp.concatenate([total[h].T for h in range(heads)], axis=1)
        out_ref[:, place * width : (place + 1) * width] = turned.astype(BF16)


def attend_back(qkv, bias, ctx, lse, grad, heads, step=256):
    tokens = qkv.shape[0]
    return pl.pallas_call(
        functools.partial(attend_back_kernel, heads, step),
        out_shape=jax.ShapeDtypeStruct((tokens, 3 * heads * HD), BF16),
        in_specs=[VMEM] * 5,
        out_specs=VMEM,
        scratch_shapes=[pltpu.VMEM((heads, tokens, 2 * HD), BF16)] * 2
        + [pltpu.VMEM((heads, HD, tokens), F32)] * 2,
        compiler_params=pltpu.CompilerParams(vmem_limit_bytes=48 * 2**20),
        cost_estimate=pl.CostEstimate(flops=0, bytes_accessed=1, transcendentals=0),
        name="attend_back",
    )(qkv, bias, ctx, lse, grad)


def swap(value, axis, bits):
    size = lax.axis_size(axis)
    return lax.ppermute(value, axis, [(i, i ^ bits) for i in range(size)])


def core_swap(value):
    return swap(value, "tensor", 1)


def side_swap(value):
    return swap(value, "tensor", 2)


def tie(*values):
    return lax.optimization_barrier(values)


def dp_split(size):
    fast = 2 if size < 16 else 4
    return size // fast, fast


def high_swap(value, k):
    return swap(value, "dp", k * dp_split(lax.axis_size("dp"))[1])


def gather_small(shard):
    size = lax.axis_size("dp")
    blocks = shard[None]
    bits = 1
    while bits < size:
        blocks = jnp.concatenate([blocks, swap(blocks, "dp", bits)])
        bits *= 2
    index = lax.axis_index("dp")
    return jnp.stack([blocks[index ^ n] for n in range(size)])


def spread(block):
    _, fast = dp_split(lax.axis_size("dp"))
    return [block] + [swap(block, "dp", j) for j in range(1, fast)]


def entries(k, line, at=None):
    return [(k, j, block, at if j else None) for j, block in enumerate(line)]


def joined_entries(ks, blocks, others):
    return [
        entry
        for n, (k, block) in enumerate(zip(ks, blocks, strict=True))
        for entry in entries(k, [block, *others], n)
    ]


def pack_kernel(qkv_ref, out_ref, packed_ref):
    rows, width = out_ref.shape
    step = width * rows // qkv_ref.shape[0]
    parts = [qkv_ref[:, n, :] for n in range(qkv_ref.shape[1])]
    turned = [out_ref[:, n : n + step] for n in range(0, width, step)]
    packed = jnp.concatenate([*parts, jnp.concatenate(turned, axis=0)], axis=1)
    packed_ref[...] = packed.astype(BF16)


def pack_first(qkv, out):
    shape = (qkv.shape[0], qkv.shape[1] * qkv.shape[2] + out.size // qkv.shape[0])
    if out.shape[0] % 8:
        step = out.shape[1] * out.shape[0] // qkv.shape[0]
        turned = jnp.concatenate([out[:, n : n + step] for n in range(0, out.shape[1], step)])
        packed = jnp.concatenate([qkv.reshape(qkv.shape[0], -1), turned], axis=1)
        return packed.astype(BF16)
    return pl.pallas_call(
        pack_kernel,
        out_shape=jax.ShapeDtypeStruct(shape, BF16),
        in_specs=[VMEM] * 2,
        out_specs=VMEM,
        compiler_params=pltpu.CompilerParams(vmem_limit_bytes=16 * 2**20),
        cost_estimate=pl.CostEstimate(flops=0, bytes_accessed=1, transcendentals=0),
        name="pack_first",
    )(qkv, out)


def assemble(blocks, cut=None):
    slow, fast = dp_split(lax.axis_size("dp"))
    rows, columns = blocks[0][2].shape[-2:]
    kind = blocks[0][2].dtype
    index = lax.axis_index("dp")
    place = jnp.stack([index // fast, index % fast]).astype(jnp.int32)
    where = [(k, j, at) for k, j, _, at in blocks]
    out_rows = rows * (columns - cut) // columns if cut else 0

    def kernel(place_ref, *refs):
        ins, outs = refs[: len(where)], refs[len(where) : -2]
        whole, sems = refs[-2:] if cut else (outs[0], refs[-1])
        copies = []
        for n, (source, (k, j, at)) in enumerate(zip(ins, where, strict=True)):
            target = (place_ref[0] ^ k) * fast + (place_ref[1] ^ j)
            source = source if at is None else source.at[at]
            copies.append(pltpu.make_async_copy(source, whole.at[target], sems.at[n]))
        for copy in copies:
            copy.start()
        for copy in copies:
            copy.wait()
        if cut:
            outs[0][...] = whole[:, :, :cut]
            if out_rows % 8:
                outs[1][...] = whole[:, :, cut:]
            else:
                turned = []
                for n in range(slow * fast):
                    block = whole[n, :, cut:].astype(F32)
                    parts = [block[m : m + out_rows] for m in range(0, rows, out_rows)]
                    turned.append(jnp.concatenate(parts, axis=1))
                outs[1][...] = jnp.concatenate(turned, axis=0).astype(kind)

    size = slow * fast
    full = (size, rows, columns)
    if not cut:
        shapes = [full]
    elif out_rows % 8:
        shapes = [(size, rows, cut), (size, rows, columns - cut)]
    else:
        shapes = [(size, rows, cut), (size * out_rows, columns)]
    outs = pl.pallas_call(
        kernel,
        out_shape=[jax.ShapeDtypeStruct(shape, kind) for shape in shapes],
        in_specs=[pl.BlockSpec(memory_space=pltpu.SMEM)]
        + [pl.BlockSpec(memory_space=pltpu.HBM)] * len(where),
        out_specs=[VMEM] * len(shapes),
        scratch_shapes=[
            pltpu.VMEM(full if cut else (8, 16, 128), kind),
            pltpu.SemaphoreType.DMA((len(where),)),
        ],
        compiler_params=pltpu.CompilerParams(vmem_limit_bytes=24 * 2**20),
        cost_estimate=pl.CostEstimate(flops=0, bytes_accessed=1, transcendentals=0),
        name="assemble",
    )(place, *[array for _, _, array, _ in blocks])
    outs = list(outs)
    if cut and out_rows % 8:
        turned = outs[1].reshape(size, rows // out_rows, out_rows, columns - cut)
        outs[1] = turned.transpose(0, 2, 1, 3).reshape(size * out_rows, columns)
    return [out.reshape(-1, out.shape[-1]) for out in outs]


def pick(total, k, j):
    slow, fast = dp_split(lax.axis_size("dp"))
    rows = total.shape[0] // (slow * fast)
    index = lax.axis_index("dp")
    start = (((index // fast) ^ k) * fast + ((index % fast) ^ j)) * rows
    return lax.dynamic_slice_in_dim(total, start, rows, 0)


def rows_first(value):
    return with_layout_constraint(value, Layout(tuple(range(value.ndim))))


def scatter_send(total, ks):
    _, fast = dp_split(lax.axis_size("dp"))
    return [
        swap(jnp.concatenate([rows_first(pick(total, k, j)) for k in ks]), "dp", j)
        for j in range(1, fast)
    ]


def scatter_lines(total, ks, received):
    lines = {}
    for n, k in enumerate(ks):
        line = pick(total, k, 0).astype(F32)
        rows = line.shape[0]
        for part in received:
            line = line + part[n * rows : (n + 1) * rows].astype(F32)
        lines[k] = rows_first(line.astype(BF16))
    return lines


def scatter_last(lines):
    return [high_swap(line, k) if k else line for k, line in lines.items()]


def scatter_order():
    slow, _ = dp_split(lax.axis_size("dp"))
    order = list(range(2, slow, 2)) + list(range(1, slow, 2)) + [0]
    return order[: slow // 2], order[slow // 2 :]


def parts_sum(parts):
    return functools.reduce(jnp.add, [part.astype(F32) for part in parts])


def cores_sum(left, right, dims=NN):
    return own_sum(left, right, mates_part(left, right, dims), dims)


def mates_part(left, right, dims=NN):
    return core_swap(dot(left[left.shape[0] // 2 :], right, dims).astype(BF16))


def own_sum(left, right, mate, dims=NN):
    return dot(left[: left.shape[0] // 2], right, dims) + mate.astype(F32)


def side_send(value):
    half = value.shape[0] // 2
    return [side_swap(value[:half]), side_swap(value[half:])]


def join(parts):
    return jnp.concatenate(parts)


def with_mate(own):
    return jnp.concatenate([own, core_swap(own)])


def norm_kernel(top_ref, rest_ref, rows_ref, out_ref):
    gain, shift = rows_ref[0:1, :], rows_ref[1:2, :]
    for n, ref in enumerate((top_ref, rest_ref)):
        values = ref[...].astype(F32)
        centered = values - jnp.mean(values, axis=-1, keepdims=True)
        inverse = lax.rsqrt(jnp.mean(centered * centered, axis=-1, keepdims=True) + NORM_EPS)
        out_ref[n] = (centered * inverse * gain + shift).astype(BF16)


def norm_tokens(top, rest, rows, step=128):
    half, width = top.shape
    block = pl.BlockSpec((step, width), lambda i: (i, 0))
    out = pl.pallas_call(
        norm_kernel,
        grid=(half // step,),
        out_shape=jax.ShapeDtypeStruct((2, half, width), BF16),
        in_specs=[block, block, pl.BlockSpec((2, width), lambda i: (0, 0))],
        out_specs=pl.BlockSpec((2, step, width), lambda i: (0, i, 0)),
        compiler_params=pltpu.CompilerParams(vmem_limit_bytes=24 * 2**20),
        cost_estimate=pl.CostEstimate(flops=0, bytes_accessed=1, transcendentals=0),
        name="norm_tokens",
    )(top, rest, rows)
    return out.reshape(2 * half, width)


def sum_all(value):
    for axis in ("tensor", "dp"):
        bits = 1
        while bits < lax.axis_size(axis):
            value = value + swap(value, axis, bits)
            bits *= 2
    return value


def layer_norm_parts(values, gain_row, shift_row):
    centered = values - jnp.mean(values, axis=-1, keepdims=True)
    inverse = lax.rsqrt(jnp.mean(centered * centered, axis=-1, keepdims=True) + NORM_EPS)
    normed = centered * inverse
    return (normed * gain_row + shift_row, normed, inverse)


def layer_norm_back(grad_normed, normed, inverse, gain_row):
    scaled = grad_normed * gain_row
    return inverse * (
        scaled
        - jnp.mean(scaled, axis=-1, keepdims=True)
        - normed * jnp.mean(scaled * normed, axis=-1, keepdims=True)
    )


def adam_update(master, grad_sum, moment_one, moment_two, step_rate, clip_factor):
    clipped = grad_sum * clip_factor
    one_new = BETA_FIRST * moment_one + (1.0 - BETA_FIRST) * clipped
    two_new = BETA_SECOND * moment_two + (1.0 - BETA_SECOND) * clipped * clipped
    one_hat = one_new / (1.0 - BETA_FIRST**STEP)
    two_hat = two_new / (1.0 - BETA_SECOND**STEP)
    master_new = master - step_rate * (
        one_hat / (jnp.sqrt(two_hat) + ADAM_EPS) + DECAY_RATE * master
    )
    return (master_new, one_new, two_new)


def gelu_parts(value):
    share = 0.5 + 0.5 * lax.erf(value * 0.5**0.5)
    slope = share + value * jnp.exp(-0.5 * value * value) * (0.5 / jnp.pi) ** 0.5
    return (value * share).astype(BF16), slope.astype(BF16)


def on_device(
    tokens,
    cotangent,
    lengths,
    key_mask,
    qkv_weight,
    out_weight,
    up_weight,
    down_weight,
    norm_params,
    qkv_first,
    qkv_second,
    out_first,
    out_second,
    up_first,
    up_second,
    down_first,
    down_second,
    norm_first,
    norm_second,
):
    own, width = tokens.shape
    cell = 2 * own
    heads = qkv_weight.shape[2] // HD
    dp, tensor = lax.axis_index("dp"), lax.axis_index("tensor")
    side, core = tensor // 2, tensor % 2

    norm_rows = norm_params.shape[1]

    positions = jnp.arange(cell, dtype=jnp.int32)
    key_valid = (positions[None, :] < lengths[:, None]) & (
        (key_mask == 1) | (positions[None, :] == 0)
    )
    bias = jnp.where(key_valid, 0.0, -1e30).astype(F32)
    bias = jnp.where(side == 0, bias, bias[::-1])
    bias = jnp.where(core == 0, bias, jnp.roll(bias, own, axis=1))
    bias_near, bias_far = bias[0][:, None], bias[1][:, None]

    slow, _ = dp_split(lax.axis_size("dp"))
    odds, evens = list(range(1, slow, 2)), list(range(2, slow, 2))
    qkv_width = 3 * heads * HD
    first_low = pack_first(qkv_weight, out_weight)
    first_odd = [high_swap(first_low, k) for k in odds]
    first_own = spread(first_low)
    mate_tokens = core_swap(tokens)
    norm_low, mate_tokens = tie(norm_params.astype(BF16), mate_tokens)
    norm_low = gather_small(norm_low)
    side_tokens = side_swap(tokens)
    first_low, first_odd, first_own, up_low, down_low = tie(
        first_low, first_odd, first_own, up_weight, down_weight
    )
    first_even = [high_swap(first_low, k) for k in evens]
    first_odd = [spread(block) for block in first_odd]
    up_low, down_low = up_low.astype(BF16), down_low.astype(BF16)
    norm_values = jnp.moveaxis(norm_low, 0, 1).reshape(4, width).astype(F32)
    one_near = norm_tokens(tokens, mate_tokens, norm_values[:2])
    first_even, first_odd, one_near, side_tokens, up_low, down_low, cotangent = tie(
        first_even, first_odd, one_near, side_tokens, up_low, down_low, cotangent
    )
    first_even = [spread(block) for block in first_even]
    one_far = norm_tokens(side_tokens, core_swap(side_tokens), norm_values[:2])
    lines = odds + evens
    up_lines = [high_swap(up_low, k) for k in lines]
    both_own = spread(jnp.stack([up_low, down_low]))[1:]
    cot_side = side_swap(cotangent)
    first_even, one_far = tie(first_even, one_far)

    qkv_full, out_full = assemble(
        sum(
            [entries(k, line) for k, line in zip(odds + evens, first_odd + first_even, strict=True)],
            entries(0, first_own),
        ),
        qkv_width,
    )
    qkv_far = dot(one_far, qkv_full).astype(BF16)
    ctx_far, lse_far = attend(qkv_far, bias_far, heads)
    ctx_far, up_lines, both_own, cot_side, down_low = tie(
        ctx_far, up_lines, both_own, cot_side, down_low
    )
    up_others = spread(jnp.stack(up_lines))[1:]
    down_odd = [high_swap(down_low, k) for k in odds]
    far_sum = cores_sum(ctx_far, out_full).astype(BF16)
    far_sum, one_near, qkv_full = tie(far_sum, one_near, qkv_full)
    out_far = side_swap(far_sum)
    qkv_near = dot(one_near, qkv_full).astype(BF16)
    ctx_near, lse_near = attend(qkv_near, bias_near, heads)
    ctx_near, out_far, up_others, down_odd, down_low, cotangent, cot_side = tie(
        ctx_near, out_far, up_others, down_odd, down_low, cotangent, cot_side
    )
    down_even = [high_swap(down_low, k) for k in evens]
    odd_others = spread(jnp.stack(down_odd))[1:]
    grad_near = with_mate(cotangent)
    grad_far = with_mate(cot_side)
    out_near = cores_sum(ctx_near, out_full)
    stream_in = tokens.astype(F32)
    residual = stream_in + (out_near + out_far.astype(F32))

    ln_two, normed_two, inverse_two = layer_norm_parts(residual, norm_values[2], norm_values[3])
    ln_two = ln_two.astype(BF16)
    two_near = with_mate(ln_two)
    two_side = side_swap(ln_two)
    two_near, up_lines, up_others, both_own, down_low = tie(
        two_near, up_lines, up_others, both_own, down_low
    )
    (up_full,) = assemble(
        [(0, 0, up_low, None)]
        + [(0, j + 1, block, 0) for j, block in enumerate(both_own)]
        + joined_entries(lines, up_lines, up_others)
    )
    hid_near, slope_near = gelu_parts(dot(two_near, up_full))
    hid_near, down_even, odd_others, grad_near, grad_far = tie(
        hid_near, down_even, odd_others, grad_near, grad_far
    )
    even_others = [spread(block) for block in down_even]
    hid_near, even_others = tie(hid_near, even_others)
    (down_full,) = assemble(
        sum(
            [entries(k, line) for k, line in zip(evens, even_others, strict=True)],
            [(0, 0, down_low, None)] + [(0, j + 1, block, 1) for j, block in enumerate(both_own)],
        )
        + joined_entries(odds, down_odd, odd_others)
    )
    pre_near = (dot(grad_near, down_full, NT) * slope_near.astype(F32)).astype(BF16)
    pre_near, hid_near, two_side = tie(pre_near, hid_near, two_side)
    two_far = with_mate(two_side)
    hid_far, slope_far = gelu_parts(dot(two_far, up_full))
    pre_far = (dot(grad_far, down_full, NT) * slope_far.astype(F32)).astype(BF16)
    far_sum = cores_sum(pre_far, up_full, NT).astype(BF16)
    far_sum, pre_near, pre_far, hid_near, hid_far = tie(
        far_sum, pre_near, pre_far, hid_near, hid_far
    )
    back_far = side_swap(far_sum)
    back_near = cores_sum(pre_near, up_full, NT)
    back_near, hid_near, hid_far, grad_near, grad_far = tie(
        back_near, hid_near, hid_far, grad_near, grad_far
    )
    heavy, light = scatter_order()
    order = heavy + light
    grad_down = dot(join([hid_near, hid_far]), join([grad_near, grad_far]), TN).astype(BF16)
    half = own
    last_terms = [dot(v[half:], down_full).astype(BF16) for v in (hid_far, hid_near)]
    last_terms, grad_down, back_far, pre_near, pre_far = tie(
        last_terms, grad_down, back_far, pre_near, pre_far
    )
    down_received = scatter_send(grad_down, order)
    grad_ln_two = back_near + back_far.astype(F32)
    grad_residual = cotangent.astype(F32) + layer_norm_back(
        grad_ln_two, normed_two, inverse_two, norm_values[2]
    )
    gain_two = jnp.sum(grad_ln_two * normed_two, axis=0)
    shift_two = jnp.sum(grad_ln_two, axis=0)

    res_low = grad_residual.astype(BF16)
    res_side = side_swap(res_low)
    res_near = with_mate(res_low)
    last_mates = [core_swap(v) for v in last_terms]
    res_near, last_mates, pre_near, pre_far = tie(res_near, last_mates, pre_near, pre_far)
    grad_up = dot(join([two_near, two_far]), join([pre_near, pre_far]), TN).astype(BF16)
    grad_up, res_near, grad_down, down_received = tie(grad_up, res_near, grad_down, down_received)
    up_received = scatter_send(grad_up, order)
    down_lines = scatter_lines(grad_down, order, down_received)
    down_parts = {k: high_swap(down_lines[k], k) for k in heavy}
    dctx_near = dot(res_near, out_full, NT).astype(BF16)
    dqkv_near = attend_back(qkv_near, bias_near, ctx_near, lse_near, dctx_near, heads)
    dqkv_near, res_side, up_received, grad_up, down_parts, down_lines, last_mates, hid_far = tie(
        dqkv_near, res_side, up_received, grad_up, down_parts, down_lines, last_mates, hid_far
    )
    for k in light:
        down_parts[k] = high_swap(down_lines[k], k) if k else down_lines[k]
    last_far = own_sum(hid_far, down_full, last_mates[0]).astype(BF16)
    last_side = side_swap(last_far)
    up_lines = scatter_lines(grad_up, order, up_received)
    up_parts = {k: high_swap(up_lines[k], k) for k in heavy}
    res_far = with_mate(res_side)
    grad_out = dot(join([ctx_near, ctx_far]), join([res_near, res_far]), TN).astype(BF16)
    dctx_far = dot(res_far, out_full, NT).astype(BF16)
    dctx_far, grad_out = tie(dctx_far, grad_out)
    dqkv_far = attend_back(qkv_far, bias_far, ctx_far, lse_far, dctx_far, heads)
    dqkv_far, up_parts, up_lines, down_parts, last_side, grad_out = tie(
        dqkv_far, up_parts, up_lines, down_parts, last_side, grad_out
    )

    for k in light:
        up_parts[k] = high_swap(up_lines[k], k) if k else up_lines[k]
    out_received = scatter_send(grad_out, order)
    grad_qkv = dot(join([one_near, one_far]), join([dqkv_near, dqkv_far]), TN).astype(BF16)
    grad_qkv, dqkv_far, dqkv_near = tie(rows_first(grad_qkv), dqkv_far, dqkv_near)
    received = {k: scatter_send(grad_qkv, [k]) for k in order}
    mate = mates_part(dqkv_far, qkv_full, NT)
    first_lines = {}
    for k in evens:
        first_lines.update(scatter_lines(grad_qkv, [k], received[k]))
    first_lines, mate, grad_qkv, dqkv_far, out_received, grad_out = tie(
        first_lines, mate, grad_qkv, dqkv_far, out_received, grad_out
    )
    qkv_parts = scatter_last(first_lines)
    out_parts = scatter_last(scatter_lines(grad_out, order, out_received))
    far_sum = own_sum(dqkv_far, qkv_full, mate, NT).astype(BF16)
    far_sum, dqkv_near = tie(far_sum, dqkv_near)
    first_far = side_swap(far_sum)
    first_near = cores_sum(dqkv_near, qkv_full, NT)
    odd_lines = {}
    for k in odds:
        odd_lines.update(scatter_lines(grad_qkv, [k], received[k]))
    odd_lines, grad_qkv, first_near = tie(odd_lines, grad_qkv, first_near)
    qkv_parts = qkv_parts + scatter_last(odd_lines)
    qkv_parts = qkv_parts + scatter_last(scatter_lines(grad_qkv, [0], received[0]))

    last_near = own_sum(hid_near, down_full, last_mates[1])
    layer_out = (residual + (last_near + last_side.astype(F32))).astype(BF16)
    summed_up, summed_down = parts_sum(up_parts.values()), parts_sum(down_parts.values())
    summed_out = parts_sum(out_parts)
    early_squares = (
        jnp.sum(summed_up * summed_up)
        + jnp.sum(summed_down * summed_down)
        + jnp.sum(summed_out * summed_out)
    )
    _, normed_one, inverse_one = layer_norm_parts(stream_in, norm_values[0], norm_values[1])
    layer_out, first_far, early_squares = tie(layer_out, first_far, early_squares)
    grad_ln_one = first_near + first_far.astype(F32)
    input_grad = (
        grad_residual + layer_norm_back(grad_ln_one, normed_one, inverse_one, norm_values[0])
    ).astype(BF16)
    gain_one = jnp.sum(grad_ln_one * normed_one, axis=0)
    shift_one = jnp.sum(grad_ln_one, axis=0)
    rows = jnp.stack([gain_one, shift_one, gain_two, shift_two])
    qkv_parts, rows, input_grad, early_squares = tie(qkv_parts, rows, input_grad, early_squares)
    summed_qkv = parts_sum(qkv_parts)

    local_squares = early_squares + jnp.sum(summed_qkv * summed_qkv)
    packed = jnp.concatenate([rows, jnp.full((4, 128), local_squares, F32)], axis=1)
    packed = sum_all(packed)
    norm_grad = packed[:, :width]
    squares_total = packed[0, width] + jnp.sum(norm_grad * norm_grad)
    summed_norm = lax.dynamic_slice_in_dim(norm_grad, dp * norm_rows, norm_rows, 1)
    grad_norm = jnp.sqrt(squares_total)
    clip_factor = jnp.minimum(1.0, CLIP_LIMIT / grad_norm)

    qkv_new, qkv_one, qkv_two = adam_update(
        qkv_weight,
        summed_qkv.reshape(qkv_weight.shape),
        qkv_first,
        qkv_second,
        RATE_QKV,
        clip_factor,
    )
    out_new, out_one, out_two = adam_update(
        out_weight, summed_out, out_first, out_second, RATE_OUT, clip_factor
    )
    up_new, up_one, up_two = adam_update(
        up_weight, summed_up, up_first, up_second, RATE_UP, clip_factor
    )
    down_new, down_one, down_two = adam_update(
        down_weight, summed_down, down_first, down_second, RATE_DOWN, clip_factor
    )
    norm_new, norm_one, norm_two = adam_update(
        norm_params, summed_norm, norm_first, norm_second, RATE_NORM, clip_factor
    )
    shift_grad = clip_factor * summed_norm[3]
    return (
        layer_out,
        input_grad,
        grad_norm,
        qkv_new,
        qkv_one,
        qkv_two,
        out_new,
        out_one,
        out_two,
        up_new,
        up_one,
        up_two,
        down_new,
        down_one,
        down_two,
        norm_new,
        norm_one,
        norm_two,
        shift_grad,
    )


def solution(mesh):
    tokens = P(("dp", "tensor"), None)
    columns = P("dp", None, "tensor")
    rows = P(("tensor", "dp"), None)
    both = P("dp", "tensor")
    norms = P(None, "dp")
    return jax.shard_map(
        on_device,
        mesh=mesh,
        in_specs=(tokens, tokens, P("dp"), P("dp", None), columns, rows, both, rows, norms)
        + (columns,) * 2
        + (rows,) * 2
        + (both,) * 2
        + (rows,) * 2
        + (norms,) * 2,
        out_specs=(tokens, tokens, P())
        + (columns,) * 3
        + (rows,) * 3
        + (both,) * 3
        + (rows,) * 3
        + (norms,) * 3
        + (P("dp"),),
        check_vma=False,
    )
```

```python
import functools

import jax
import jax.numpy as jnp
from jax import lax
from jax.experimental import pallas as pl
from jax.experimental.layout import Layout, with_layout_constraint
from jax.experimental.pallas import tpu as pltpu
from jax.sharding import PartitionSpec as P

HD = 64
STEP = 5

NORM_EPS = 1e-05
CLIP_LIMIT = 1.0
BETA_FIRST = 0.5
BETA_SECOND = 0.5
ADAM_EPS = 1e-08
DECAY_RATE = 0.01
RATE_QKV = 0.03
RATE_OUT = 0.5
RATE_UP = 0.03
RATE_DOWN = 0.015
RATE_NORM = 0.2

F32 = jnp.float32
BF16 = jnp.bfloat16
NN = (((1,), (0,)), ((), ()))
NT = (((1,), (1,)), ((), ()))
TN = (((0,), (0,)), ((), ()))
VMEM = pl.BlockSpec(memory_space=pltpu.VMEM)


def dot(left, right, dims=NN):
    return lax.dot_general(left, right, dims, preferred_element_type=F32)


def widen(block, columns, lane):
    rows = block.shape[0]
    wide = jnp.concatenate([block.astype(F32), jnp.zeros((rows, HD), F32)], axis=1)
    for n, column in enumerate(columns):
        wide = jnp.where(lane == HD + n, column, wide)
    return wide.astype(BF16)


def minus_parts(column):
    high = column.astype(BF16).astype(F32)
    rest = column - high
    middle = rest.astype(BF16).astype(F32)
    return [-high, -middle, middle - rest]


def attend_kernel(heads, step, one_ref, weight_ref, bias_ref, qkv_ref, ctx_ref, lse_ref, keys):
    tokens = qkv_ref.shape[0]
    width = heads * HD
    lane = lax.broadcasted_iota(jnp.int32, (1, 2 * HD), 1)

    def project(n, _):
        rows = pl.ds(pl.multiple_of(n * step, step), step)
        qkv_ref[rows, :] = dot(one_ref[rows, :], weight_ref[...]).astype(BF16)
        return 0

    lax.fori_loop(0, tokens // step, project, 0)
    bias = bias_ref[...].T[:, 0:1]
    for h in range(heads):
        keys[h] = widen(qkv_ref[:, width + h * HD : width + (h + 1) * HD], [bias], lane)

    def block(n, _):
        rows = pl.ds(pl.multiple_of(n * step, step), step)
        outs = []
        stat = jnp.zeros((step, 2 * HD), F32)
        for h in range(heads):
            query = qkv_ref[rows, h * HD : (h + 1) * HD].astype(F32) * HD ** (-0.5)
            scores = dot(widen(query, [jnp.ones((step, 1), F32)], lane), keys[h], NT)
            top = jnp.max(scores, axis=1, keepdims=True)
            weights = jnp.exp(scores - top)
            total = jnp.sum(weights, axis=1, keepdims=True)
            values = qkv_ref[:, 2 * width + h * HD : 2 * width + (h + 1) * HD]
            outs.append((dot(weights.astype(BF16), values) / total).astype(BF16))
            stat = jnp.where(lane == h, top + jnp.log(total), stat)
        ctx_ref[rows, :] = jnp.concatenate(outs, axis=1)
        lse_ref[rows, :] = stat
        return 0

    lax.fori_loop(0, tokens // step, block, 0)


def attend(one, weight, bias, heads, step=512):
    tokens = one.shape[0]
    return pl.pallas_call(
        functools.partial(attend_kernel, heads, step),
        out_shape=(
            jax.ShapeDtypeStruct((tokens, 3 * heads * HD), BF16),
            jax.ShapeDtypeStruct((tokens, heads * HD), BF16),
            jax.ShapeDtypeStruct((tokens, 2 * HD), F32),
        ),
        in_specs=[VMEM] * 3,
        out_specs=[VMEM] * 3,
        scratch_shapes=[pltpu.VMEM((heads, tokens, 2 * HD), BF16)],
        compiler_params=pltpu.CompilerParams(vmem_limit_bytes=48 * 2**20),
        cost_estimate=pl.CostEstimate(flops=0, bytes_accessed=1, transcendentals=0),
        name="attend",
    )(one, weight, bias)


def attend_back_kernel(
    heads,
    step,
    qkv_ref,
    bias_ref,
    ctx_ref,
    lse_ref,
    own_ref,
    mate_ref,
    weight_ref,
    out_ref,
    keys,
    values,
    dk,
    dv,
    grad_ref,
):
    tokens = qkv_ref.shape[0]
    width = heads * HD
    scale = HD ** (-0.5)
    lane = lax.broadcasted_iota(jnp.int32, (1, 2 * HD), 1)
    one = jnp.ones((tokens, 1), F32)
    bias = bias_ref[...].T[:, 0:1]
    half = tokens // 2
    for n, ref in enumerate((own_ref, mate_ref)):
        grad_ref[n * half : (n + 1) * half, :] = dot(ref[...], weight_ref[...], NT).astype(BF16)
    for h in range(heads):
        key = qkv_ref[:, width + h * HD : width + (h + 1) * HD]
        value = qkv_ref[:, 2 * width + h * HD : 2 * width + (h + 1) * HD]
        keys[h] = widen(key, [bias, one, one, one], lane)
        values[h] = widen(value, [one, one, one], lane)
    dk[...] = jnp.zeros_like(dk)
    dv[...] = jnp.zeros_like(dv)

    def block(n, _):
        rows = pl.ds(pl.multiple_of(n * step, step), step)
        outs = []
        ones = jnp.ones((step, 1), F32)
        for h in range(heads):
            cols = slice(h * HD, (h + 1) * HD)
            query = qkv_ref[rows, cols].astype(F32) * scale
            grad = grad_ref[rows, cols].astype(F32)
            delta = jnp.sum(grad * ctx_ref[rows, cols].astype(F32), axis=1, keepdims=True)
            lse = lse_ref[rows, h : h + 1]
            weights = jnp.exp(dot(widen(query, [ones] + minus_parts(lse), lane), keys[h], NT))
            slopes = dot(widen(grad, minus_parts(delta), lane), values[h], NT)
            slopes = (weights * slopes).astype(BF16)
            weights = weights.astype(BF16)
            key = qkv_ref[:, width + h * HD : width + (h + 1) * HD]
            outs.append((dot(slopes, key) * scale).astype(BF16))
            dk[h] += dot(query.T.astype(BF16), slopes)
            dv[h] += dot(grad.T.astype(BF16), weights)
        out_ref[rows, :width] = jnp.concatenate(outs, axis=1)
        return 0

    lax.fori_loop(0, tokens // step, block, 0)
    for place, total in ((1, dk), (2, dv)):
        turned = jnp.concatenate([total[h].T for h in range(heads)], axis=1)
        out_ref[:, place * width : (place + 1) * width] = turned.astype(BF16)


def attend_back(qkv, bias, ctx, lse, own, mate, weight, heads, step=256):
    tokens = qkv.shape[0]
    return pl.pallas_call(
        functools.partial(attend_back_kernel, heads, step),
        out_shape=jax.ShapeDtypeStruct((tokens, 3 * heads * HD), BF16),
        in_specs=[VMEM] * 7,
        out_specs=VMEM,
        scratch_shapes=[pltpu.VMEM((heads, tokens, 2 * HD), BF16)] * 2
        + [pltpu.VMEM((heads, HD, tokens), F32)] * 2
        + [pltpu.VMEM((tokens, heads * HD), BF16)],
        compiler_params=pltpu.CompilerParams(vmem_limit_bytes=48 * 2**20),
        cost_estimate=pl.CostEstimate(flops=0, bytes_accessed=1, transcendentals=0),
        name="attend_back",
    )(qkv, bias, ctx, lse, own, mate, weight)


def swap(value, axis, bits):
    size = lax.axis_size(axis)
    return lax.ppermute(value, axis, [(i, i ^ bits) for i in range(size)])


def core_swap(value):
    return swap(value, "tensor", 1)


def side_swap(value):
    return swap(value, "tensor", 2)


def tie(*values):
    return lax.optimization_barrier(values)


def dp_split(size):
    fast = 2 if size < 16 else 4
    return size // fast, fast


def high_swap(value, k):
    return swap(value, "dp", k * dp_split(lax.axis_size("dp"))[1])


def gather_small(shard):
    size = lax.axis_size("dp")
    blocks = shard[None]
    bits = 1
    while bits < size:
        blocks = jnp.concatenate([blocks, swap(blocks, "dp", bits)])
        bits *= 2
    index = lax.axis_index("dp")
    return jnp.stack([blocks[index ^ n] for n in range(size)])


def spread(block):
    _, fast = dp_split(lax.axis_size("dp"))
    return [block] + [swap(block, "dp", j) for j in range(1, fast)]


def entries(k, line, at=None):
    return [(k, j, block, at if j else None) for j, block in enumerate(line)]


def joined_entries(ks, blocks, others):
    return [
        entry
        for n, (k, block) in enumerate(zip(ks, blocks, strict=True))
        for entry in entries(k, [block, *others], n)
    ]


def pack_kernel(qkv_ref, out_ref, packed_ref):
    rows, width = out_ref.shape
    step = width * rows // qkv_ref.shape[0]
    parts = [qkv_ref[:, n, :] for n in range(qkv_ref.shape[1])]
    turned = [out_ref[:, n : n + step] for n in range(0, width, step)]
    packed = jnp.concatenate([*parts, jnp.concatenate(turned, axis=0)], axis=1)
    packed_ref[...] = packed.astype(BF16)


def pack_first(qkv, out):
    shape = (qkv.shape[0], qkv.shape[1] * qkv.shape[2] + out.size // qkv.shape[0])
    if out.shape[0] % 8:
        step = out.shape[1] * out.shape[0] // qkv.shape[0]
        turned = jnp.concatenate([out[:, n : n + step] for n in range(0, out.shape[1], step)])
        packed = jnp.concatenate([qkv.reshape(qkv.shape[0], -1), turned], axis=1)
        return packed.astype(BF16)
    return pl.pallas_call(
        pack_kernel,
        out_shape=jax.ShapeDtypeStruct(shape, BF16),
        in_specs=[VMEM] * 2,
        out_specs=VMEM,
        compiler_params=pltpu.CompilerParams(vmem_limit_bytes=16 * 2**20),
        cost_estimate=pl.CostEstimate(flops=0, bytes_accessed=1, transcendentals=0),
        name="pack_first",
    )(qkv, out)


def assemble(blocks, cut=None):
    slow, fast = dp_split(lax.axis_size("dp"))
    rows, columns = blocks[0][2].shape[-2:]
    kind = blocks[0][2].dtype
    index = lax.axis_index("dp")
    place = jnp.stack([index // fast, index % fast]).astype(jnp.int32)
    where = [(k, j, at) for k, j, _, at in blocks]
    out_rows = rows * (columns - cut) // columns if cut else 0

    def kernel(place_ref, *refs):
        ins, outs = refs[: len(where)], refs[len(where) : -2]
        whole, sems = refs[-2:] if cut else (outs[0], refs[-1])
        copies = []
        for n, (source, (k, j, at)) in enumerate(zip(ins, where, strict=True)):
            target = (place_ref[0] ^ k) * fast + (place_ref[1] ^ j)
            source = source if at is None else source.at[at]
            copies.append(pltpu.make_async_copy(source, whole.at[target], sems.at[n]))
        for copy in copies:
            copy.start()
        for copy in copies:
            copy.wait()
        if cut:
            outs[0][...] = whole[:, :, :cut]
            if out_rows % 8:
                outs[1][...] = whole[:, :, cut:]
            else:
                turned = []
                for n in range(slow * fast):
                    block = whole[n, :, cut:].astype(F32)
                    parts = [block[m : m + out_rows] for m in range(0, rows, out_rows)]
                    turned.append(jnp.concatenate(parts, axis=1))
                outs[1][...] = jnp.concatenate(turned, axis=0).astype(kind)

    size = slow * fast
    full = (size, rows, columns)
    if not cut:
        shapes = [full]
    elif out_rows % 8:
        shapes = [(size, rows, cut), (size, rows, columns - cut)]
    else:
        shapes = [(size, rows, cut), (size * out_rows, columns)]
    outs = pl.pallas_call(
        kernel,
        out_shape=[jax.ShapeDtypeStruct(shape, kind) for shape in shapes],
        in_specs=[pl.BlockSpec(memory_space=pltpu.SMEM)]
        + [pl.BlockSpec(memory_space=pltpu.HBM)] * len(where),
        out_specs=[VMEM] * len(shapes),
        scratch_shapes=[
            pltpu.VMEM(full if cut else (8, 16, 128), kind),
            pltpu.SemaphoreType.DMA((len(where),)),
        ],
        compiler_params=pltpu.CompilerParams(vmem_limit_bytes=24 * 2**20),
        cost_estimate=pl.CostEstimate(flops=0, bytes_accessed=1, transcendentals=0),
        name="assemble",
    )(place, *[array for _, _, array, _ in blocks])
    outs = list(outs)
    if cut and out_rows % 8:
        turned = outs[1].reshape(size, rows // out_rows, out_rows, columns - cut)
        outs[1] = turned.transpose(0, 2, 1, 3).reshape(size * out_rows, columns)
    return [out.reshape(-1, out.shape[-1]) for out in outs]


def pick(total, k, j):
    slow, fast = dp_split(lax.axis_size("dp"))
    rows = total.shape[0] // (slow * fast)
    index = lax.axis_index("dp")
    start = (((index // fast) ^ k) * fast + ((index % fast) ^ j)) * rows
    return lax.dynamic_slice_in_dim(total, start, rows, 0)


def rows_first(value):
    return with_layout_constraint(value, Layout(tuple(range(value.ndim))))


def scatter_send(total, ks):
    _, fast = dp_split(lax.axis_size("dp"))
    return [
        swap(jnp.concatenate([rows_first(pick(total, k, j)) for k in ks]), "dp", j)
        for j in range(1, fast)
    ]


def scatter_lines(total, ks, received):
    lines = {}
    for n, k in enumerate(ks):
        line = pick(total, k, 0).astype(F32)
        rows = line.shape[0]
        for part in received:
            line = line + part[n * rows : (n + 1) * rows].astype(F32)
        lines[k] = rows_first(line.astype(BF16))
    return lines


def relay_ks():
    slow, _ = dp_split(lax.axis_size("dp"))
    return [1, *range(2, slow, 2)], [*range(3, slow, 2), 0]


def relay_send(lines):
    ks, _ = relay_ks()
    return high_swap(jnp.concatenate([lines[k] for k in ks]), 1)


def relay_split(received):
    ks, _ = relay_ks()
    rows = received.shape[0] // len(ks)
    return {k: received[n * rows : (n + 1) * rows] for n, k in enumerate(ks)}


def relay_last(lines, received):
    _, ks = relay_ks()
    got = relay_split(received)
    parts = [lines[0], got[1]]
    for k in ks[:-1]:
        line = lines[k].astype(F32) + got[k ^ 1].astype(F32)
        parts.append(high_swap(line.astype(BF16), k))
    return parts


def parts_sum(parts):
    return functools.reduce(jnp.add, [part.astype(F32) for part in parts])


def cores_sum(left, right, dims=NN):
    return own_sum(left, right, mates_part(left, right, dims), dims)


def mates_part(left, right, dims=NN):
    return core_swap(dot(left[left.shape[0] // 2 :], right, dims).astype(BF16))


def own_sum(left, right, mate, dims=NN):
    return dot(left[: left.shape[0] // 2], right, dims) + mate.astype(F32)


def side_send(value):
    half = value.shape[0] // 2
    return [side_swap(value[:half]), side_swap(value[half:])]


def join(parts):
    return jnp.concatenate(parts)


def with_mate(own):
    return jnp.concatenate([own, core_swap(own)])


def norm_kernel(top_ref, rest_ref, rows_ref, out_ref):
    gain, shift = rows_ref[0:1, :], rows_ref[1:2, :]
    for n, ref in enumerate((top_ref, rest_ref)):
        values = ref[...].astype(F32)
        centered = values - jnp.mean(values, axis=-1, keepdims=True)
        inverse = lax.rsqrt(jnp.mean(centered * centered, axis=-1, keepdims=True) + NORM_EPS)
        out_ref[n] = (centered * inverse * gain + shift).astype(BF16)


def norm_tokens(top, rest, rows, step=128):
    half, width = top.shape
    block = pl.BlockSpec((step, width), lambda i: (i, 0))
    out = pl.pallas_call(
        norm_kernel,
        grid=(half // step,),
        out_shape=jax.ShapeDtypeStruct((2, half, width), BF16),
        in_specs=[block, block, pl.BlockSpec((2, width), lambda i: (0, 0))],
        out_specs=pl.BlockSpec((2, step, width), lambda i: (0, i, 0)),
        compiler_params=pltpu.CompilerParams(vmem_limit_bytes=24 * 2**20),
        cost_estimate=pl.CostEstimate(flops=0, bytes_accessed=1, transcendentals=0),
        name="norm_tokens",
    )(top, rest, rows)
    return out.reshape(2 * half, width)


def sum_all(value):
    size = lax.axis_size("dp")
    value = value + core_swap(value)
    steps = [("tensor", 2)] + [("dp", 1 << n) for n in range(size.bit_length() - 1)]
    for n in range(0, len(steps), 2):
        first = steps[n]
        if n + 1 == len(steps):
            value = value + swap(value, *first)
            continue
        second = steps[n + 1]
        if first[0] == second[0]:
            both = swap(value, first[0], first[1] | second[1])
        else:
            tensor = lax.axis_size("tensor")
            bits = first[1] | second[1] * tensor
            pairs = [(i, i ^ bits) for i in range(size * tensor)]
            both = lax.ppermute(value, ("dp", "tensor"), pairs)
        value = (value + swap(value, *first)) + (swap(value, *second) + both)
    return value


def layer_norm_parts(values, gain_row, shift_row):
    centered = values - jnp.mean(values, axis=-1, keepdims=True)
    inverse = lax.rsqrt(jnp.mean(centered * centered, axis=-1, keepdims=True) + NORM_EPS)
    normed = centered * inverse
    return (normed * gain_row + shift_row, normed, inverse)


def layer_norm_back(grad_normed, normed, inverse, gain_row):
    scaled = grad_normed * gain_row
    return inverse * (
        scaled
        - jnp.mean(scaled, axis=-1, keepdims=True)
        - normed * jnp.mean(scaled * normed, axis=-1, keepdims=True)
    )


def adam_update(master, grad_sum, moment_one, moment_two, step_rate, clip_factor):
    clipped = grad_sum * clip_factor
    one_new = BETA_FIRST * moment_one + (1.0 - BETA_FIRST) * clipped
    two_new = BETA_SECOND * moment_two + (1.0 - BETA_SECOND) * clipped * clipped
    one_hat = one_new / (1.0 - BETA_FIRST**STEP)
    two_hat = two_new / (1.0 - BETA_SECOND**STEP)
    master_new = master - step_rate * (
        one_hat / (jnp.sqrt(two_hat) + ADAM_EPS) + DECAY_RATE * master
    )
    return (master_new, one_new, two_new)


def gelu_parts(value):
    share = 0.5 + 0.5 * lax.erf(value * 0.5**0.5)
    slope = share + value * jnp.exp(-0.5 * value * value) * (0.5 / jnp.pi) ** 0.5
    return (value * share).astype(BF16), slope.astype(BF16)


def on_device(
    tokens,
    cotangent,
    lengths,
    key_mask,
    qkv_weight,
    out_weight,
    up_weight,
    down_weight,
    norm_params,
    qkv_first,
    qkv_second,
    out_first,
    out_second,
    up_first,
    up_second,
    down_first,
    down_second,
    norm_first,
    norm_second,
):
    own, width = tokens.shape
    cell = 2 * own
    heads = qkv_weight.shape[2] // HD
    dp, tensor = lax.axis_index("dp"), lax.axis_index("tensor")
    side, core = tensor // 2, tensor % 2

    norm_rows = norm_params.shape[1]

    positions = jnp.arange(cell, dtype=jnp.int32)
    key_valid = (positions[None, :] < lengths[:, None]) & (
        (key_mask == 1) | (positions[None, :] == 0)
    )
    bias = jnp.where(key_valid, 0.0, -1e30).astype(F32)
    bias = jnp.where(side == 0, bias, bias[::-1])
    bias = jnp.where(core == 0, bias, jnp.roll(bias, own, axis=1))
    bias_near, bias_far = [jnp.broadcast_to(row, (8, cell)) for row in bias]

    slow, _ = dp_split(lax.axis_size("dp"))
    odds, evens = list(range(1, slow, 2)), list(range(2, slow, 2))
    qkv_width = 3 * heads * HD
    head = own // 4
    first_low = pack_first(qkv_weight, out_weight)
    first = {k: high_swap(first_low, k) for k in odds}
    first_own = spread(first_low)
    side_top = side_swap(tokens[:head])
    mate_tokens = core_swap(tokens)
    norm_low, mate_tokens = tie(norm_params.astype(BF16), mate_tokens)
    norm_low = gather_small(norm_low)
    up_low, down_low = up_weight.astype(BF16), down_weight.astype(BF16)
    both_low = jnp.stack([up_low, down_low])
    first, first_own, side_top, tokens, up_low, down_low, both_low = tie(
        first, first_own, side_top, tokens, up_low, down_low, both_low
    )
    for k in evens:
        first[k] = high_swap(first[k ^ 1], 1)
    first_lines = {k: spread(first[k]) for k in odds}
    side_rest = side_swap(tokens[head:])
    norm_values = jnp.moveaxis(norm_low, 0, 1).reshape(4, width).astype(F32)
    one_near = norm_tokens(tokens, mate_tokens, norm_values[:2])
    first, first_lines, one_near, side_rest, up_low, down_low, cotangent = tie(
        first, first_lines, one_near, side_rest, up_low, down_low, cotangent
    )
    for k in evens:
        first_lines[k] = spread(first[k])
    side_tokens = join([side_top, side_rest])
    one_far = norm_tokens(side_tokens, core_swap(side_tokens), norm_values[:2])
    up = {k: high_swap(up_low, k) for k in odds}
    cot_side = side_swap(cotangent)
    first_lines, one_far, both_low = tie(first_lines, one_far, both_low)
    both_own = spread(both_low)[1:]

    qkv_full, out_full = assemble(
        sum([entries(k, line) for k, line in first_lines.items()], entries(0, first_own)),
        qkv_width,
    )
    qkv_far, ctx_far, lse_far = attend(one_far, qkv_full, bias_far, heads)
    ctx_far, up, both_own, cot_side, down_low = tie(ctx_far, up, both_own, cot_side, down_low)
    for k in evens:
        up[k] = high_swap(up[k ^ 1], 1)
    up_others = spread(jnp.stack([up[k] for k in odds]))[1:]
    down = {k: high_swap(down_low, k) for k in odds}
    far_sum = cores_sum(ctx_far, out_full).astype(BF16)
    far_sum, one_near, qkv_full = tie(far_sum, one_near, qkv_full)
    out_far = side_swap(far_sum)
    qkv_near, ctx_near, lse_near = attend(one_near, qkv_full, bias_near, heads)
    ctx_near, out_far, up, up_others, down, cotangent, cot_side = tie(
        ctx_near, out_far, up, up_others, down, cotangent, cot_side
    )
    for k in evens:
        down[k] = high_swap(down[k ^ 1], 1)
    down_others = spread(jnp.stack([down[k] for k in odds]))[1:]
    up_even = [entry for k in evens for entry in entries(k, spread(up[k]))]
    grad_near = with_mate(cotangent)
    grad_far = with_mate(cot_side)
    out_near = cores_sum(ctx_near, out_full)
    stream_in = tokens.astype(F32)
    residual = stream_in + (out_near + out_far.astype(F32))

    ln_two, normed_two, inverse_two = layer_norm_parts(residual, norm_values[2], norm_values[3])
    ln_two = ln_two.astype(BF16)
    two_near = with_mate(ln_two)
    two_side = side_swap(ln_two)
    arrays = [array for _, _, array, _ in up_even]
    two_near, arrays, down = tie(two_near, arrays, down)
    up_even = [(k, j, array, at) for (k, j, _, at), array in zip(up_even, arrays, strict=True)]
    (up_full,) = assemble(
        [(0, 0, up_low, None)]
        + [(0, j + 1, block, 0) for j, block in enumerate(both_own)]
        + joined_entries(odds, [up[k] for k in odds], up_others)
        + up_even
    )
    hid_near, slope_near = gelu_parts(dot(two_near, up_full))
    down_even = [entry for k in evens for entry in entries(k, spread(down[k]))]
    arrays = [array for _, _, array, _ in down_even]
    hid_near, arrays, down_others, grad_near, grad_far = tie(
        hid_near, arrays, down_others, grad_near, grad_far
    )
    down_even = [(k, j, array, at) for (k, j, _, at), array in zip(down_even, arrays, strict=True)]
    (down_full,) = assemble(
        [(0, 0, down_low, None)]
        + [(0, j + 1, block, 1) for j, block in enumerate(both_own)]
        + joined_entries(odds, [down[k] for k in odds], down_others)
        + down_even
    )
    pre_near = (dot(grad_near, down_full, NT) * slope_near.astype(F32)).astype(BF16)
    pre_near, hid_near, two_side = tie(pre_near, hid_near, two_side)
    two_far = with_mate(two_side)
    hid_far, slope_far = gelu_parts(dot(two_far, up_full))
    pre_far = (dot(grad_far, down_full, NT) * slope_far.astype(F32)).astype(BF16)
    far_sum = cores_sum(pre_far, up_full, NT).astype(BF16)
    far_sum, pre_near, pre_far, hid_near, hid_far = tie(
        far_sum, pre_near, pre_far, hid_near, hid_far
    )
    back_far = side_swap(far_sum)
    back_near = cores_sum(pre_near, up_full, NT)
    back_near, hid_near, hid_far, grad_near, grad_far = tie(
        back_near, hid_near, hid_far, grad_near, grad_far
    )
    heavy, light = relay_ks()
    order = heavy + light
    grad_down = dot(join([hid_near, hid_far]), join([grad_near, grad_far]), TN).astype(BF16)
    grad_down, hid_near, hid_far = tie(grad_down, hid_near, hid_far)
    down_received = [scatter_send(grad_down, heavy)]
    last_terms = [dot(v[own:], down_full).astype(BF16) for v in (hid_far, hid_near)]
    last_terms, grad_down, back_far, pre_near, pre_far, down_received = tie(
        last_terms, grad_down, back_far, pre_near, pre_far, down_received
    )
    grad_ln_two = back_near + back_far.astype(F32)
    grad_residual = cotangent.astype(F32) + layer_norm_back(
        grad_ln_two, normed_two, inverse_two, norm_values[2]
    )
    gain_two = jnp.sum(grad_ln_two * normed_two, axis=0)
    shift_two = jnp.sum(grad_ln_two, axis=0)

    res_low = grad_residual.astype(BF16)
    res_side = side_swap(res_low)
    res_mate = core_swap(res_low)
    last_mates = [core_swap(v) for v in last_terms]
    down_lines = scatter_lines(grad_down, heavy, down_received[0])
    res_mate, last_mates, pre_near, pre_far, down_lines = tie(
        res_mate, last_mates, pre_near, pre_far, down_lines
    )
    down_got = relay_send(down_lines)
    down_received.append(scatter_send(grad_down, light))
    grad_up = dot(join([two_near, two_far]), join([pre_near, pre_far]), TN).astype(BF16)
    grad_up, res_mate = tie(grad_up, res_mate)
    up_received = [scatter_send(grad_up, heavy)]
    dqkv_near = attend_back(
        qkv_near, bias_near, ctx_near, lse_near, res_low, res_mate, out_full, heads
    )
    (
        dqkv_near, res_side, up_received, grad_up, down_got, down_received, grad_down,
        last_mates, hid_far,
    ) = tie(
        dqkv_near, res_side, up_received, grad_up, down_got, down_received, grad_down,
        last_mates, hid_far,
    )
    res_side_mate = core_swap(res_side)
    down_lines.update(scatter_lines(grad_down, light, down_received[1]))
    up_lines = scatter_lines(grad_up, heavy, up_received[0])
    last_far = own_sum(hid_far, down_full, last_mates[0]).astype(BF16)
    grad_out = dot(
        join([ctx_near, ctx_far]), join([res_low, res_mate, res_side, res_side_mate]), TN
    ).astype(BF16)
    res_side_mate, grad_out, down_lines, up_lines, last_far = tie(
        res_side_mate, grad_out, down_lines, up_lines, last_far
    )
    up_received.append(scatter_send(grad_up, light))
    out_received = scatter_send(grad_out, order)
    down_parts = relay_last(down_lines, down_got)
    up_got = relay_send(up_lines)
    last_side = side_swap(last_far)
    dqkv_far = attend_back(
        qkv_far, bias_far, ctx_far, lse_far, res_side, res_side_mate, out_full, heads
    )
    dqkv_far, up_got, up_received, grad_up, down_parts, grad_out, out_received = tie(
        dqkv_far, up_got, up_received, grad_up, down_parts, grad_out, out_received
    )

    up_lines.update(scatter_lines(grad_up, light, up_received[1]))
    out_lines = scatter_lines(grad_out, order, out_received)
    dqkv_far, dqkv_near, up_lines, out_lines = tie(dqkv_far, dqkv_near, up_lines, out_lines)
    up_parts = relay_last(up_lines, up_got)
    out_got = relay_send(out_lines)
    grad_qkv = dot(join([one_near, one_far]), join([dqkv_near, dqkv_far]), TN).astype(BF16)
    grad_qkv, dqkv_far, dqkv_near = tie(rows_first(grad_qkv), dqkv_far, dqkv_near)
    received = [scatter_send(grad_qkv, heavy)]
    first_mates = [mates_part(v, qkv_full, NT) for v in (dqkv_far, dqkv_near)]
    far_sum = own_sum(dqkv_far, qkv_full, first_mates[0], NT).astype(BF16)
    far_sum, first_mates, grad_qkv, dqkv_near, hid_near = tie(
        far_sum, first_mates, grad_qkv, dqkv_near, hid_near
    )
    first_far = side_swap(far_sum)
    received.append(scatter_send(grad_qkv, light))
    first_near = own_sum(dqkv_near, qkv_full, first_mates[1], NT)
    first_near, received[0], grad_qkv, hid_near = tie(first_near, received[0], grad_qkv, hid_near)
    qkv_lines = scatter_lines(grad_qkv, heavy, received[0])
    qkv_got = relay_send(qkv_lines)
    last_near = own_sum(hid_near, down_full, last_mates[1])
    layer_out = (residual + (last_near + last_side.astype(F32))).astype(BF16)
    (
        received[1], qkv_got, qkv_lines, out_got, out_lines, layer_out, up_parts, down_parts,
        grad_qkv,
    ) = tie(
        received[1], qkv_got, qkv_lines, out_got, out_lines, layer_out, up_parts, down_parts,
        grad_qkv,
    )
    qkv_lines.update(scatter_lines(grad_qkv, light, received[1]))
    qkv_parts = relay_last(qkv_lines, qkv_got)
    out_parts = relay_last(out_lines, out_got)
    summed_up, summed_down = parts_sum(up_parts), parts_sum(down_parts)
    early_squares = jnp.sum(summed_up * summed_up) + jnp.sum(summed_down * summed_down)

    _, normed_one, inverse_one = layer_norm_parts(stream_in, norm_values[0], norm_values[1])
    grad_ln_one = first_near + first_far.astype(F32)
    input_grad = (
        grad_residual + layer_norm_back(grad_ln_one, normed_one, inverse_one, norm_values[0])
    ).astype(BF16)
    gain_one = jnp.sum(grad_ln_one * normed_one, axis=0)
    shift_one = jnp.sum(grad_ln_one, axis=0)
    rows = jnp.stack([gain_one, shift_one, gain_two, shift_two])
    qkv_parts, out_parts, rows, input_grad, early_squares = tie(
        qkv_parts, out_parts, rows, input_grad, early_squares
    )
    summed_qkv, summed_out = parts_sum(qkv_parts), parts_sum(out_parts)
    early_squares = early_squares + jnp.sum(summed_out * summed_out)

    local_squares = early_squares + jnp.sum(summed_qkv * summed_qkv)
    packed = jnp.concatenate([rows, jnp.full((4, 128), local_squares, F32)], axis=1)
    packed = sum_all(packed)
    norm_grad = packed[:, :width]
    squares_total = packed[0, width] + jnp.sum(norm_grad * norm_grad)
    summed_norm = lax.dynamic_slice_in_dim(norm_grad, dp * norm_rows, norm_rows, 1)
    grad_norm = jnp.sqrt(squares_total)
    clip_factor = jnp.minimum(1.0, CLIP_LIMIT / grad_norm)

    qkv_new, qkv_one, qkv_two = adam_update(
        qkv_weight,
        summed_qkv.reshape(qkv_weight.shape),
        qkv_first,
        qkv_second,
        RATE_QKV,
        clip_factor,
    )
    out_new, out_one, out_two = adam_update(
        out_weight, summed_out, out_first, out_second, RATE_OUT, clip_factor
    )
    up_new, up_one, up_two = adam_update(
        up_weight, summed_up, up_first, up_second, RATE_UP, clip_factor
    )
    down_new, down_one, down_two = adam_update(
        down_weight, summed_down, down_first, down_second, RATE_DOWN, clip_factor
    )
    norm_new, norm_one, norm_two = adam_update(
        norm_params, summed_norm, norm_first, norm_second, RATE_NORM, clip_factor
    )
    shift_grad = clip_factor * summed_norm[3]
    return (
        layer_out,
        input_grad,
        grad_norm,
        qkv_new,
        qkv_one,
        qkv_two,
        out_new,
        out_one,
        out_two,
        up_new,
        up_one,
        up_two,
        down_new,
        down_one,
        down_two,
        norm_new,
        norm_one,
        norm_two,
        shift_grad,
    )


def solution(mesh):
    tokens = P(("dp", "tensor"), None)
    columns = P("dp", None, "tensor")
    rows = P(("tensor", "dp"), None)
    both = P("dp", "tensor")
    norms = P(None, "dp")
    return jax.shard_map(
        on_device,
        mesh=mesh,
        in_specs=(tokens, tokens, P("dp"), P("dp", None), columns, rows, both, rows, norms)
        + (columns,) * 2
        + (rows,) * 2
        + (both,) * 2
        + (rows,) * 2
        + (norms,) * 2,
        out_specs=(tokens, tokens, P())
        + (columns,) * 3
        + (rows,) * 3
        + (both,) * 3
        + (rows,) * 3
        + (norms,) * 3
        + (P("dp"),),
        check_vma=False,
    )
```

```python
import functools

import jax
import jax.numpy as jnp
from jax import lax
from jax.experimental import pallas as pl
from jax.experimental.layout import Layout, with_layout_constraint
from jax.experimental.pallas import tpu as pltpu
from jax.sharding import PartitionSpec as P

HD = 64
STEP = 5

NORM_EPS = 1e-05
CLIP_LIMIT = 1.0
BETA_FIRST = 0.5
BETA_SECOND = 0.5
ADAM_EPS = 1e-08
DECAY_RATE = 0.01
RATE_QKV = 0.03
RATE_OUT = 0.5
RATE_UP = 0.03
RATE_DOWN = 0.015
RATE_NORM = 0.2

F32 = jnp.float32
BF16 = jnp.bfloat16
NN = (((1,), (0,)), ((), ()))
NT = (((1,), (1,)), ((), ()))
TN = (((0,), (0,)), ((), ()))
VMEM = pl.BlockSpec(memory_space=pltpu.VMEM)


def dot(left, right, dims=NN):
    return lax.dot_general(left, right, dims, preferred_element_type=F32)


def widen(block, columns, lane):
    rows = block.shape[0]
    wide = jnp.concatenate([block.astype(F32), jnp.zeros((rows, HD), F32)], axis=1)
    for n, column in enumerate(columns):
        wide = jnp.where(lane == HD + n, column, wide)
    return wide.astype(BF16)


def minus_parts(column):
    high = column.astype(BF16).astype(F32)
    rest = column - high
    middle = rest.astype(BF16).astype(F32)
    return [-high, -middle, middle - rest]


def attend_kernel(heads, step, one_ref, weight_ref, bias_ref, qkv_ref, ctx_ref, lse_ref, keys):
    tokens = qkv_ref.shape[0]
    width = heads * HD
    lane = lax.broadcasted_iota(jnp.int32, (1, 2 * HD), 1)

    def project(n, _):
        rows = pl.ds(pl.multiple_of(n * step, step), step)
        qkv_ref[rows, :] = dot(one_ref[rows, :], weight_ref[...]).astype(BF16)
        return 0

    lax.fori_loop(0, tokens // step, project, 0)
    bias = bias_ref[...].T[:, 0:1]
    for h in range(heads):
        keys[h] = widen(qkv_ref[:, width + h * HD : width + (h + 1) * HD], [bias], lane)

    def block(n, _):
        rows = pl.ds(pl.multiple_of(n * step, step), step)
        outs = []
        stat = jnp.zeros((step, 2 * HD), F32)
        for h in range(heads):
            query = qkv_ref[rows, h * HD : (h + 1) * HD].astype(F32) * HD ** (-0.5)
            scores = dot(widen(query, [jnp.ones((step, 1), F32)], lane), keys[h], NT)
            top = jnp.max(scores, axis=1, keepdims=True)
            weights = jnp.exp(scores - top)
            total = jnp.sum(weights, axis=1, keepdims=True)
            values = qkv_ref[:, 2 * width + h * HD : 2 * width + (h + 1) * HD]
            outs.append((dot(weights.astype(BF16), values) / total).astype(BF16))
            stat = jnp.where(lane == h, top + jnp.log(total), stat)
        ctx_ref[rows, :] = jnp.concatenate(outs, axis=1)
        lse_ref[rows, :] = stat
        return 0

    lax.fori_loop(0, tokens // step, block, 0)


def attend(one, weight, bias, heads, step=1024):
    tokens = one.shape[0]
    return pl.pallas_call(
        functools.partial(attend_kernel, heads, step),
        out_shape=(
            jax.ShapeDtypeStruct((tokens, 3 * heads * HD), BF16),
            jax.ShapeDtypeStruct((tokens, heads * HD), BF16),
            jax.ShapeDtypeStruct((tokens, 2 * HD), F32),
        ),
        in_specs=[VMEM] * 3,
        out_specs=[VMEM] * 3,
        scratch_shapes=[pltpu.VMEM((heads, tokens, 2 * HD), BF16)],
        compiler_params=pltpu.CompilerParams(vmem_limit_bytes=48 * 2**20),
        cost_estimate=pl.CostEstimate(flops=0, bytes_accessed=1, transcendentals=0),
        name="attend",
    )(one, weight, bias)


def attend_back_kernel(
    heads,
    step,
    qkv_ref,
    bias_ref,
    ctx_ref,
    lse_ref,
    own_ref,
    mate_ref,
    weight_ref,
    out_ref,
    keys,
    values,
    dk,
    dv,
    grad_ref,
):
    tokens = qkv_ref.shape[0]
    width = heads * HD
    scale = HD ** (-0.5)
    lane = lax.broadcasted_iota(jnp.int32, (1, 2 * HD), 1)
    one = jnp.ones((tokens, 1), F32)
    bias = bias_ref[...].T[:, 0:1]
    half = tokens // 2
    for n, ref in enumerate((own_ref, mate_ref)):
        grad_ref[n * half : (n + 1) * half, :] = dot(ref[...], weight_ref[...], NT).astype(BF16)
    for h in range(heads):
        key = qkv_ref[:, width + h * HD : width + (h + 1) * HD]
        value = qkv_ref[:, 2 * width + h * HD : 2 * width + (h + 1) * HD]
        keys[h] = widen(key, [bias, one, one, one], lane)
        values[h] = widen(value, [one, one, one], lane)
    dk[...] = jnp.zeros_like(dk)
    dv[...] = jnp.zeros_like(dv)

    def block(n, _):
        rows = pl.ds(pl.multiple_of(n * step, step), step)
        outs = []
        ones = jnp.ones((step, 1), F32)
        for h in range(heads):
            cols = slice(h * HD, (h + 1) * HD)
            query = qkv_ref[rows, cols].astype(F32) * scale
            grad = grad_ref[rows, cols].astype(F32)
            delta = jnp.sum(grad * ctx_ref[rows, cols].astype(F32), axis=1, keepdims=True)
            lse = lse_ref[rows, h : h + 1]
            weights = jnp.exp(dot(widen(query, [ones] + minus_parts(lse), lane), keys[h], NT))
            slopes = dot(widen(grad, minus_parts(delta), lane), values[h], NT)
            slopes = (weights * slopes).astype(BF16)
            weights = weights.astype(BF16)
            key = qkv_ref[:, width + h * HD : width + (h + 1) * HD]
            outs.append((dot(slopes, key) * scale).astype(BF16))
            dk[h] += dot(query.T.astype(BF16), slopes)
            dv[h] += dot(grad.T.astype(BF16), weights)
        out_ref[rows, :width] = jnp.concatenate(outs, axis=1)
        return 0

    lax.fori_loop(0, tokens // step, block, 0)
    for place, total in ((1, dk), (2, dv)):
        turned = jnp.concatenate([total[h].T for h in range(heads)], axis=1)
        out_ref[:, place * width : (place + 1) * width] = turned.astype(BF16)


def attend_back(qkv, bias, ctx, lse, own, mate, weight, heads, step=1024):
    tokens = qkv.shape[0]
    return pl.pallas_call(
        functools.partial(attend_back_kernel, heads, step),
        out_shape=jax.ShapeDtypeStruct((tokens, 3 * heads * HD), BF16),
        in_specs=[VMEM] * 7,
        out_specs=VMEM,
        scratch_shapes=[pltpu.VMEM((heads, tokens, 2 * HD), BF16)] * 2
        + [pltpu.VMEM((heads, HD, tokens), F32)] * 2
        + [pltpu.VMEM((tokens, heads * HD), BF16)],
        compiler_params=pltpu.CompilerParams(vmem_limit_bytes=48 * 2**20),
        cost_estimate=pl.CostEstimate(flops=0, bytes_accessed=1, transcendentals=0),
        name="attend_back",
    )(qkv, bias, ctx, lse, own, mate, weight)


def swap(value, axis, bits):
    size = lax.axis_size(axis)
    return lax.ppermute(value, axis, [(i, i ^ bits) for i in range(size)])


def core_swap(value):
    return swap(value, "tensor", 1)


def side_swap(value):
    return swap(value, "tensor", 2)


def tie(*values):
    return lax.optimization_barrier(values)


def dp_split(size):
    fast = 2 if size < 16 else 4
    return size // fast, fast


def high_swap(value, k):
    return swap(value, "dp", k * dp_split(lax.axis_size("dp"))[1])


def gather_small(shard):
    size = lax.axis_size("dp")
    blocks = shard[None]
    bits = 1
    while bits < size:
        blocks = jnp.concatenate([blocks, swap(blocks, "dp", bits)])
        bits *= 2
    index = lax.axis_index("dp")
    return jnp.stack([blocks[index ^ n] for n in range(size)])


def spread(block):
    _, fast = dp_split(lax.axis_size("dp"))
    return [block] + [swap(block, "dp", j) for j in range(1, fast)]


def entries(k, line, at=None):
    return [(k, j, block, at if j else None) for j, block in enumerate(line)]


def joined_entries(ks, blocks, others):
    return [
        entry
        for n, (k, block) in enumerate(zip(ks, blocks, strict=True))
        for entry in entries(k, [block, *others], n)
    ]


def pack_kernel(qkv_ref, out_ref, packed_ref):
    rows, width = out_ref.shape
    step = width * rows // qkv_ref.shape[1]
    parts = [qkv_ref[n] for n in range(qkv_ref.shape[0])]
    turned = [out_ref[:, n : n + step] for n in range(0, width, step)]
    packed = jnp.concatenate([*parts, jnp.concatenate(turned, axis=0)], axis=1)
    packed_ref[...] = packed.astype(BF16)


def pack_first(qkv, out):
    rows = qkv.shape[1]
    shape = (rows, qkv.shape[0] * qkv.shape[2] + out.size // rows)
    if out.shape[0] % 8:
        step = out.shape[1] * out.shape[0] // rows
        turned = jnp.concatenate([out[:, n : n + step] for n in range(0, out.shape[1], step)])
        return jnp.concatenate([*qkv, turned], axis=1).astype(BF16)
    return pl.pallas_call(
        pack_kernel,
        out_shape=jax.ShapeDtypeStruct(shape, BF16),
        in_specs=[VMEM] * 2,
        out_specs=VMEM,
        compiler_params=pltpu.CompilerParams(vmem_limit_bytes=16 * 2**20),
        cost_estimate=pl.CostEstimate(flops=0, bytes_accessed=1, transcendentals=0),
        name="pack_first",
    )(qkv, out)


def assemble(blocks, cut=None):
    slow, fast = dp_split(lax.axis_size("dp"))
    rows, columns = blocks[0][2].shape[-2:]
    kind = blocks[0][2].dtype
    index = lax.axis_index("dp")
    place = jnp.stack([index // fast, index % fast]).astype(jnp.int32)
    where = [(k, j, at) for k, j, _, at in blocks]
    out_rows = rows * (columns - cut) // columns if cut else 0

    def kernel(place_ref, *refs):
        ins, outs = refs[: len(where)], refs[len(where) : -2]
        whole, sems = refs[-2:] if cut else (outs[0], refs[-1])
        copies = []
        for n, (source, (k, j, at)) in enumerate(zip(ins, where, strict=True)):
            target = (place_ref[0] ^ k) * fast + (place_ref[1] ^ j)
            source = source if at is None else source.at[at]
            copies.append(pltpu.make_async_copy(source, whole.at[target], sems.at[n]))
        for copy in copies:
            copy.start()
        for copy in copies:
            copy.wait()
        if cut:
            outs[0][...] = whole[:, :, :cut]
            if out_rows % 8:
                outs[1][...] = whole[:, :, cut:]
            else:
                turned = []
                for n in range(slow * fast):
                    block = whole[n, :, cut:].astype(F32)
                    parts = [block[m : m + out_rows] for m in range(0, rows, out_rows)]
                    turned.append(jnp.concatenate(parts, axis=1))
                outs[1][...] = jnp.concatenate(turned, axis=0).astype(kind)

    size = slow * fast
    full = (size, rows, columns)
    if not cut:
        shapes = [full]
    elif out_rows % 8:
        shapes = [(size, rows, cut), (size, rows, columns - cut)]
    else:
        shapes = [(size, rows, cut), (size * out_rows, columns)]
    outs = pl.pallas_call(
        kernel,
        out_shape=[jax.ShapeDtypeStruct(shape, kind) for shape in shapes],
        in_specs=[pl.BlockSpec(memory_space=pltpu.SMEM)]
        + [pl.BlockSpec(memory_space=pltpu.HBM)] * len(where),
        out_specs=[VMEM] * len(shapes),
        scratch_shapes=[
            pltpu.VMEM(full if cut else (8, 16, 128), kind),
            pltpu.SemaphoreType.DMA((len(where),)),
        ],
        compiler_params=pltpu.CompilerParams(vmem_limit_bytes=24 * 2**20),
        cost_estimate=pl.CostEstimate(flops=0, bytes_accessed=1, transcendentals=0),
        name="assemble",
    )(place, *[array for _, _, array, _ in blocks])
    outs = list(outs)
    if cut and out_rows % 8:
        turned = outs[1].reshape(size, rows // out_rows, out_rows, columns - cut)
        outs[1] = turned.transpose(0, 2, 1, 3).reshape(size * out_rows, columns)
    return [out.reshape(-1, out.shape[-1]) for out in outs]


def pick(total, k, j):
    slow, fast = dp_split(lax.axis_size("dp"))
    rows = total.shape[0] // (slow * fast)
    index = lax.axis_index("dp")
    start = (((index // fast) ^ k) * fast + ((index % fast) ^ j)) * rows
    return lax.dynamic_slice_in_dim(total, start, rows, 0)


def rows_first(value):
    return with_layout_constraint(value, Layout(tuple(range(value.ndim))))


def scatter_send(total, ks):
    _, fast = dp_split(lax.axis_size("dp"))
    return [
        swap(jnp.concatenate([rows_first(pick(total, k, j)) for k in ks]), "dp", j)
        for j in range(1, fast)
    ]


def scatter_lines(total, ks, received):
    lines = {}
    for n, k in enumerate(ks):
        line = pick(total, k, 0).astype(F32)
        rows = line.shape[0]
        for part in received:
            line = line + part[n * rows : (n + 1) * rows].astype(F32)
        lines[k] = rows_first(line.astype(BF16))
    return lines


def relay_ks():
    slow, _ = dp_split(lax.axis_size("dp"))
    return [1, *range(2, slow, 2)], [*range(3, slow, 2), 0]


def relay_send(lines):
    ks, _ = relay_ks()
    return high_swap(jnp.concatenate([lines[k] for k in ks]), 1)


def relay_split(received):
    ks, _ = relay_ks()
    rows = received.shape[0] // len(ks)
    return {k: received[n * rows : (n + 1) * rows] for n, k in enumerate(ks)}


def relay_last(lines, received):
    _, ks = relay_ks()
    got = relay_split(received)
    parts = [lines[0], got[1]]
    for k in ks[:-1]:
        line = lines[k].astype(F32) + got[k ^ 1].astype(F32)
        parts.append(high_swap(line.astype(BF16), k))
    return parts


def parts_sum(parts):
    return functools.reduce(jnp.add, [part.astype(F32) for part in parts])


def cores_sum(left, right, dims=NN):
    return own_sum(left, right, mates_part(left, right, dims), dims)


def mates_part(left, right, dims=NN):
    return core_swap(dot(left[left.shape[0] // 2 :], right, dims).astype(BF16))


def own_sum(left, right, mate, dims=NN):
    return dot(left[: left.shape[0] // 2], right, dims) + mate.astype(F32)


def side_send(value):
    half = value.shape[0] // 2
    return [side_swap(value[:half]), side_swap(value[half:])]


def join(parts):
    return jnp.concatenate(parts)


def with_mate(own):
    return jnp.concatenate([own, core_swap(own)])


def norm_kernel(step, *refs):
    *pieces, rows_ref, out_ref = refs
    gain, shift = rows_ref[0:1, :], rows_ref[1:2, :]
    at = 0
    for ref in pieces:
        for start in range(0, ref.shape[0], step):
            values = ref[start : start + step, :].astype(F32)
            centered = values - jnp.mean(values, axis=-1, keepdims=True)
            inverse = lax.rsqrt(jnp.mean(centered * centered, axis=-1, keepdims=True) + NORM_EPS)
            out_ref[at : at + step, :] = (centered * inverse * gain + shift).astype(BF16)
            at += step


def norm_tokens(pieces, rows, step=128):
    size, width = sum(v.shape[0] for v in pieces), pieces[0].shape[1]
    return pl.pallas_call(
        functools.partial(norm_kernel, step),
        out_shape=jax.ShapeDtypeStruct((size, width), BF16),
        in_specs=[VMEM] * (len(pieces) + 1),
        out_specs=VMEM,
        compiler_params=pltpu.CompilerParams(vmem_limit_bytes=24 * 2**20),
        cost_estimate=pl.CostEstimate(flops=0, bytes_accessed=1, transcendentals=0),
        name="norm_tokens",
    )(*pieces, rows)


def weight_grad_kernel(count, *refs):
    lefts, rights, out_ref = refs[:count], refs[count:-1], refs[-1]
    total = None
    at = 0
    for left in lefts:
        for start in range(0, left.shape[0], rights[0].shape[0]):
            right = rights[at]
            at += 1
            term = dot(left[start : start + right.shape[0], :], right[...], TN)
            total = term if total is None else total + term
    out_ref[...] = total.astype(BF16)


def weight_grad(lefts, rights, step=256):
    rows, columns = lefts[0].shape[1], rights[0].shape[1]
    return pl.pallas_call(
        functools.partial(weight_grad_kernel, len(lefts)),
        grid=(rows // step,),
        out_shape=jax.ShapeDtypeStruct((rows, columns), BF16),
        in_specs=[pl.BlockSpec((v.shape[0], step), lambda i: (0, i)) for v in lefts]
        + [pl.BlockSpec(v.shape, lambda i: (0, 0)) for v in rights],
        out_specs=pl.BlockSpec((step, columns), lambda i: (i, 0)),
        compiler_params=pltpu.CompilerParams(vmem_limit_bytes=40 * 2**20),
        cost_estimate=pl.CostEstimate(flops=0, bytes_accessed=1, transcendentals=0),
        name="weight_grad",
    )(*lefts, *rights)


def sum_all(value):
    size = lax.axis_size("dp")
    value = value + core_swap(value)
    steps = [("tensor", 2)] + [("dp", 1 << n) for n in range(size.bit_length() - 1)]
    for n in range(0, len(steps), 2):
        first = steps[n]
        if n + 1 == len(steps):
            value = value + swap(value, *first)
            continue
        second = steps[n + 1]
        if first[0] == second[0]:
            both = swap(value, first[0], first[1] | second[1])
        else:
            tensor = lax.axis_size("tensor")
            bits = first[1] | second[1] * tensor
            pairs = [(i, i ^ bits) for i in range(size * tensor)]
            both = lax.ppermute(value, ("dp", "tensor"), pairs)
        value = (value + swap(value, *first)) + (swap(value, *second) + both)
    return value


def layer_norm_parts(values, gain_row, shift_row):
    centered = values - jnp.mean(values, axis=-1, keepdims=True)
    inverse = lax.rsqrt(jnp.mean(centered * centered, axis=-1, keepdims=True) + NORM_EPS)
    normed = centered * inverse
    return (normed * gain_row + shift_row, normed, inverse)


def layer_norm_back(grad_normed, normed, inverse, gain_row):
    scaled = grad_normed * gain_row
    return inverse * (
        scaled
        - jnp.mean(scaled, axis=-1, keepdims=True)
        - normed * jnp.mean(scaled * normed, axis=-1, keepdims=True)
    )


def adam_update(master, grad_sum, moment_one, moment_two, step_rate, clip_factor):
    clipped = grad_sum * clip_factor
    one_new = BETA_FIRST * moment_one + (1.0 - BETA_FIRST) * clipped
    two_new = BETA_SECOND * moment_two + (1.0 - BETA_SECOND) * clipped * clipped
    one_hat = one_new / (1.0 - BETA_FIRST**STEP)
    two_hat = two_new / (1.0 - BETA_SECOND**STEP)
    master_new = master - step_rate * (
        one_hat / (jnp.sqrt(two_hat) + ADAM_EPS) + DECAY_RATE * master
    )
    return (master_new, one_new, two_new)


def adam_kernel(rates, counts, clip_ref, *refs):
    clip_factor = clip_ref[0, 0]
    ins, outs = refs[: -3 * len(rates)], refs[-3 * len(rates) :]
    at = 0
    for n, (rate, count) in enumerate(zip(rates, counts, strict=True)):
        master, one, two = ins[at : at + 3]
        parts = ins[at + 3 : at + 3 + count]
        at += 3 + count
        total = functools.reduce(jnp.add, [part[...].astype(F32) for part in parts])
        results = outs[3 * n : 3 * n + 3]
        if master.ndim == 2:
            for out, value in zip(
                results,
                adam_update(master[...], total, one[...], two[...], rate, clip_factor),
                strict=True,
            ):
                out[...] = value
            continue
        width = master.shape[2]
        for c in range(master.shape[0]):
            grad = total[:, c * width : (c + 1) * width]
            values = adam_update(master[c], grad, one[c], two[c], rate, clip_factor)
            for out, value in zip(results, values, strict=True):
                out[c] = value


def adam_all(clip_factor, weights):
    arrays = [v for master, one, two, parts, _ in weights for v in (master, one, two, *parts)]
    outs = pl.pallas_call(
        functools.partial(
            adam_kernel, [rate for *_, rate in weights], [len(w[3]) for w in weights]
        ),
        out_shape=[
            jax.ShapeDtypeStruct(master.shape, F32) for master, *_ in weights for _ in range(3)
        ],
        in_specs=[pl.BlockSpec(memory_space=pltpu.SMEM)] + [VMEM] * len(arrays),
        out_specs=[VMEM] * (3 * len(weights)),
        compiler_params=pltpu.CompilerParams(vmem_limit_bytes=60 * 2**20),
        name="adam_all",
    )(clip_factor.reshape(1, 1), *arrays)
    return [outs[n : n + 3] for n in range(0, len(outs), 3)]


def gelu_parts(value):
    share = 0.5 + 0.5 * lax.erf(value * 0.5**0.5)
    slope = share + value * jnp.exp(-0.5 * value * value) * (0.5 / jnp.pi) ** 0.5
    return (value * share).astype(BF16), slope.astype(BF16)


def on_device(
    tokens,
    cotangent,
    lengths,
    key_mask,
    qkv_weight,
    out_weight,
    up_weight,
    down_weight,
    norm_params,
    qkv_first,
    qkv_second,
    out_first,
    out_second,
    up_first,
    up_second,
    down_first,
    down_second,
    norm_first,
    norm_second,
):
    own, width = tokens.shape
    cell = 2 * own
    heads = qkv_weight.shape[2] // HD
    dp, tensor = lax.axis_index("dp"), lax.axis_index("tensor")
    side, core = tensor // 2, tensor % 2

    norm_rows = norm_params.shape[1]

    positions = jnp.arange(cell, dtype=jnp.int32)
    key_valid = (positions[None, :] < lengths[:, None]) & (
        (key_mask == 1) | (positions[None, :] == 0)
    )
    bias = jnp.where(key_valid, 0.0, -1e30).astype(F32)
    bias = jnp.where(side == 0, bias, bias[::-1])
    bias = jnp.where(core == 0, bias, jnp.roll(bias, own, axis=1))
    bias_near, bias_far = [jnp.broadcast_to(row, (8, cell)) for row in bias]

    slow, _ = dp_split(lax.axis_size("dp"))
    odds, evens = list(range(1, slow, 2)), list(range(2, slow, 2))
    qkv_width = 3 * heads * HD
    head = own // 4
    first_low = pack_first(qkv_weight.transpose(1, 0, 2), out_weight)
    first = {k: high_swap(first_low, k) for k in odds}
    first_own = spread(first_low)
    top = own * 3 // 4
    side_top = side_swap(tokens[:top])
    mate_tokens = core_swap(tokens)
    norm_low, mate_tokens = tie(norm_params.astype(BF16), mate_tokens)
    norm_low = gather_small(norm_low)
    up_low, down_low = up_weight.astype(BF16), down_weight.astype(BF16)
    first, first_own, side_top, tokens, up_low, down_low = tie(
        first, first_own, side_top, tokens, up_low, down_low
    )
    for k in evens:
        first[k] = high_swap(first[k ^ 1], 1)
    first_lines = {k: spread(first[k]) for k in odds}
    side_rest = side_swap(tokens[top:])
    top_mate = core_swap(side_top)
    first, first_lines, up_low, down_low, cotangent, side_rest, top_mate, norm_low = tie(
        first, first_lines, up_low, down_low, cotangent, side_rest, top_mate, norm_low
    )
    for k in evens:
        first_lines[k] = spread(first[k])
    rest_mate = core_swap(side_rest)
    up = {k: high_swap(up_low, k) for k in odds}
    norm_values = jnp.moveaxis(norm_low, 0, 1).reshape(4, width).astype(F32)
    one_near = norm_tokens([tokens, mate_tokens], norm_values[:2])
    one_far = norm_tokens([side_top, side_rest, top_mate, rest_mate], norm_values[:2])
    cot_side = side_swap(cotangent)
    first_lines, one_far, one_near, up_low = tie(first_lines, one_far, one_near, up_low)
    up_own = spread(up_low)[1:]

    qkv_full, out_full = assemble(
        sum([entries(k, line) for k, line in first_lines.items()], entries(0, first_own)),
        qkv_width,
    )
    qkv_far, ctx_far, lse_far = attend(one_far, qkv_full, bias_far, heads)
    ctx_far, up, up_own, cot_side, down_low = tie(ctx_far, up, up_own, cot_side, down_low)
    for k in evens:
        up[k] = high_swap(up[k ^ 1], 1)
    up_others = spread(jnp.stack([up[k] for k in odds] + [down_low]))[1:]
    down = {k: high_swap(down_low, k) for k in odds}
    far_sum = cores_sum(ctx_far, out_full).astype(BF16)
    far_sum, one_near, qkv_full = tie(far_sum, one_near, qkv_full)
    out_far = side_swap(far_sum)
    qkv_near, ctx_near, lse_near = attend(one_near, qkv_full, bias_near, heads)
    ctx_near, out_far, up, up_others, down, cotangent, cot_side = tie(
        ctx_near, out_far, up, up_others, down, cotangent, cot_side
    )
    for k in evens:
        down[k] = high_swap(down[k ^ 1], 1)
    up_even = [spread(up[k])[1:] for k in evens]
    out_near = cores_sum(ctx_near, out_full)
    stream_in = tokens.astype(F32)
    residual = stream_in + (out_near + out_far.astype(F32))

    ln_two, normed_two, inverse_two = layer_norm_parts(residual, norm_values[2], norm_values[3])
    ln_two = ln_two.astype(BF16)
    ln_two, up_even, down = tie(ln_two, up_even, down)
    two_mate = core_swap(ln_two)
    two_side = side_swap(ln_two)
    places = odds + evens
    down_line = jnp.stack([down[k] for k in places])
    down_others = spread(down_line)[1:]
    grad_near = with_mate(cotangent)
    grad_far = with_mate(cot_side)
    two_near = join([ln_two, two_mate])
    two_near, grad_near, grad_far = tie(two_near, grad_near, grad_far)
    (up_full,) = assemble(
        entries(0, [up_low, *up_own])
        + joined_entries(odds, [up[k] for k in odds], up_others)
        + [
            entry
            for k, line in zip(evens, up_even, strict=True)
            for entry in entries(k, [up[k], *line])
        ]
    )
    hid_near, slope_near = gelu_parts(dot(two_near, up_full))
    hid_near, down_line, down_others, two_side = tie(hid_near, down_line, down_others, two_side)
    (down_full,) = assemble(
        [(0, 0, down_low, None)]
        + [(0, j + 1, other, len(odds)) for j, other in enumerate(up_others)]
        + [
            entry
            for n, k in enumerate(places)
            for entry in [(k, 0, down_line, n)]
            + [(k, j + 1, other, n) for j, other in enumerate(down_others)]
        ]
    )
    two_far = with_mate(two_side)
    pre_near = (dot(grad_near, down_full, NT) * slope_near.astype(F32)).astype(BF16)
    two_far, pre_near = tie(two_far, pre_near)
    hid_far, slope_far = gelu_parts(dot(two_far, up_full))
    pre_far = (dot(grad_far, down_full, NT) * slope_far.astype(F32)).astype(BF16)
    far_sum = cores_sum(pre_far, up_full, NT).astype(BF16)
    far_sum, pre_near, pre_far, hid_near, hid_far = tie(
        far_sum, pre_near, pre_far, hid_near, hid_far
    )
    back_far = side_swap(far_sum)
    back_near = cores_sum(pre_near, up_full, NT)
    back_near, hid_near, hid_far, grad_near, grad_far = tie(
        back_near, hid_near, hid_far, grad_near, grad_far
    )
    heavy, light = relay_ks()
    order = heavy + light
    grad_down = dot(join([hid_near, hid_far]), join([grad_near, grad_far]), TN).astype(BF16)
    grad_down, hid_near, hid_far = tie(grad_down, hid_near, hid_far)
    down_received = [scatter_send(grad_down, heavy)]
    last_terms = [dot(v[own:], down_full).astype(BF16) for v in (hid_far, hid_near)]
    last_terms, pre_near, pre_far = tie(last_terms, pre_near, pre_far)
    grad_up = weight_grad([two_near, two_far], [pre_near, pre_far])
    last_terms, grad_down, back_far, grad_up, down_received = tie(
        last_terms, grad_down, back_far, grad_up, down_received
    )
    grad_ln_two = back_near + back_far.astype(F32)
    grad_residual = cotangent.astype(F32) + layer_norm_back(
        grad_ln_two, normed_two, inverse_two, norm_values[2]
    )
    gain_two = jnp.sum(grad_ln_two * normed_two, axis=0)
    shift_two = jnp.sum(grad_ln_two, axis=0)

    res_low = grad_residual.astype(BF16)
    res_side = side_swap(res_low)
    res_mate = core_swap(res_low)
    last_mates = [core_swap(v) for v in last_terms]
    down_lines = scatter_lines(grad_down, heavy, down_received[0])
    res_mate, last_mates, down_lines = tie(res_mate, last_mates, down_lines)
    down_got = relay_send(down_lines)
    down_received.append(scatter_send(grad_down, light))
    up_received = [scatter_send(grad_up, heavy)]
    dqkv_near = attend_back(
        qkv_near, bias_near, ctx_near, lse_near, res_low, res_mate, out_full, heads
    )
    (
        dqkv_near, res_side, up_received, grad_up, down_got, down_received, grad_down,
        last_mates, hid_far,
    ) = tie(
        dqkv_near, res_side, up_received, grad_up, down_got, down_received, grad_down,
        last_mates, hid_far,
    )
    res_side_mate = core_swap(res_side)
    down_lines.update(scatter_lines(grad_down, light, down_received[1]))
    up_lines = scatter_lines(grad_up, heavy, up_received[0])
    last_far = own_sum(hid_far, down_full, last_mates[0]).astype(BF16)
    grad_out = dot(
        join([ctx_near, ctx_far]), join([res_low, res_mate, res_side, res_side_mate]), TN
    ).astype(BF16)
    res_side_mate, grad_out, down_lines, up_lines, last_far = tie(
        res_side_mate, grad_out, down_lines, up_lines, last_far
    )
    up_received.append(scatter_send(grad_up, light))
    out_received = scatter_send(grad_out, order)
    down_parts = relay_last(down_lines, down_got)
    up_got = relay_send(up_lines)
    last_side = side_swap(last_far)
    dqkv_far = attend_back(
        qkv_far, bias_far, ctx_far, lse_far, res_side, res_side_mate, out_full, heads
    )
    dqkv_far, up_got, up_received, grad_up, down_parts, grad_out, out_received, last_side = tie(
        dqkv_far, up_got, up_received, grad_up, down_parts, grad_out, out_received, last_side
    )

    up_lines.update(scatter_lines(grad_up, light, up_received[1]))
    out_lines = scatter_lines(grad_out, order, out_received)
    dqkv_far, dqkv_near, up_lines, out_lines = tie(dqkv_far, dqkv_near, up_lines, out_lines)
    up_parts = relay_last(up_lines, up_got)
    out_got = relay_send(out_lines)
    grad_qkv = dot(join([one_near, one_far]), join([dqkv_near, dqkv_far]), TN).astype(BF16)
    grad_qkv, dqkv_far, dqkv_near = tie(rows_first(grad_qkv), dqkv_far, dqkv_near)
    received = [scatter_send(grad_qkv, heavy)]
    first_mates = [mates_part(v, qkv_full, NT) for v in (dqkv_far, dqkv_near)]
    far_sum = own_sum(dqkv_far, qkv_full, first_mates[0], NT).astype(BF16)
    far_sum, first_mates, grad_qkv, dqkv_near, hid_near = tie(
        far_sum, first_mates, grad_qkv, dqkv_near, hid_near
    )
    first_far = side_swap(far_sum)
    received.append(scatter_send(grad_qkv, light))
    first_near = own_sum(dqkv_near, qkv_full, first_mates[1], NT)
    first_near, received[0], grad_qkv, hid_near = tie(first_near, received[0], grad_qkv, hid_near)
    qkv_lines = scatter_lines(grad_qkv, heavy, received[0])
    qkv_got = relay_send(qkv_lines)
    last_near = own_sum(hid_near, down_full, last_mates[1])
    layer_out = (residual + (last_near + last_side.astype(F32))).astype(BF16)
    (
        received[1], qkv_got, qkv_lines, out_got, out_lines, layer_out, up_parts, down_parts,
        grad_qkv,
    ) = tie(
        received[1], qkv_got, qkv_lines, out_got, out_lines, layer_out, up_parts, down_parts,
        grad_qkv,
    )
    qkv_lines.update(scatter_lines(grad_qkv, light, received[1]))
    qkv_parts = relay_last(qkv_lines, qkv_got)
    out_parts = relay_last(out_lines, out_got)
    summed_up, summed_down = parts_sum(up_parts), parts_sum(down_parts)
    early_squares = jnp.sum(summed_up * summed_up) + jnp.sum(summed_down * summed_down)

    _, normed_one, inverse_one = layer_norm_parts(stream_in, norm_values[0], norm_values[1])
    grad_ln_one = first_near + first_far.astype(F32)
    input_grad = (
        grad_residual + layer_norm_back(grad_ln_one, normed_one, inverse_one, norm_values[0])
    ).astype(BF16)
    gain_one = jnp.sum(grad_ln_one * normed_one, axis=0)
    shift_one = jnp.sum(grad_ln_one, axis=0)
    rows = jnp.stack([gain_one, shift_one, gain_two, shift_two])
    qkv_parts, out_parts, rows, input_grad, early_squares = tie(
        qkv_parts, out_parts, rows, input_grad, early_squares
    )
    summed_qkv, summed_out = parts_sum(qkv_parts), parts_sum(out_parts)
    early_squares = early_squares + jnp.sum(summed_out * summed_out)

    local_squares = early_squares + jnp.sum(summed_qkv * summed_qkv)
    packed = jnp.concatenate([rows, jnp.full((4, 128), local_squares, F32)], axis=1)
    packed = sum_all(packed)
    norm_grad = packed[:, :width]
    squares_total = packed[0, width] + jnp.sum(norm_grad * norm_grad)
    summed_norm = lax.dynamic_slice_in_dim(norm_grad, dp * norm_rows, norm_rows, 1)
    grad_norm = jnp.sqrt(squares_total)
    clip_factor = jnp.minimum(1.0, CLIP_LIMIT / grad_norm)

    qkv_results, out_results, up_results, down_results = adam_all(
        clip_factor,
        [
            (*[v.transpose(1, 0, 2) for v in (qkv_weight, qkv_first, qkv_second)], qkv_parts, RATE_QKV),
            (out_weight, out_first, out_second, out_parts, RATE_OUT),
            (up_weight, up_first, up_second, up_parts, RATE_UP),
            (down_weight, down_first, down_second, down_parts, RATE_DOWN),
        ],
    )
    qkv_new, qkv_one, qkv_two = [v.transpose(1, 0, 2) for v in qkv_results]
    out_new, out_one, out_two = out_results
    up_new, up_one, up_two = up_results
    down_new, down_one, down_two = down_results
    norm_new, norm_one, norm_two = adam_update(
        norm_params, summed_norm, norm_first, norm_second, RATE_NORM, clip_factor
    )
    shift_grad = clip_factor * summed_norm[3]
    return (
        layer_out,
        input_grad,
        grad_norm,
        qkv_new,
        qkv_one,
        qkv_two,
        out_new,
        out_one,
        out_two,
        up_new,
        up_one,
        up_two,
        down_new,
        down_one,
        down_two,
        norm_new,
        norm_one,
        norm_two,
        shift_grad,
    )


def solution(mesh):
    tokens = P(("dp", "tensor"), None)
    columns = P("dp", None, "tensor")
    rows = P(("tensor", "dp"), None)
    both = P("dp", "tensor")
    norms = P(None, "dp")
    return jax.shard_map(
        on_device,
        mesh=mesh,
        in_specs=(tokens, tokens, P("dp"), P("dp", None), columns, rows, both, rows, norms)
        + (columns,) * 2
        + (rows,) * 2
        + (both,) * 2
        + (rows,) * 2
        + (norms,) * 2,
        out_specs=(tokens, tokens, P())
        + (columns,) * 3
        + (rows,) * 3
        + (both,) * 3
        + (rows,) * 3
        + (norms,) * 3
        + (P("dp"),),
        check_vma=False,
    )
```

```python
import functools

import jax
import jax.numpy as jnp
from jax import lax
from jax.experimental import pallas as pl
from jax.experimental.layout import Layout, with_layout_constraint
from jax.experimental.pallas import tpu as pltpu
from jax.sharding import PartitionSpec as P

HD = 64
STEP = 5

NORM_EPS = 1e-05
CLIP_LIMIT = 1.0
BETA_FIRST = 0.5
BETA_SECOND = 0.5
ADAM_EPS = 1e-08
DECAY_RATE = 0.01
RATE_QKV = 0.03
RATE_OUT = 0.5
RATE_UP = 0.03
RATE_DOWN = 0.015
RATE_NORM = 0.2

F32 = jnp.float32
BF16 = jnp.bfloat16
NN = (((1,), (0,)), ((), ()))
NT = (((1,), (1,)), ((), ()))
TN = (((0,), (0,)), ((), ()))
VMEM = pl.BlockSpec(memory_space=pltpu.VMEM)


def dot(left, right, dims=NN):
    return lax.dot_general(left, right, dims, preferred_element_type=F32)


def widen(block, columns, lane):
    rows = block.shape[0]
    wide = jnp.concatenate([block.astype(F32), jnp.zeros((rows, HD), F32)], axis=1)
    for n, column in enumerate(columns):
        wide = jnp.where(lane == HD + n, column, wide)
    return wide.astype(BF16)


def minus_parts(column):
    high = column.astype(BF16).astype(F32)
    rest = column - high
    middle = rest.astype(BF16).astype(F32)
    return [-high, -middle, middle - rest]


def attend_kernel(heads, step, one_ref, weight_ref, bias_ref, qkv_ref, ctx_ref, lse_ref, keys):
    tokens = qkv_ref.shape[0]
    width = heads * HD
    lane = lax.broadcasted_iota(jnp.int32, (1, 2 * HD), 1)

    def project(n, _):
        rows = pl.ds(pl.multiple_of(n * step, step), step)
        qkv_ref[rows, :] = dot(one_ref[rows, :], weight_ref[...]).astype(BF16)
        return 0

    lax.fori_loop(0, tokens // step, project, 0)
    bias = bias_ref[...].T[:, 0:1]
    for h in range(heads):
        keys[h] = widen(qkv_ref[:, width + h * HD : width + (h + 1) * HD], [bias], lane)

    def block(n, _):
        rows = pl.ds(pl.multiple_of(n * step, step), step)
        outs = []
        stat = jnp.zeros((step, 2 * HD), F32)
        for h in range(heads):
            query = qkv_ref[rows, h * HD : (h + 1) * HD].astype(F32) * HD ** (-0.5)
            scores = dot(widen(query, [jnp.ones((step, 1), F32)], lane), keys[h], NT)
            top = jnp.max(scores, axis=1, keepdims=True)
            weights = jnp.exp(scores - top)
            total = jnp.sum(weights, axis=1, keepdims=True)
            values = qkv_ref[:, 2 * width + h * HD : 2 * width + (h + 1) * HD]
            outs.append((dot(weights.astype(BF16), values) / total).astype(BF16))
            stat = jnp.where(lane == h, top + jnp.log(total), stat)
        ctx_ref[rows, :] = jnp.concatenate(outs, axis=1)
        lse_ref[rows, :] = stat
        return 0

    lax.fori_loop(0, tokens // step, block, 0)


def attend(one, weight, bias, heads, step=1024):
    tokens = one.shape[0]
    return pl.pallas_call(
        functools.partial(attend_kernel, heads, step),
        out_shape=(
            jax.ShapeDtypeStruct((tokens, 3 * heads * HD), BF16),
            jax.ShapeDtypeStruct((tokens, heads * HD), BF16),
            jax.ShapeDtypeStruct((tokens, 2 * HD), F32),
        ),
        in_specs=[VMEM] * 3,
        out_specs=[VMEM] * 3,
        scratch_shapes=[pltpu.VMEM((heads, tokens, 2 * HD), BF16)],
        compiler_params=pltpu.CompilerParams(vmem_limit_bytes=48 * 2**20),
        cost_estimate=pl.CostEstimate(flops=0, bytes_accessed=1, transcendentals=0),
        name="attend",
    )(one, weight, bias)


def attend_back_kernel(
    heads,
    step,
    qkv_ref,
    bias_ref,
    ctx_ref,
    lse_ref,
    own_ref,
    mate_ref,
    weight_ref,
    out_ref,
    keys,
    values,
    dk,
    dv,
    grad_ref,
):
    tokens = qkv_ref.shape[0]
    width = heads * HD
    scale = HD ** (-0.5)
    lane = lax.broadcasted_iota(jnp.int32, (1, 2 * HD), 1)
    one = jnp.ones((tokens, 1), F32)
    bias = bias_ref[...].T[:, 0:1]
    half = tokens // 2
    for n, ref in enumerate((own_ref, mate_ref)):
        grad_ref[n * half : (n + 1) * half, :] = dot(ref[...], weight_ref[...], NT).astype(BF16)
    for h in range(heads):
        key = qkv_ref[:, width + h * HD : width + (h + 1) * HD]
        value = qkv_ref[:, 2 * width + h * HD : 2 * width + (h + 1) * HD]
        keys[h] = widen(key, [bias, one, one, one], lane)
        values[h] = widen(value, [one, one, one], lane)
    dk[...] = jnp.zeros_like(dk)
    dv[...] = jnp.zeros_like(dv)

    def block(n, _):
        rows = pl.ds(pl.multiple_of(n * step, step), step)
        outs = []
        ones = jnp.ones((step, 1), F32)
        for h in range(heads):
            cols = slice(h * HD, (h + 1) * HD)
            query = qkv_ref[rows, cols].astype(F32) * scale
            grad = grad_ref[rows, cols].astype(F32)
            delta = jnp.sum(grad * ctx_ref[rows, cols].astype(F32), axis=1, keepdims=True)
            lse = lse_ref[rows, h : h + 1]
            weights = jnp.exp(dot(widen(query, [ones] + minus_parts(lse), lane), keys[h], NT))
            slopes = dot(widen(grad, minus_parts(delta), lane), values[h], NT)
            slopes = (weights * slopes).astype(BF16)
            weights = weights.astype(BF16)
            key = qkv_ref[:, width + h * HD : width + (h + 1) * HD]
            outs.append((dot(slopes, key) * scale).astype(BF16))
            dk[h] += dot(query.T.astype(BF16), slopes)
            dv[h] += dot(grad.T.astype(BF16), weights)
        out_ref[rows, :width] = jnp.concatenate(outs, axis=1)
        return 0

    lax.fori_loop(0, tokens // step, block, 0)
    for place, total in ((1, dk), (2, dv)):
        turned = jnp.concatenate([total[h].T for h in range(heads)], axis=1)
        out_ref[:, place * width : (place + 1) * width] = turned.astype(BF16)


def attend_back(qkv, bias, ctx, lse, own, mate, weight, heads, step=1024):
    tokens = qkv.shape[0]
    return pl.pallas_call(
        functools.partial(attend_back_kernel, heads, step),
        out_shape=jax.ShapeDtypeStruct((tokens, 3 * heads * HD), BF16),
        in_specs=[VMEM] * 7,
        out_specs=VMEM,
        scratch_shapes=[pltpu.VMEM((heads, tokens, 2 * HD), BF16)] * 2
        + [pltpu.VMEM((heads, HD, tokens), F32)] * 2
        + [pltpu.VMEM((tokens, heads * HD), BF16)],
        compiler_params=pltpu.CompilerParams(vmem_limit_bytes=48 * 2**20),
        cost_estimate=pl.CostEstimate(flops=0, bytes_accessed=1, transcendentals=0),
        name="attend_back",
    )(qkv, bias, ctx, lse, own, mate, weight)


def swap(value, axis, bits):
    size = lax.axis_size(axis)
    return lax.ppermute(value, axis, [(i, i ^ bits) for i in range(size)])


def core_swap(value):
    return swap(value, "tensor", 1)


def side_swap(value):
    return swap(value, "tensor", 2)


def tie(*values):
    return lax.optimization_barrier(values)


def dp_split(size):
    fast = 2 if size < 16 else 4
    return size // fast, fast


def high_swap(value, k):
    return swap(value, "dp", k * dp_split(lax.axis_size("dp"))[1])


def gather_small(shard):
    size = lax.axis_size("dp")
    blocks = shard[None]
    bits = 1
    while bits < size:
        blocks = jnp.concatenate([blocks, swap(blocks, "dp", bits)])
        bits *= 2
    index = lax.axis_index("dp")
    return jnp.stack([blocks[index ^ n] for n in range(size)])


def spread(block):
    _, fast = dp_split(lax.axis_size("dp"))
    return [block] + [swap(block, "dp", j) for j in range(1, fast)]


def entries(k, line, at=None):
    return [(k, j, block, at if j else None) for j, block in enumerate(line)]


def joined_entries(ks, blocks, others):
    return [
        entry
        for n, (k, block) in enumerate(zip(ks, blocks, strict=True))
        for entry in entries(k, [block, *others], n)
    ]


def pack_kernel(qkv_ref, out_ref, packed_ref):
    rows, width = out_ref.shape
    step = width * rows // qkv_ref.shape[1]
    parts = [qkv_ref[n] for n in range(qkv_ref.shape[0])]
    turned = [out_ref[:, n : n + step] for n in range(0, width, step)]
    packed = jnp.concatenate([*parts, jnp.concatenate(turned, axis=0)], axis=1)
    packed_ref[...] = packed.astype(BF16)


def pack_first(qkv, out):
    rows = qkv.shape[1]
    shape = (rows, qkv.shape[0] * qkv.shape[2] + out.size // rows)
    if out.shape[0] % 8:
        step = out.shape[1] * out.shape[0] // rows
        turned = jnp.concatenate([out[:, n : n + step] for n in range(0, out.shape[1], step)])
        return jnp.concatenate([*qkv, turned], axis=1).astype(BF16)
    return pl.pallas_call(
        pack_kernel,
        out_shape=jax.ShapeDtypeStruct(shape, BF16),
        in_specs=[VMEM] * 2,
        out_specs=VMEM,
        compiler_params=pltpu.CompilerParams(vmem_limit_bytes=16 * 2**20),
        cost_estimate=pl.CostEstimate(flops=0, bytes_accessed=1, transcendentals=0),
        name="pack_first",
    )(qkv, out)


def assemble(blocks, cut=None):
    slow, fast = dp_split(lax.axis_size("dp"))
    rows, columns = blocks[0][2].shape[-2:]
    kind = blocks[0][2].dtype
    index = lax.axis_index("dp")
    place = jnp.stack([index // fast, index % fast]).astype(jnp.int32)
    where = [(k, j, at) for k, j, _, at in blocks]
    out_rows = rows * (columns - cut) // columns if cut else 0

    def kernel(place_ref, *refs):
        ins, outs = refs[: len(where)], refs[len(where) : -2]
        whole, sems = refs[-2:] if cut else (outs[0], refs[-1])
        copies = []
        for n, (source, (k, j, at)) in enumerate(zip(ins, where, strict=True)):
            target = (place_ref[0] ^ k) * fast + (place_ref[1] ^ j)
            source = source if at is None else source.at[at]
            copies.append(pltpu.make_async_copy(source, whole.at[target], sems.at[n]))
        for copy in copies:
            copy.start()
        for copy in copies:
            copy.wait()
        if cut:
            outs[0][...] = whole[:, :, :cut]
            if out_rows % 8:
                outs[1][...] = whole[:, :, cut:]
            else:
                turned = []
                for n in range(slow * fast):
                    block = whole[n, :, cut:].astype(F32)
                    parts = [block[m : m + out_rows] for m in range(0, rows, out_rows)]
                    turned.append(jnp.concatenate(parts, axis=1))
                outs[1][...] = jnp.concatenate(turned, axis=0).astype(kind)

    size = slow * fast
    full = (size, rows, columns)
    if not cut:
        shapes = [full]
    elif out_rows % 8:
        shapes = [(size, rows, cut), (size, rows, columns - cut)]
    else:
        shapes = [(size, rows, cut), (size * out_rows, columns)]
    outs = pl.pallas_call(
        kernel,
        out_shape=[jax.ShapeDtypeStruct(shape, kind) for shape in shapes],
        in_specs=[pl.BlockSpec(memory_space=pltpu.SMEM)]
        + [pl.BlockSpec(memory_space=pltpu.HBM)] * len(where),
        out_specs=[VMEM] * len(shapes),
        scratch_shapes=[
            pltpu.VMEM(full if cut else (8, 16, 128), kind),
            pltpu.SemaphoreType.DMA((len(where),)),
        ],
        compiler_params=pltpu.CompilerParams(vmem_limit_bytes=24 * 2**20),
        cost_estimate=pl.CostEstimate(flops=0, bytes_accessed=1, transcendentals=0),
        name="assemble",
    )(place, *[array for _, _, array, _ in blocks])
    outs = list(outs)
    if cut and out_rows % 8:
        turned = outs[1].reshape(size, rows // out_rows, out_rows, columns - cut)
        outs[1] = turned.transpose(0, 2, 1, 3).reshape(size * out_rows, columns)
    return [out.reshape(-1, out.shape[-1]) for out in outs]


def pick(total, k, j):
    slow, fast = dp_split(lax.axis_size("dp"))
    rows = total.shape[0] // (slow * fast)
    index = lax.axis_index("dp")
    start = (((index // fast) ^ k) * fast + ((index % fast) ^ j)) * rows
    return lax.dynamic_slice_in_dim(total, start, rows, 0)


def rows_first(value):
    return with_layout_constraint(value, Layout(tuple(range(value.ndim))))


def scatter_send(total, ks):
    _, fast = dp_split(lax.axis_size("dp"))
    return [
        swap(jnp.concatenate([rows_first(pick(total, k, j)) for k in ks]), "dp", j)
        for j in range(1, fast)
    ]


def scatter_lines(total, ks, received):
    lines = {}
    for n, k in enumerate(ks):
        line = pick(total, k, 0).astype(F32)
        rows = line.shape[0]
        for part in received:
            line = line + part[n * rows : (n + 1) * rows].astype(F32)
        lines[k] = rows_first(line.astype(BF16))
    return lines


def relay_ks():
    slow, _ = dp_split(lax.axis_size("dp"))
    return [1, *range(2, slow, 2)], [*range(3, slow, 2), 0]


def relay_send(lines):
    ks, _ = relay_ks()
    return high_swap(jnp.concatenate([lines[k] for k in ks]), 1)


def relay_split(received):
    ks, _ = relay_ks()
    rows = received.shape[0] // len(ks)
    return {k: received[n * rows : (n + 1) * rows] for n, k in enumerate(ks)}


def relay_last(lines, received):
    _, ks = relay_ks()
    got = relay_split(received)
    parts = [lines[0], got[1]]
    for k in ks[:-1]:
        line = lines[k].astype(F32) + got[k ^ 1].astype(F32)
        parts.append(high_swap(line.astype(BF16), k))
    return parts


def parts_sum(parts):
    return functools.reduce(jnp.add, [part.astype(F32) for part in parts])


def cores_sum(left, right, dims=NN):
    return own_sum(left, right, mates_part(left, right, dims), dims)


def mates_part(left, right, dims=NN):
    return core_swap(dot(left[left.shape[0] // 2 :], right, dims).astype(BF16))


def own_sum(left, right, mate, dims=NN):
    return dot(left[: left.shape[0] // 2], right, dims) + mate.astype(F32)


def side_send(value):
    half = value.shape[0] // 2
    return [side_swap(value[:half]), side_swap(value[half:])]


def join(parts):
    return jnp.concatenate(parts)


def with_mate(own):
    return jnp.concatenate([own, core_swap(own)])


def norm_kernel(step, *refs):
    *pieces, rows_ref, out_ref = refs
    gain, shift = rows_ref[0:1, :], rows_ref[1:2, :]
    at = 0
    for ref in pieces:
        for start in range(0, ref.shape[0], step):
            values = ref[start : start + step, :].astype(F32)
            centered = values - jnp.mean(values, axis=-1, keepdims=True)
            inverse = lax.rsqrt(jnp.mean(centered * centered, axis=-1, keepdims=True) + NORM_EPS)
            out_ref[at : at + step, :] = (centered * inverse * gain + shift).astype(BF16)
            at += step


def norm_tokens(pieces, rows, step=128):
    size, width = sum(v.shape[0] for v in pieces), pieces[0].shape[1]
    return pl.pallas_call(
        functools.partial(norm_kernel, step),
        out_shape=jax.ShapeDtypeStruct((size, width), BF16),
        in_specs=[VMEM] * (len(pieces) + 1),
        out_specs=VMEM,
        compiler_params=pltpu.CompilerParams(vmem_limit_bytes=24 * 2**20),
        cost_estimate=pl.CostEstimate(flops=0, bytes_accessed=1, transcendentals=0),
        name="norm_tokens",
    )(*pieces, rows)


def weight_grad_kernel(count, *refs):
    lefts, rights, out_ref = refs[:count], refs[count:-1], refs[-1]
    total = None
    at = 0
    for left in lefts:
        for start in range(0, left.shape[0], rights[0].shape[0]):
            right = rights[at]
            at += 1
            term = dot(left[start : start + right.shape[0], :], right[...], TN)
            total = term if total is None else total + term
    out_ref[...] = total.astype(BF16)


def weight_grad(lefts, rights, step=256):
    rows, columns = lefts[0].shape[1], rights[0].shape[1]
    return pl.pallas_call(
        functools.partial(weight_grad_kernel, len(lefts)),
        grid=(rows // step,),
        out_shape=jax.ShapeDtypeStruct((rows, columns), BF16),
        in_specs=[pl.BlockSpec((v.shape[0], step), lambda i: (0, i)) for v in lefts]
        + [pl.BlockSpec(v.shape, lambda i: (0, 0)) for v in rights],
        out_specs=pl.BlockSpec((step, columns), lambda i: (i, 0)),
        compiler_params=pltpu.CompilerParams(vmem_limit_bytes=40 * 2**20),
        cost_estimate=pl.CostEstimate(flops=0, bytes_accessed=1, transcendentals=0),
        name="weight_grad",
    )(*lefts, *rights)


def sum_all(value):
    size = lax.axis_size("dp")
    value = value + core_swap(value)
    steps = [("tensor", 2)] + [("dp", 1 << n) for n in range(size.bit_length() - 1)]
    for n in range(0, len(steps), 2):
        first = steps[n]
        if n + 1 == len(steps):
            value = value + swap(value, *first)
            continue
        second = steps[n + 1]
        if first[0] == second[0]:
            both = swap(value, first[0], first[1] | second[1])
        else:
            tensor = lax.axis_size("tensor")
            bits = first[1] | second[1] * tensor
            pairs = [(i, i ^ bits) for i in range(size * tensor)]
            both = lax.ppermute(value, ("dp", "tensor"), pairs)
        value = (value + swap(value, *first)) + (swap(value, *second) + both)
    return value


def layer_norm_parts(values, gain_row, shift_row):
    centered = values - jnp.mean(values, axis=-1, keepdims=True)
    inverse = lax.rsqrt(jnp.mean(centered * centered, axis=-1, keepdims=True) + NORM_EPS)
    normed = centered * inverse
    return (normed * gain_row + shift_row, normed, inverse)


def layer_norm_back(grad_normed, normed, inverse, gain_row):
    scaled = grad_normed * gain_row
    return inverse * (
        scaled
        - jnp.mean(scaled, axis=-1, keepdims=True)
        - normed * jnp.mean(scaled * normed, axis=-1, keepdims=True)
    )


def adam_update(master, grad_sum, moment_one, moment_two, step_rate, clip_factor):
    clipped = grad_sum * clip_factor
    one_new = BETA_FIRST * moment_one + (1.0 - BETA_FIRST) * clipped
    two_new = BETA_SECOND * moment_two + (1.0 - BETA_SECOND) * clipped * clipped
    one_hat = one_new / (1.0 - BETA_FIRST**STEP)
    two_hat = two_new / (1.0 - BETA_SECOND**STEP)
    master_new = master - step_rate * (
        one_hat / (jnp.sqrt(two_hat) + ADAM_EPS) + DECAY_RATE * master
    )
    return (master_new, one_new, two_new)


def squares_kernel(counts, rows_ref, early_ref, *refs):
    *parts, out_ref = refs
    width = rows_ref.shape[1]
    total = early_ref[...]
    for count in counts:
        value = functools.reduce(jnp.add, [part[...].astype(F32) for part in parts[:count]])
        parts = parts[count:]
        total += jnp.sum(jnp.sum(value * value, axis=0, keepdims=True), axis=1, keepdims=True)
    out_ref[:, :width] = rows_ref[...]
    out_ref[:, width:] = jnp.broadcast_to(total, (out_ref.shape[0], 128))


def squares_packed(rows, early, gradients):
    return pl.pallas_call(
        functools.partial(squares_kernel, [len(parts) for parts in gradients]),
        out_shape=jax.ShapeDtypeStruct((rows.shape[0], rows.shape[1] + 128), F32),
        in_specs=[VMEM] * (2 + sum(len(parts) for parts in gradients)),
        out_specs=VMEM,
        compiler_params=pltpu.CompilerParams(vmem_limit_bytes=24 * 2**20),
        cost_estimate=pl.CostEstimate(flops=0, bytes_accessed=1, transcendentals=0),
        name="squares_packed",
    )(rows, early.reshape(1, 1), *[part for parts in gradients for part in parts])


def adam_kernel(rates, counts, packed_ref, *refs):
    *refs, norm_ref, shift_ref = refs
    width = packed_ref.shape[1] - 128
    rows = packed_ref[:, :width]
    squares = jnp.sum(jnp.sum(rows * rows, axis=0, keepdims=True), axis=1, keepdims=True)
    grad_norm = jnp.sqrt(packed_ref[0:1, width : width + 1] + squares)
    clip_factor = jnp.minimum(1.0, CLIP_LIMIT / grad_norm)
    norm_ref[...] = grad_norm
    ins, outs = refs[: -3 * len(rates)], refs[-3 * len(rates) :]
    at = 0
    for n, (rate, count) in enumerate(zip(rates, counts, strict=True)):
        master, one, two = ins[at : at + 3]
        parts = ins[at + 3 : at + 3 + count]
        at += 3 + count
        total = functools.reduce(jnp.add, [part[...].astype(F32) for part in parts])
        results = outs[3 * n : 3 * n + 3]
        if n == len(rates) - 1:
            shift_ref[...] = clip_factor * total[3:4, :]
        if master.ndim == 2:
            for out, value in zip(
                results,
                adam_update(master[...], total, one[...], two[...], rate, clip_factor),
                strict=True,
            ):
                out[...] = value
            continue
        width = master.shape[2]
        for c in range(master.shape[0]):
            grad = total[:, c * width : (c + 1) * width]
            values = adam_update(master[c], grad, one[c], two[c], rate, clip_factor)
            for out, value in zip(results, values, strict=True):
                out[c] = value


def adam_all(packed, weights):
    arrays = [v for master, one, two, parts, _ in weights for v in (master, one, two, *parts)]
    shapes = [master.shape for master, *_ in weights for _ in range(3)]
    shapes += [(1, 1), (1, weights[-1][0].shape[1])]
    outs = pl.pallas_call(
        functools.partial(
            adam_kernel, [rate for *_, rate in weights], [len(w[3]) for w in weights]
        ),
        out_shape=[jax.ShapeDtypeStruct(shape, F32) for shape in shapes],
        in_specs=[VMEM] * (len(arrays) + 1),
        out_specs=[VMEM] * len(shapes),
        compiler_params=pltpu.CompilerParams(vmem_limit_bytes=60 * 2**20),
        name="adam_all",
    )(packed, *arrays)
    return outs[-2], outs[-1], [outs[n : n + 3] for n in range(0, len(outs) - 2, 3)]


def gelu_parts(value):
    share = 0.5 + 0.5 * lax.erf(value * 0.5**0.5)
    slope = share + value * jnp.exp(-0.5 * value * value) * (0.5 / jnp.pi) ** 0.5
    return (value * share).astype(BF16), slope.astype(BF16)


def on_device(
    tokens,
    cotangent,
    lengths,
    key_mask,
    qkv_weight,
    out_weight,
    up_weight,
    down_weight,
    norm_params,
    qkv_first,
    qkv_second,
    out_first,
    out_second,
    up_first,
    up_second,
    down_first,
    down_second,
    norm_first,
    norm_second,
):
    own, width = tokens.shape
    cell = 2 * own
    heads = qkv_weight.shape[2] // HD
    dp, tensor = lax.axis_index("dp"), lax.axis_index("tensor")
    side, core = tensor // 2, tensor % 2

    norm_rows = norm_params.shape[1]

    positions = jnp.arange(cell, dtype=jnp.int32)
    key_valid = (positions[None, :] < lengths[:, None]) & (
        (key_mask == 1) | (positions[None, :] == 0)
    )
    bias = jnp.where(key_valid, 0.0, -1e30).astype(F32)
    bias = jnp.where(side == 0, bias, bias[::-1])
    bias = jnp.where(core == 0, bias, jnp.roll(bias, own, axis=1))
    bias_near, bias_far = [jnp.broadcast_to(row, (8, cell)) for row in bias]

    slow, _ = dp_split(lax.axis_size("dp"))
    odds, evens = list(range(1, slow, 2)), list(range(2, slow, 2))
    qkv_width = 3 * heads * HD
    head = own // 4
    first_low = pack_first(qkv_weight.transpose(1, 0, 2), out_weight)
    first = {k: high_swap(first_low, k) for k in odds}
    first_own = spread(first_low)
    top = own * 3 // 4
    side_top = side_swap(tokens[:top])
    mate_tokens = core_swap(tokens)
    norm_low, mate_tokens = tie(norm_params.astype(BF16), mate_tokens)
    norm_low = gather_small(norm_low)
    up_low, down_low = up_weight.astype(BF16), down_weight.astype(BF16)
    first, first_own, side_top, tokens, up_low, down_low = tie(
        first, first_own, side_top, tokens, up_low, down_low
    )
    for k in evens:
        first[k] = high_swap(first[k ^ 1], 1)
    first_lines = {k: spread(first[k]) for k in odds}
    side_rest = side_swap(tokens[top:])
    top_mate = core_swap(side_top)
    first, first_lines, up_low, down_low, cotangent, side_rest, top_mate, norm_low = tie(
        first, first_lines, up_low, down_low, cotangent, side_rest, top_mate, norm_low
    )
    for k in evens:
        first_lines[k] = spread(first[k])
    rest_mate = core_swap(side_rest)
    up = {k: high_swap(up_low, k) for k in odds}
    norm_values = jnp.moveaxis(norm_low, 0, 1).reshape(4, width).astype(F32)
    one_near = norm_tokens([tokens, mate_tokens], norm_values[:2])
    one_far = norm_tokens([side_top, side_rest, top_mate, rest_mate], norm_values[:2])
    cot_side = side_swap(cotangent)
    first_lines, one_far, one_near, up_low = tie(first_lines, one_far, one_near, up_low)
    up_own = spread(up_low)[1:]

    qkv_full, out_full = assemble(
        sum([entries(k, line) for k, line in first_lines.items()], entries(0, first_own)),
        qkv_width,
    )
    qkv_far, ctx_far, lse_far = attend(one_far, qkv_full, bias_far, heads)
    ctx_far, up, up_own, cot_side, down_low = tie(ctx_far, up, up_own, cot_side, down_low)
    for k in evens:
        up[k] = high_swap(up[k ^ 1], 1)
    up_others = spread(jnp.stack([up[k] for k in odds] + [down_low]))[1:]
    down = {k: high_swap(down_low, k) for k in odds}
    far_sum = cores_sum(ctx_far, out_full).astype(BF16)
    far_sum, one_near, qkv_full = tie(far_sum, one_near, qkv_full)
    out_far = side_swap(far_sum)
    qkv_near, ctx_near, lse_near = attend(one_near, qkv_full, bias_near, heads)
    ctx_near, out_far, up, up_others, down, cotangent, cot_side = tie(
        ctx_near, out_far, up, up_others, down, cotangent, cot_side
    )
    for k in evens:
        down[k] = high_swap(down[k ^ 1], 1)
    up_even = [spread(up[k])[1:] for k in evens]
    out_near = cores_sum(ctx_near, out_full)
    stream_in = tokens.astype(F32)
    residual = stream_in + (out_near + out_far.astype(F32))

    ln_two, normed_two, inverse_two = layer_norm_parts(residual, norm_values[2], norm_values[3])
    ln_two = ln_two.astype(BF16)
    ln_two, up_even, down = tie(ln_two, up_even, down)
    two_mate = core_swap(ln_two)
    two_side = side_swap(ln_two)
    places = odds + evens
    down_line = jnp.stack([down[k] for k in places])
    down_others = spread(down_line)[1:]
    grad_near = with_mate(cotangent)
    grad_far = with_mate(cot_side)
    two_near = join([ln_two, two_mate])
    two_near, grad_near, grad_far = tie(two_near, grad_near, grad_far)
    (up_full,) = assemble(
        entries(0, [up_low, *up_own])
        + joined_entries(odds, [up[k] for k in odds], up_others)
        + [
            entry
            for k, line in zip(evens, up_even, strict=True)
            for entry in entries(k, [up[k], *line])
        ]
    )
    hid_near, slope_near = gelu_parts(dot(two_near, up_full))
    hid_near, down_line, down_others, two_side = tie(hid_near, down_line, down_others, two_side)
    (down_full,) = assemble(
        [(0, 0, down_low, None)]
        + [(0, j + 1, other, len(odds)) for j, other in enumerate(up_others)]
        + [
            entry
            for n, k in enumerate(places)
            for entry in [(k, 0, down_line, n)]
            + [(k, j + 1, other, n) for j, other in enumerate(down_others)]
        ]
    )
    two_far = with_mate(two_side)
    pre_near = (dot(grad_near, down_full, NT) * slope_near.astype(F32)).astype(BF16)
    two_far, pre_near = tie(two_far, pre_near)
    hid_far, slope_far = gelu_parts(dot(two_far, up_full))
    pre_far = (dot(grad_far, down_full, NT) * slope_far.astype(F32)).astype(BF16)
    far_sum = cores_sum(pre_far, up_full, NT).astype(BF16)
    far_sum, pre_near, pre_far, hid_near, hid_far = tie(
        far_sum, pre_near, pre_far, hid_near, hid_far
    )
    back_far = side_swap(far_sum)
    back_near = cores_sum(pre_near, up_full, NT)
    back_near, hid_near, hid_far, grad_near, grad_far = tie(
        back_near, hid_near, hid_far, grad_near, grad_far
    )
    heavy, light = relay_ks()
    order = heavy + light
    grad_down = dot(join([hid_near, hid_far]), join([grad_near, grad_far]), TN).astype(BF16)
    grad_down, hid_near, hid_far = tie(grad_down, hid_near, hid_far)
    down_received = [scatter_send(grad_down, heavy)]
    last_terms = [dot(v[own:], down_full).astype(BF16) for v in (hid_far, hid_near)]
    last_terms, pre_near, pre_far = tie(last_terms, pre_near, pre_far)
    grad_up = weight_grad([two_near, two_far], [pre_near, pre_far])
    last_terms, grad_down, back_far, grad_up, down_received = tie(
        last_terms, grad_down, back_far, grad_up, down_received
    )
    grad_ln_two = back_near + back_far.astype(F32)
    grad_residual = cotangent.astype(F32) + layer_norm_back(
        grad_ln_two, normed_two, inverse_two, norm_values[2]
    )
    gain_two = jnp.sum(grad_ln_two * normed_two, axis=0)
    shift_two = jnp.sum(grad_ln_two, axis=0)

    res_low = grad_residual.astype(BF16)
    res_side = side_swap(res_low)
    res_mate = core_swap(res_low)
    last_mates = [core_swap(v) for v in last_terms]
    down_lines = scatter_lines(grad_down, heavy, down_received[0])
    res_mate, last_mates, down_lines = tie(res_mate, last_mates, down_lines)
    down_got = relay_send(down_lines)
    up_received = [scatter_send(grad_up, heavy)]
    dqkv_near = attend_back(
        qkv_near, bias_near, ctx_near, lse_near, res_low, res_mate, out_full, heads
    )
    dqkv_near, res_side, up_received, grad_up, down_got, grad_down, last_mates, hid_far = tie(
        dqkv_near, res_side, up_received, grad_up, down_got, grad_down, last_mates, hid_far
    )
    down_received.append(scatter_send(grad_down, light))
    res_side_mate = core_swap(res_side)
    up_lines = scatter_lines(grad_up, heavy, up_received[0])
    last_far = own_sum(hid_far, down_full, last_mates[0]).astype(BF16)
    grad_out = weight_grad(
        [ctx_near, ctx_far], [res_low, res_mate, res_side, res_side_mate], ctx_near.shape[1]
    )
    grad_out, last_far, grad_down, down_received[1] = tie(
        grad_out, last_far, grad_down, down_received[1]
    )
    down_lines.update(scatter_lines(grad_down, light, down_received[1]))
    res_side_mate, grad_out, down_lines, up_lines, last_far = tie(
        res_side_mate, grad_out, down_lines, up_lines, last_far
    )
    up_received.append(scatter_send(grad_up, light))
    out_received = scatter_send(grad_out, order)
    down_parts = relay_last(down_lines, down_got)
    up_got = relay_send(up_lines)
    last_side = side_swap(last_far)
    dqkv_far = attend_back(
        qkv_far, bias_far, ctx_far, lse_far, res_side, res_side_mate, out_full, heads
    )
    dqkv_far, up_got, up_received, grad_up, down_parts, grad_out, out_received, last_side = tie(
        dqkv_far, up_got, up_received, grad_up, down_parts, grad_out, out_received, last_side
    )

    up_lines.update(scatter_lines(grad_up, light, up_received[1]))
    out_lines = scatter_lines(grad_out, order, out_received)
    dqkv_far, dqkv_near, up_lines, out_lines = tie(dqkv_far, dqkv_near, up_lines, out_lines)
    up_parts = relay_last(up_lines, up_got)
    out_got = relay_send(out_lines)
    grad_qkv = dot(join([one_near, one_far]), join([dqkv_near, dqkv_far]), TN).astype(BF16)
    grad_qkv, dqkv_far, dqkv_near = tie(rows_first(grad_qkv), dqkv_far, dqkv_near)
    received = [scatter_send(grad_qkv, heavy)]
    first_mates = [mates_part(v, qkv_full, NT) for v in (dqkv_far, dqkv_near)]
    far_sum = own_sum(dqkv_far, qkv_full, first_mates[0], NT).astype(BF16)
    far_sum, first_mates, grad_qkv, dqkv_near, hid_near = tie(
        far_sum, first_mates, grad_qkv, dqkv_near, hid_near
    )
    first_far = side_swap(far_sum)
    received.append(scatter_send(grad_qkv, light))
    first_near = own_sum(dqkv_near, qkv_full, first_mates[1], NT)
    first_near, received[0], grad_qkv, hid_near = tie(first_near, received[0], grad_qkv, hid_near)
    qkv_lines = scatter_lines(grad_qkv, heavy, received[0])
    qkv_got = relay_send(qkv_lines)
    last_near = own_sum(hid_near, down_full, last_mates[1])
    layer_out = (residual + (last_near + last_side.astype(F32))).astype(BF16)
    (
        received[1], qkv_got, qkv_lines, out_got, out_lines, layer_out, up_parts, down_parts,
        grad_qkv,
    ) = tie(
        received[1], qkv_got, qkv_lines, out_got, out_lines, layer_out, up_parts, down_parts,
        grad_qkv,
    )
    qkv_lines.update(scatter_lines(grad_qkv, light, received[1]))
    qkv_parts = relay_last(qkv_lines, qkv_got)
    out_parts = relay_last(out_lines, out_got)
    summed_up, summed_down = parts_sum(up_parts), parts_sum(down_parts)
    early_squares = jnp.sum(summed_up * summed_up) + jnp.sum(summed_down * summed_down)

    _, normed_one, inverse_one = layer_norm_parts(stream_in, norm_values[0], norm_values[1])
    grad_ln_one = first_near + first_far.astype(F32)
    input_grad = (
        grad_residual + layer_norm_back(grad_ln_one, normed_one, inverse_one, norm_values[0])
    ).astype(BF16)
    gain_one = jnp.sum(grad_ln_one * normed_one, axis=0)
    shift_one = jnp.sum(grad_ln_one, axis=0)
    rows = jnp.stack([gain_one, shift_one, gain_two, shift_two])
    qkv_parts, out_parts, rows, input_grad, early_squares = tie(
        qkv_parts, out_parts, rows, input_grad, early_squares
    )
    packed = squares_packed(rows, early_squares, [qkv_parts, out_parts])
    packed = sum_all(packed)
    summed_norm = lax.dynamic_slice_in_dim(packed, dp * norm_rows, norm_rows, 1)
    grad_norm, shift_grad, results = adam_all(
        packed,
        [
            (*[v.transpose(1, 0, 2) for v in (qkv_weight, qkv_first, qkv_second)], qkv_parts, RATE_QKV),
            (out_weight, out_first, out_second, out_parts, RATE_OUT),
            (up_weight, up_first, up_second, up_parts, RATE_UP),
            (down_weight, down_first, down_second, down_parts, RATE_DOWN),
            (norm_params, norm_first, norm_second, [summed_norm], RATE_NORM),
        ],
    )
    grad_norm, shift_grad = grad_norm[0, 0], shift_grad[0]
    qkv_new, qkv_one, qkv_two = [v.transpose(1, 0, 2) for v in results[0]]
    out_new, out_one, out_two = results[1]
    up_new, up_one, up_two = results[2]
    down_new, down_one, down_two = results[3]
    norm_new, norm_one, norm_two = results[4]
    return (
        layer_out,
        input_grad,
        grad_norm,
        qkv_new,
        qkv_one,
        qkv_two,
        out_new,
        out_one,
        out_two,
        up_new,
        up_one,
        up_two,
        down_new,
        down_one,
        down_two,
        norm_new,
        norm_one,
        norm_two,
        shift_grad,
    )


def solution(mesh):
    tokens = P(("dp", "tensor"), None)
    columns = P("dp", None, "tensor")
    rows = P(("tensor", "dp"), None)
    both = P("dp", "tensor")
    norms = P(None, "dp")
    return jax.shard_map(
        on_device,
        mesh=mesh,
        in_specs=(tokens, tokens, P("dp"), P("dp", None), columns, rows, both, rows, norms)
        + (columns,) * 2
        + (rows,) * 2
        + (both,) * 2
        + (rows,) * 2
        + (norms,) * 2,
        out_specs=(tokens, tokens, P())
        + (columns,) * 3
        + (rows,) * 3
        + (both,) * 3
        + (rows,) * 3
        + (norms,) * 3
        + (P("dp"),),
        check_vma=False,
    )
```

```python
import functools

import jax
import jax.numpy as jnp
from jax import lax
from jax.experimental import pallas as pl
from jax.experimental.layout import Layout, with_layout_constraint
from jax.experimental.pallas import tpu as pltpu
from jax.sharding import PartitionSpec as P

HD = 64
STEP = 5

NORM_EPS = 1e-05
CLIP_LIMIT = 1.0
BETA_FIRST = 0.5
BETA_SECOND = 0.5
ADAM_EPS = 1e-08
DECAY_RATE = 0.01
RATE_QKV = 0.03
RATE_OUT = 0.5
RATE_UP = 0.03
RATE_DOWN = 0.015
RATE_NORM = 0.2

F32 = jnp.float32
BF16 = jnp.bfloat16
NN = (((1,), (0,)), ((), ()))
NT = (((1,), (1,)), ((), ()))
TN = (((0,), (0,)), ((), ()))
VMEM = pl.BlockSpec(memory_space=pltpu.VMEM)


def dot(left, right, dims=NN):
    return lax.dot_general(left, right, dims, preferred_element_type=F32)


def widen(block, columns, lane):
    rows = block.shape[0]
    wide = jnp.concatenate([block.astype(F32), jnp.zeros((rows, HD), F32)], axis=1)
    for n, column in enumerate(columns):
        wide = jnp.where(lane == HD + n, column, wide)
    return wide.astype(BF16)


def minus_parts(column):
    high = column.astype(BF16).astype(F32)
    rest = column - high
    middle = rest.astype(BF16).astype(F32)
    return [-high, -middle, middle - rest]


def attend_kernel(heads, step, one_ref, weight_ref, bias_ref, qkv_ref, ctx_ref, lse_ref, keys):
    tokens = qkv_ref.shape[0]
    width = heads * HD
    lane = lax.broadcasted_iota(jnp.int32, (1, 2 * HD), 1)

    def project(n, _):
        rows = pl.ds(pl.multiple_of(n * step, step), step)
        qkv_ref[rows, :] = dot(one_ref[rows, :], weight_ref[...]).astype(BF16)
        return 0

    lax.fori_loop(0, tokens // step, project, 0)
    bias = bias_ref[...].T[:, 0:1]
    for h in range(heads):
        keys[h] = widen(qkv_ref[:, width + h * HD : width + (h + 1) * HD], [bias], lane)

    def block(n, _):
        rows = pl.ds(pl.multiple_of(n * step, step), step)
        outs = []
        stat = jnp.zeros((step, 2 * HD), F32)
        for h in range(heads):
            query = qkv_ref[rows, h * HD : (h + 1) * HD].astype(F32) * HD ** (-0.5)
            scores = dot(widen(query, [jnp.ones((step, 1), F32)], lane), keys[h], NT)
            top = jnp.max(scores, axis=1, keepdims=True)
            weights = jnp.exp(scores - top)
            total = jnp.sum(weights, axis=1, keepdims=True)
            values = qkv_ref[:, 2 * width + h * HD : 2 * width + (h + 1) * HD]
            outs.append((dot(weights.astype(BF16), values) / total).astype(BF16))
            stat = jnp.where(lane == h, top + jnp.log(total), stat)
        ctx_ref[rows, :] = jnp.concatenate(outs, axis=1)
        lse_ref[rows, :] = stat
        return 0

    lax.fori_loop(0, tokens // step, block, 0)


def attend(one, weight, bias, heads, step=1024):
    tokens = one.shape[0]
    return pl.pallas_call(
        functools.partial(attend_kernel, heads, step),
        out_shape=(
            jax.ShapeDtypeStruct((tokens, 3 * heads * HD), BF16),
            jax.ShapeDtypeStruct((tokens, heads * HD), BF16),
            jax.ShapeDtypeStruct((tokens, 2 * HD), F32),
        ),
        in_specs=[VMEM] * 3,
        out_specs=[VMEM] * 3,
        scratch_shapes=[pltpu.VMEM((heads, tokens, 2 * HD), BF16)],
        compiler_params=pltpu.CompilerParams(vmem_limit_bytes=48 * 2**20),
        cost_estimate=pl.CostEstimate(flops=0, bytes_accessed=1, transcendentals=0),
        name="attend",
    )(one, weight, bias)


def attend_back_kernel(
    heads,
    step,
    qkv_ref,
    bias_ref,
    ctx_ref,
    lse_ref,
    own_ref,
    mate_ref,
    weight_ref,
    out_ref,
    keys,
    values,
    dk,
    dv,
    grad_ref,
):
    tokens = qkv_ref.shape[0]
    width = heads * HD
    scale = HD ** (-0.5)
    lane = lax.broadcasted_iota(jnp.int32, (1, 2 * HD), 1)
    one = jnp.ones((tokens, 1), F32)
    bias = bias_ref[...].T[:, 0:1]
    half = tokens // 2
    for n, ref in enumerate((own_ref, mate_ref)):
        grad_ref[n * half : (n + 1) * half, :] = dot(ref[...], weight_ref[...], NT).astype(BF16)
    for h in range(heads):
        key = qkv_ref[:, width + h * HD : width + (h + 1) * HD]
        value = qkv_ref[:, 2 * width + h * HD : 2 * width + (h + 1) * HD]
        keys[h] = widen(key, [bias, one, one, one], lane)
        values[h] = widen(value, [one, one, one], lane)
    dk[...] = jnp.zeros_like(dk)
    dv[...] = jnp.zeros_like(dv)

    def block(n, _):
        rows = pl.ds(pl.multiple_of(n * step, step), step)
        outs = []
        ones = jnp.ones((step, 1), F32)
        for h in range(heads):
            cols = slice(h * HD, (h + 1) * HD)
            query = qkv_ref[rows, cols].astype(F32) * scale
            grad = grad_ref[rows, cols].astype(F32)
            delta = jnp.sum(grad * ctx_ref[rows, cols].astype(F32), axis=1, keepdims=True)
            lse = lse_ref[rows, h : h + 1]
            weights = jnp.exp(dot(widen(query, [ones] + minus_parts(lse), lane), keys[h], NT))
            slopes = dot(widen(grad, minus_parts(delta), lane), values[h], NT)
            slopes = (weights * slopes).astype(BF16)
            weights = weights.astype(BF16)
            key = qkv_ref[:, width + h * HD : width + (h + 1) * HD]
            outs.append((dot(slopes, key) * scale).astype(BF16))
            dk[h] += dot(query.T.astype(BF16), slopes)
            dv[h] += dot(grad.T.astype(BF16), weights)
        out_ref[rows, :width] = jnp.concatenate(outs, axis=1)
        return 0

    lax.fori_loop(0, tokens // step, block, 0)
    for place, total in ((1, dk), (2, dv)):
        turned = jnp.concatenate([total[h].T for h in range(heads)], axis=1)
        out_ref[:, place * width : (place + 1) * width] = turned.astype(BF16)


def attend_back(qkv, bias, ctx, lse, own, mate, weight, heads, step=1024):
    tokens = qkv.shape[0]
    return pl.pallas_call(
        functools.partial(attend_back_kernel, heads, step),
        out_shape=jax.ShapeDtypeStruct((tokens, 3 * heads * HD), BF16),
        in_specs=[VMEM] * 7,
        out_specs=VMEM,
        scratch_shapes=[pltpu.VMEM((heads, tokens, 2 * HD), BF16)] * 2
        + [pltpu.VMEM((heads, HD, tokens), F32)] * 2
        + [pltpu.VMEM((tokens, heads * HD), BF16)],
        compiler_params=pltpu.CompilerParams(vmem_limit_bytes=48 * 2**20),
        cost_estimate=pl.CostEstimate(flops=0, bytes_accessed=1, transcendentals=0),
        name="attend_back",
    )(qkv, bias, ctx, lse, own, mate, weight)


def swap(value, axis, bits):
    size = lax.axis_size(axis)
    return lax.ppermute(value, axis, [(i, i ^ bits) for i in range(size)])


def core_swap(value):
    return swap(value, "tensor", 1)


def side_swap(value):
    return swap(value, "tensor", 2)


def tie(*values):
    return lax.optimization_barrier(values)


def dp_split(size):
    fast = 2 if size < 16 else 4
    return size // fast, fast


def high_swap(value, k):
    return swap(value, "dp", k * dp_split(lax.axis_size("dp"))[1])


def gather_small(shard):
    size = lax.axis_size("dp")
    blocks = shard[None]
    bits = 1
    while bits < size:
        blocks = jnp.concatenate([blocks, swap(blocks, "dp", bits)])
        bits *= 2
    index = lax.axis_index("dp")
    return jnp.stack([blocks[index ^ n] for n in range(size)])


def spread(block):
    _, fast = dp_split(lax.axis_size("dp"))
    return [block] + [swap(block, "dp", j) for j in range(1, fast)]


def entries(k, line, at=None):
    return [(k, j, block, at if j else None) for j, block in enumerate(line)]


def joined_entries(ks, blocks, others):
    return [
        entry
        for n, (k, block) in enumerate(zip(ks, blocks, strict=True))
        for entry in entries(k, [block, *others], n)
    ]


def pack_kernel(qkv_ref, out_ref, packed_ref):
    rows, width = out_ref.shape
    step = width * rows // qkv_ref.shape[1]
    parts = [qkv_ref[n] for n in range(qkv_ref.shape[0])]
    turned = [out_ref[:, n : n + step] for n in range(0, width, step)]
    packed = jnp.concatenate([*parts, jnp.concatenate(turned, axis=0)], axis=1)
    packed_ref[...] = packed.astype(BF16)


def pack_first(qkv, out):
    rows = qkv.shape[1]
    shape = (rows, qkv.shape[0] * qkv.shape[2] + out.size // rows)
    if out.shape[0] % 8:
        step = out.shape[1] * out.shape[0] // rows
        turned = jnp.concatenate([out[:, n : n + step] for n in range(0, out.shape[1], step)])
        return jnp.concatenate([*qkv, turned], axis=1).astype(BF16)
    return pl.pallas_call(
        pack_kernel,
        out_shape=jax.ShapeDtypeStruct(shape, BF16),
        in_specs=[VMEM] * 2,
        out_specs=VMEM,
        compiler_params=pltpu.CompilerParams(vmem_limit_bytes=16 * 2**20),
        cost_estimate=pl.CostEstimate(flops=0, bytes_accessed=1, transcendentals=0),
        name="pack_first",
    )(qkv, out)


def assemble(blocks, cut=None):
    slow, fast = dp_split(lax.axis_size("dp"))
    rows, columns = blocks[0][2].shape[-2:]
    kind = blocks[0][2].dtype
    index = lax.axis_index("dp")
    place = jnp.stack([index // fast, index % fast]).astype(jnp.int32)
    where = [(k, j, at) for k, j, _, at in blocks]
    out_rows = rows * (columns - cut) // columns if cut else 0

    def kernel(place_ref, *refs):
        ins, outs = refs[: len(where)], refs[len(where) : -2]
        whole, sems = refs[-2:] if cut else (outs[0], refs[-1])
        copies = []
        for n, (source, (k, j, at)) in enumerate(zip(ins, where, strict=True)):
            target = (place_ref[0] ^ k) * fast + (place_ref[1] ^ j)
            source = source if at is None else source.at[at]
            copies.append(pltpu.make_async_copy(source, whole.at[target], sems.at[n]))
        for copy in copies:
            copy.start()
        for copy in copies:
            copy.wait()
        if cut:
            outs[0][...] = whole[:, :, :cut]
            if out_rows % 8:
                outs[1][...] = whole[:, :, cut:]
            else:
                turned = []
                for n in range(slow * fast):
                    block = whole[n, :, cut:].astype(F32)
                    parts = [block[m : m + out_rows] for m in range(0, rows, out_rows)]
                    turned.append(jnp.concatenate(parts, axis=1))
                outs[1][...] = jnp.concatenate(turned, axis=0).astype(kind)

    size = slow * fast
    full = (size, rows, columns)
    if not cut:
        shapes = [full]
    elif out_rows % 8:
        shapes = [(size, rows, cut), (size, rows, columns - cut)]
    else:
        shapes = [(size, rows, cut), (size * out_rows, columns)]
    outs = pl.pallas_call(
        kernel,
        out_shape=[jax.ShapeDtypeStruct(shape, kind) for shape in shapes],
        in_specs=[pl.BlockSpec(memory_space=pltpu.SMEM)]
        + [pl.BlockSpec(memory_space=pltpu.HBM)] * len(where),
        out_specs=[VMEM] * len(shapes),
        scratch_shapes=[
            pltpu.VMEM(full if cut else (8, 16, 128), kind),
            pltpu.SemaphoreType.DMA((len(where),)),
        ],
        compiler_params=pltpu.CompilerParams(vmem_limit_bytes=24 * 2**20),
        cost_estimate=pl.CostEstimate(flops=0, bytes_accessed=1, transcendentals=0),
        name="assemble",
    )(place, *[array for _, _, array, _ in blocks])
    outs = list(outs)
    if cut and out_rows % 8:
        turned = outs[1].reshape(size, rows // out_rows, out_rows, columns - cut)
        outs[1] = turned.transpose(0, 2, 1, 3).reshape(size * out_rows, columns)
    return [out.reshape(-1, out.shape[-1]) for out in outs]


def pick(total, k, j):
    slow, fast = dp_split(lax.axis_size("dp"))
    rows = total.shape[0] // (slow * fast)
    index = lax.axis_index("dp")
    start = (((index // fast) ^ k) * fast + ((index % fast) ^ j)) * rows
    return lax.dynamic_slice_in_dim(total, start, rows, 0)


def rows_first(value):
    return with_layout_constraint(value, Layout(tuple(range(value.ndim))))


def scatter_send(total, ks):
    _, fast = dp_split(lax.axis_size("dp"))
    return [
        swap(jnp.concatenate([rows_first(pick(total, k, j)) for k in ks]), "dp", j)
        for j in range(1, fast)
    ]


def scatter_lines(total, ks, received):
    lines = {}
    for n, k in enumerate(ks):
        line = pick(total, k, 0).astype(F32)
        rows = line.shape[0]
        for part in received:
            line = line + part[n * rows : (n + 1) * rows].astype(F32)
        lines[k] = rows_first(line.astype(BF16))
    return lines


def relay_ks():
    slow, _ = dp_split(lax.axis_size("dp"))
    return [1, *range(2, slow, 2)], [*range(3, slow, 2), 0]


def relay_send(lines):
    ks, _ = relay_ks()
    return high_swap(jnp.concatenate([lines[k] for k in ks]), 1)


def relay_split(received):
    ks, _ = relay_ks()
    rows = received.shape[0] // len(ks)
    return {k: received[n * rows : (n + 1) * rows] for n, k in enumerate(ks)}


def relay_last(lines, received):
    _, ks = relay_ks()
    got = relay_split(received)
    parts = [lines[0], got[1]]
    for k in ks[:-1]:
        line = lines[k].astype(F32) + got[k ^ 1].astype(F32)
        parts.append(high_swap(line.astype(BF16), k))
    return parts


def parts_sum(parts):
    return functools.reduce(jnp.add, [part.astype(F32) for part in parts])


def cores_sum(left, right, dims=NN):
    return own_sum(left, right, mates_part(left, right, dims), dims)


def mates_part(left, right, dims=NN):
    return core_swap(dot(left[left.shape[0] // 2 :], right, dims).astype(BF16))


def own_sum(left, right, mate, dims=NN):
    return dot(left[: left.shape[0] // 2], right, dims) + mate.astype(F32)


def side_send(value):
    half = value.shape[0] // 2
    return [side_swap(value[:half]), side_swap(value[half:])]


def join(parts):
    return jnp.concatenate(parts)


def with_mate(own):
    return jnp.concatenate([own, core_swap(own)])


def norm_kernel(step, *refs):
    *pieces, rows_ref, out_ref = refs
    gain, shift = rows_ref[0:1, :], rows_ref[1:2, :]
    at = 0
    for ref in pieces:
        for start in range(0, ref.shape[0], step):
            values = ref[start : start + step, :].astype(F32)
            centered = values - jnp.mean(values, axis=-1, keepdims=True)
            inverse = lax.rsqrt(jnp.mean(centered * centered, axis=-1, keepdims=True) + NORM_EPS)
            out_ref[at : at + step, :] = (centered * inverse * gain + shift).astype(BF16)
            at += step


def norm_tokens(pieces, rows, step=128):
    size, width = sum(v.shape[0] for v in pieces), pieces[0].shape[1]
    return pl.pallas_call(
        functools.partial(norm_kernel, step),
        out_shape=jax.ShapeDtypeStruct((size, width), BF16),
        in_specs=[VMEM] * (len(pieces) + 1),
        out_specs=VMEM,
        compiler_params=pltpu.CompilerParams(vmem_limit_bytes=24 * 2**20),
        cost_estimate=pl.CostEstimate(flops=0, bytes_accessed=1, transcendentals=0),
        name="norm_tokens",
    )(*pieces, rows)


def weight_grad_kernel(count, *refs):
    lefts, rights, out_ref = refs[:count], refs[count:-1], refs[-1]
    total = None
    at = 0
    for left in lefts:
        for start in range(0, left.shape[0], rights[0].shape[0]):
            right = rights[at]
            at += 1
            term = dot(left[start : start + right.shape[0], :], right[...], TN)
            total = term if total is None else total + term
    out_ref[...] = total.astype(BF16)


def weight_grad(lefts, rights, step=256):
    rows, columns = lefts[0].shape[1], rights[0].shape[1]
    return pl.pallas_call(
        functools.partial(weight_grad_kernel, len(lefts)),
        grid=(rows // step,),
        out_shape=jax.ShapeDtypeStruct((rows, columns), BF16),
        in_specs=[pl.BlockSpec((v.shape[0], step), lambda i: (0, i)) for v in lefts]
        + [pl.BlockSpec(v.shape, lambda i: (0, 0)) for v in rights],
        out_specs=pl.BlockSpec((step, columns), lambda i: (i, 0)),
        compiler_params=pltpu.CompilerParams(vmem_limit_bytes=40 * 2**20),
        cost_estimate=pl.CostEstimate(flops=0, bytes_accessed=1, transcendentals=0),
        name="weight_grad",
    )(*lefts, *rights)


def sum_all(value):
    size = lax.axis_size("dp")
    value = value + core_swap(value)
    steps = [("tensor", 2)] + [("dp", 1 << n) for n in range(size.bit_length() - 1)]
    for n in range(0, len(steps), 2):
        first = steps[n]
        if n + 1 == len(steps):
            value = value + swap(value, *first)
            continue
        second = steps[n + 1]
        if first[0] == second[0]:
            both = swap(value, first[0], first[1] | second[1])
        else:
            tensor = lax.axis_size("tensor")
            bits = first[1] | second[1] * tensor
            pairs = [(i, i ^ bits) for i in range(size * tensor)]
            both = lax.ppermute(value, ("dp", "tensor"), pairs)
        value = (value + swap(value, *first)) + (swap(value, *second) + both)
    return value


def layer_norm_parts(values, gain_row, shift_row):
    centered = values - jnp.mean(values, axis=-1, keepdims=True)
    inverse = lax.rsqrt(jnp.mean(centered * centered, axis=-1, keepdims=True) + NORM_EPS)
    normed = centered * inverse
    return (normed * gain_row + shift_row, normed, inverse)


def layer_norm_back(grad_normed, normed, inverse, gain_row):
    scaled = grad_normed * gain_row
    return inverse * (
        scaled
        - jnp.mean(scaled, axis=-1, keepdims=True)
        - normed * jnp.mean(scaled * normed, axis=-1, keepdims=True)
    )


def adam_update(master, grad_sum, moment_one, moment_two, step_rate, clip_factor):
    clipped = grad_sum * clip_factor
    one_new = BETA_FIRST * moment_one + (1.0 - BETA_FIRST) * clipped
    two_new = BETA_SECOND * moment_two + (1.0 - BETA_SECOND) * clipped * clipped
    one_hat = one_new / (1.0 - BETA_FIRST**STEP)
    two_hat = two_new / (1.0 - BETA_SECOND**STEP)
    master_new = master - step_rate * (
        one_hat / (jnp.sqrt(two_hat) + ADAM_EPS) + DECAY_RATE * master
    )
    return (master_new, one_new, two_new)


def first_back_kernel(tokens_ref, near_ref, far_ref, res_ref, rows_ref, out_ref, sums_ref):
    @pl.when(pl.program_id(0) == 0)
    def _():
        sums_ref[...] = jnp.zeros_like(sums_ref)

    values = tokens_ref[...].astype(F32)
    centered = values - jnp.mean(values, axis=-1, keepdims=True)
    inverse = lax.rsqrt(jnp.mean(centered * centered, axis=-1, keepdims=True) + NORM_EPS)
    normed = centered * inverse
    grad = near_ref[...] + far_ref[...].astype(F32)
    back = layer_norm_back(grad, normed, inverse, rows_ref[0:1, :])
    out_ref[...] = (res_ref[...] + back).astype(BF16)
    width = grad.shape[-1]
    sums_ref[0:8, :] += jnp.sum((grad * normed).reshape(-1, 8, width), axis=0)
    sums_ref[8:16, :] += jnp.sum(grad.reshape(-1, 8, width), axis=0)


def first_back(tokens, near, far, res, rows, step=128):
    size, width = tokens.shape
    block = pl.BlockSpec((step, width), lambda i: (i, 0))
    return pl.pallas_call(
        first_back_kernel,
        grid=(size // step,),
        out_shape=(
            jax.ShapeDtypeStruct((size, width), BF16),
            jax.ShapeDtypeStruct((16, width), F32),
        ),
        in_specs=[block] * 4 + [pl.BlockSpec(rows.shape, lambda i: (0, 0))],
        out_specs=[block, pl.BlockSpec((16, width), lambda i: (0, 0))],
        compiler_params=pltpu.CompilerParams(vmem_limit_bytes=60 * 2**20),
        cost_estimate=pl.CostEstimate(flops=0, bytes_accessed=1, transcendentals=0),
        name="first_back",
    )(tokens, near, far, res, rows)


def squares_kernel(counts, sums_ref, two_ref, early_ref, *refs):
    *parts, out_ref = refs
    width = two_ref.shape[1]
    total = early_ref[...]
    for count in counts:
        value = functools.reduce(jnp.add, [part[...].astype(F32) for part in parts[:count]])
        parts = parts[count:]
        total += jnp.sum(jnp.sum(value * value, axis=0, keepdims=True), axis=1, keepdims=True)
    for n in range(2):
        out_ref[n : n + 1, :width] = jnp.sum(
            sums_ref[8 * n : 8 * n + 8, :], axis=0, keepdims=True
        )
    out_ref[2:4, :width] = two_ref[...]
    out_ref[:, width:] = jnp.broadcast_to(total, (4, 128))


def squares_packed(sums, two, early, gradients):
    return pl.pallas_call(
        functools.partial(squares_kernel, [len(parts) for parts in gradients]),
        out_shape=jax.ShapeDtypeStruct((4, two.shape[1] + 128), F32),
        in_specs=[VMEM] * (3 + sum(len(parts) for parts in gradients)),
        out_specs=VMEM,
        compiler_params=pltpu.CompilerParams(vmem_limit_bytes=24 * 2**20),
        cost_estimate=pl.CostEstimate(flops=0, bytes_accessed=1, transcendentals=0),
        name="squares_packed",
    )(sums, two, early.reshape(1, 1), *[part for parts in gradients for part in parts])


def adam_kernel(rates, counts, packed_ref, *refs):
    *refs, norm_ref, shift_ref = refs
    width = packed_ref.shape[1] - 128
    rows = packed_ref[:, :width]
    squares = jnp.sum(jnp.sum(rows * rows, axis=0, keepdims=True), axis=1, keepdims=True)
    grad_norm = jnp.sqrt(packed_ref[0:1, width : width + 1] + squares)
    clip_factor = jnp.minimum(1.0, CLIP_LIMIT / grad_norm)
    norm_ref[...] = grad_norm
    ins, outs = refs[: -3 * len(rates)], refs[-3 * len(rates) :]
    at = 0
    for n, (rate, count) in enumerate(zip(rates, counts, strict=True)):
        master, one, two = ins[at : at + 3]
        parts = ins[at + 3 : at + 3 + count]
        at += 3 + count
        total = functools.reduce(jnp.add, [part[...].astype(F32) for part in parts])
        results = outs[3 * n : 3 * n + 3]
        if n == len(rates) - 1:
            shift_ref[...] = clip_factor * total[3:4, :]
        if master.ndim == 2:
            for out, value in zip(
                results,
                adam_update(master[...], total, one[...], two[...], rate, clip_factor),
                strict=True,
            ):
                out[...] = value
            continue
        width = master.shape[2]
        for c in range(master.shape[0]):
            grad = total[:, c * width : (c + 1) * width]
            values = adam_update(master[c], grad, one[c], two[c], rate, clip_factor)
            for out, value in zip(results, values, strict=True):
                out[c] = value


def adam_all(packed, weights):
    arrays = [v for master, one, two, parts, _ in weights for v in (master, one, two, *parts)]
    shapes = [master.shape for master, *_ in weights for _ in range(3)]
    shapes += [(1, 1), (1, weights[-1][0].shape[1])]
    outs = pl.pallas_call(
        functools.partial(
            adam_kernel, [rate for *_, rate in weights], [len(w[3]) for w in weights]
        ),
        out_shape=[jax.ShapeDtypeStruct(shape, F32) for shape in shapes],
        in_specs=[VMEM] * (len(arrays) + 1),
        out_specs=[VMEM] * len(shapes),
        compiler_params=pltpu.CompilerParams(vmem_limit_bytes=60 * 2**20),
        name="adam_all",
    )(packed, *arrays)
    return outs[-2], outs[-1], [outs[n : n + 3] for n in range(0, len(outs) - 2, 3)]


def gelu_parts(value):
    share = 0.5 + 0.5 * lax.erf(value * 0.5**0.5)
    slope = share + value * jnp.exp(-0.5 * value * value) * (0.5 / jnp.pi) ** 0.5
    return (value * share).astype(BF16), slope.astype(BF16)


def on_device(
    tokens,
    cotangent,
    lengths,
    key_mask,
    qkv_weight,
    out_weight,
    up_weight,
    down_weight,
    norm_params,
    qkv_first,
    qkv_second,
    out_first,
    out_second,
    up_first,
    up_second,
    down_first,
    down_second,
    norm_first,
    norm_second,
):
    own, width = tokens.shape
    cell = 2 * own
    heads = qkv_weight.shape[2] // HD
    dp, tensor = lax.axis_index("dp"), lax.axis_index("tensor")
    side, core = tensor // 2, tensor % 2

    norm_rows = norm_params.shape[1]

    positions = jnp.arange(cell, dtype=jnp.int32)
    key_valid = (positions[None, :] < lengths[:, None]) & (
        (key_mask == 1) | (positions[None, :] == 0)
    )
    bias = jnp.where(key_valid, 0.0, -1e30).astype(F32)
    bias = jnp.where(side == 0, bias, bias[::-1])
    bias = jnp.where(core == 0, bias, jnp.roll(bias, own, axis=1))
    bias_near, bias_far = [jnp.broadcast_to(row, (8, cell)) for row in bias]

    slow, _ = dp_split(lax.axis_size("dp"))
    odds, evens = list(range(1, slow, 2)), list(range(2, slow, 2))
    qkv_width = 3 * heads * HD
    head = own // 4
    first_low = pack_first(qkv_weight.transpose(1, 0, 2), out_weight)
    first = {k: high_swap(first_low, k) for k in odds}
    first_own = spread(first_low)
    top = own // 4
    side_top = side_swap(tokens[:top])
    mate_tokens = core_swap(tokens)
    norm_low, mate_tokens = tie(norm_params.astype(BF16), mate_tokens)
    norm_low = gather_small(norm_low)
    up_low, down_low = up_weight.astype(BF16), down_weight.astype(BF16)
    first, first_own, side_top, tokens, up_low, down_low = tie(
        first, first_own, side_top, tokens, up_low, down_low
    )
    for k in evens:
        first[k] = high_swap(first[k ^ 1], 1)
    first_lines = {k: spread(first[k]) for k in odds}
    side_rest = side_swap(tokens[top:])
    top_mate = core_swap(side_top)
    first, first_lines, up_low, down_low, cotangent, side_rest, top_mate, norm_low = tie(
        first, first_lines, up_low, down_low, cotangent, side_rest, top_mate, norm_low
    )
    for k in evens:
        first_lines[k] = spread(first[k])
    rest_mate = core_swap(side_rest)
    up = {k: high_swap(up_low, k) for k in odds}
    norm_values = jnp.moveaxis(norm_low, 0, 1).reshape(4, width).astype(F32)
    one_near = norm_tokens([tokens, mate_tokens], norm_values[:2])
    one_far = norm_tokens([side_top, side_rest, top_mate, rest_mate], norm_values[:2])
    cot_side = side_swap(cotangent)
    first_lines, one_far, one_near, up_low = tie(first_lines, one_far, one_near, up_low)
    up_own = spread(up_low)[1:]

    qkv_full, out_full = assemble(
        sum([entries(k, line) for k, line in first_lines.items()], entries(0, first_own)),
        qkv_width,
    )
    qkv_far, ctx_far, lse_far = attend(one_far, qkv_full, bias_far, heads)
    ctx_far, up, up_own, cot_side, down_low = tie(ctx_far, up, up_own, cot_side, down_low)
    for k in evens:
        up[k] = high_swap(up[k ^ 1], 1)
    up_others = spread(jnp.stack([up[k] for k in odds] + [down_low]))[1:]
    down = {k: high_swap(down_low, k) for k in odds}
    far_sum = cores_sum(ctx_far, out_full).astype(BF16)
    far_sum, one_near, qkv_full = tie(far_sum, one_near, qkv_full)
    out_far = side_swap(far_sum)
    qkv_near, ctx_near, lse_near = attend(one_near, qkv_full, bias_near, heads)
    ctx_near, out_far, up, up_others, down, cotangent, cot_side = tie(
        ctx_near, out_far, up, up_others, down, cotangent, cot_side
    )
    for k in evens:
        down[k] = high_swap(down[k ^ 1], 1)
    up_even = [spread(up[k])[1:] for k in evens]
    out_near = cores_sum(ctx_near, out_full)
    stream_in = tokens.astype(F32)
    residual = stream_in + (out_near + out_far.astype(F32))

    ln_two, normed_two, inverse_two = layer_norm_parts(residual, norm_values[2], norm_values[3])
    ln_two = ln_two.astype(BF16)
    ln_two, up_even, down = tie(ln_two, up_even, down)
    two_mate = core_swap(ln_two)
    two_side = side_swap(ln_two)
    places = odds + evens
    down_line = jnp.stack([down[k] for k in places])
    down_others = spread(down_line)[1:]
    grad_near = with_mate(cotangent)
    grad_far = with_mate(cot_side)
    two_near = join([ln_two, two_mate])
    two_near, grad_near, grad_far = tie(two_near, grad_near, grad_far)
    (up_full,) = assemble(
        entries(0, [up_low, *up_own])
        + joined_entries(odds, [up[k] for k in odds], up_others)
        + [
            entry
            for k, line in zip(evens, up_even, strict=True)
            for entry in entries(k, [up[k], *line])
        ]
    )
    hid_near, slope_near = gelu_parts(dot(two_near, up_full))
    hid_near, down_line, down_others, two_side = tie(hid_near, down_line, down_others, two_side)
    (down_full,) = assemble(
        [(0, 0, down_low, None)]
        + [(0, j + 1, other, len(odds)) for j, other in enumerate(up_others)]
        + [
            entry
            for n, k in enumerate(places)
            for entry in [(k, 0, down_line, n)]
            + [(k, j + 1, other, n) for j, other in enumerate(down_others)]
        ]
    )
    two_far = with_mate(two_side)
    pre_near = (dot(grad_near, down_full, NT) * slope_near.astype(F32)).astype(BF16)
    two_far, pre_near = tie(two_far, pre_near)
    hid_far, slope_far = gelu_parts(dot(two_far, up_full))
    pre_far = (dot(grad_far, down_full, NT) * slope_far.astype(F32)).astype(BF16)
    far_sum = cores_sum(pre_far, up_full, NT).astype(BF16)
    far_sum, pre_near, pre_far, hid_near, hid_far = tie(
        far_sum, pre_near, pre_far, hid_near, hid_far
    )
    back_far = side_swap(far_sum)
    back_near = cores_sum(pre_near, up_full, NT)
    back_near, hid_near, hid_far, grad_near, grad_far = tie(
        back_near, hid_near, hid_far, grad_near, grad_far
    )
    heavy, light = relay_ks()
    order = heavy + light
    grad_down = dot(join([hid_near, hid_far]), join([grad_near, grad_far]), TN).astype(BF16)
    grad_down, hid_near, hid_far = tie(grad_down, hid_near, hid_far)
    down_received = [scatter_send(grad_down, heavy)]
    last_terms = [dot(v[own:], down_full).astype(BF16) for v in (hid_far, hid_near)]
    last_terms, pre_near, pre_far = tie(last_terms, pre_near, pre_far)
    grad_up = weight_grad([two_near, two_far], [pre_near, pre_far])
    last_terms, grad_down, back_far, grad_up, down_received = tie(
        last_terms, grad_down, back_far, grad_up, down_received
    )
    grad_ln_two = back_near + back_far.astype(F32)
    grad_residual = cotangent.astype(F32) + layer_norm_back(
        grad_ln_two, normed_two, inverse_two, norm_values[2]
    )
    gain_two = jnp.sum(grad_ln_two * normed_two, axis=0)
    shift_two = jnp.sum(grad_ln_two, axis=0)

    res_low = grad_residual.astype(BF16)
    res_side = side_swap(res_low)
    res_mate = core_swap(res_low)
    last_mates = [core_swap(v) for v in last_terms]
    down_lines = scatter_lines(grad_down, heavy, down_received[0])
    res_mate, last_mates, down_lines = tie(res_mate, last_mates, down_lines)
    down_got = relay_send(down_lines)
    up_received = [scatter_send(grad_up, heavy)]
    dqkv_near = attend_back(
        qkv_near, bias_near, ctx_near, lse_near, res_low, res_mate, out_full, heads
    )
    dqkv_near, res_side, up_received, grad_up, down_got, grad_down, last_mates, hid_far = tie(
        dqkv_near, res_side, up_received, grad_up, down_got, grad_down, last_mates, hid_far
    )
    down_received.append(scatter_send(grad_down, light))
    res_side_mate = core_swap(res_side)
    up_lines = scatter_lines(grad_up, heavy, up_received[0])
    last_far = own_sum(hid_far, down_full, last_mates[0]).astype(BF16)
    grad_out = weight_grad(
        [ctx_near, ctx_far], [res_low, res_mate, res_side, res_side_mate], ctx_near.shape[1]
    )
    grad_out, last_far, grad_down, down_received[1] = tie(
        grad_out, last_far, grad_down, down_received[1]
    )
    down_lines.update(scatter_lines(grad_down, light, down_received[1]))
    res_side_mate, grad_out, down_lines, up_lines, last_far = tie(
        res_side_mate, grad_out, down_lines, up_lines, last_far
    )
    up_received.append(scatter_send(grad_up, light))
    out_received = scatter_send(grad_out, order)
    down_parts = relay_last(down_lines, down_got)
    up_got = relay_send(up_lines)
    last_side = side_swap(last_far)
    dqkv_far = attend_back(
        qkv_far, bias_far, ctx_far, lse_far, res_side, res_side_mate, out_full, heads
    )
    dqkv_far, up_got, up_received, grad_up, down_parts, grad_out, out_received, last_side = tie(
        dqkv_far, up_got, up_received, grad_up, down_parts, grad_out, out_received, last_side
    )

    up_lines.update(scatter_lines(grad_up, light, up_received[1]))
    out_lines = scatter_lines(grad_out, order, out_received)
    dqkv_far, dqkv_near, up_lines, out_lines = tie(dqkv_far, dqkv_near, up_lines, out_lines)
    up_parts = relay_last(up_lines, up_got)
    out_got = relay_send(out_lines)
    grad_qkv = dot(join([one_near, one_far]), join([dqkv_near, dqkv_far]), TN).astype(BF16)
    grad_qkv, dqkv_far, dqkv_near = tie(rows_first(grad_qkv), dqkv_far, dqkv_near)
    received = [scatter_send(grad_qkv, heavy)]
    first_mates = [mates_part(v, qkv_full, NT) for v in (dqkv_far, dqkv_near)]
    far_sum = own_sum(dqkv_far, qkv_full, first_mates[0], NT).astype(BF16)
    far_sum, first_mates, grad_qkv, dqkv_near, hid_near = tie(
        far_sum, first_mates, grad_qkv, dqkv_near, hid_near
    )
    first_far = side_swap(far_sum)
    received.append(scatter_send(grad_qkv, light))
    first_near = own_sum(dqkv_near, qkv_full, first_mates[1], NT)
    first_near, received[0], grad_qkv, hid_near = tie(first_near, received[0], grad_qkv, hid_near)
    qkv_lines = scatter_lines(grad_qkv, heavy, received[0])
    qkv_got = relay_send(qkv_lines)
    last_near = own_sum(hid_near, down_full, last_mates[1])
    layer_out = (residual + (last_near + last_side.astype(F32))).astype(BF16)
    (
        received[1], qkv_got, qkv_lines, out_got, out_lines, layer_out, up_parts, down_parts,
        grad_qkv,
    ) = tie(
        received[1], qkv_got, qkv_lines, out_got, out_lines, layer_out, up_parts, down_parts,
        grad_qkv,
    )
    qkv_lines.update(scatter_lines(grad_qkv, light, received[1]))
    qkv_parts = relay_last(qkv_lines, qkv_got)
    out_parts = relay_last(out_lines, out_got)
    summed_up, summed_down = parts_sum(up_parts), parts_sum(down_parts)
    early_squares = jnp.sum(summed_up * summed_up) + jnp.sum(summed_down * summed_down)

    input_grad, sums_one = first_back(tokens, first_near, first_far, grad_residual, norm_values)
    rows_two = jnp.stack([gain_two, shift_two])
    qkv_parts, sums_one, input_grad, early_squares = tie(
        qkv_parts, sums_one, input_grad, early_squares
    )
    packed = squares_packed(sums_one, rows_two, early_squares, [qkv_parts, out_parts])
    packed = sum_all(packed)
    summed_norm = lax.dynamic_slice_in_dim(packed, dp * norm_rows, norm_rows, 1)
    grad_norm, shift_grad, results = adam_all(
        packed,
        [
            (*[v.transpose(1, 0, 2) for v in (qkv_weight, qkv_first, qkv_second)], qkv_parts, RATE_QKV),
            (out_weight, out_first, out_second, out_parts, RATE_OUT),
            (up_weight, up_first, up_second, up_parts, RATE_UP),
            (down_weight, down_first, down_second, down_parts, RATE_DOWN),
            (norm_params, norm_first, norm_second, [summed_norm], RATE_NORM),
        ],
    )
    grad_norm, shift_grad = grad_norm[0, 0], shift_grad[0]
    qkv_new, qkv_one, qkv_two = [v.transpose(1, 0, 2) for v in results[0]]
    out_new, out_one, out_two = results[1]
    up_new, up_one, up_two = results[2]
    down_new, down_one, down_two = results[3]
    norm_new, norm_one, norm_two = results[4]
    return (
        layer_out,
        input_grad,
        grad_norm,
        qkv_new,
        qkv_one,
        qkv_two,
        out_new,
        out_one,
        out_two,
        up_new,
        up_one,
        up_two,
        down_new,
        down_one,
        down_two,
        norm_new,
        norm_one,
        norm_two,
        shift_grad,
    )


def solution(mesh):
    tokens = P(("dp", "tensor"), None)
    columns = P("dp", None, "tensor")
    rows = P(("tensor", "dp"), None)
    both = P("dp", "tensor")
    norms = P(None, "dp")
    return jax.shard_map(
        on_device,
        mesh=mesh,
        in_specs=(tokens, tokens, P("dp"), P("dp", None), columns, rows, both, rows, norms)
        + (columns,) * 2
        + (rows,) * 2
        + (both,) * 2
        + (rows,) * 2
        + (norms,) * 2,
        out_specs=(tokens, tokens, P())
        + (columns,) * 3
        + (rows,) * 3
        + (both,) * 3
        + (rows,) * 3
        + (norms,) * 3
        + (P("dp"),),
        check_vma=False,
    )
```

```python
import functools

import jax
import jax.numpy as jnp
from jax import lax
from jax.experimental import pallas as pl
from jax.experimental.layout import Layout, with_layout_constraint
from jax.experimental.pallas import tpu as pltpu
from jax.sharding import PartitionSpec as P

HD = 64
STEP = 5

NORM_EPS = 1e-05
CLIP_LIMIT = 1.0
BETA_FIRST = 0.5
BETA_SECOND = 0.5
ADAM_EPS = 1e-08
DECAY_RATE = 0.01
RATE_QKV = 0.03
RATE_OUT = 0.5
RATE_UP = 0.03
RATE_DOWN = 0.015
RATE_NORM = 0.2

F32 = jnp.float32
BF16 = jnp.bfloat16
NN = (((1,), (0,)), ((), ()))
NT = (((1,), (1,)), ((), ()))
TN = (((0,), (0,)), ((), ()))
VMEM = pl.BlockSpec(memory_space=pltpu.VMEM)


def dot(left, right, dims=NN):
    return lax.dot_general(left, right, dims, preferred_element_type=F32)


def widen(block, columns, lane):
    rows = block.shape[0]
    wide = jnp.concatenate([block.astype(F32), jnp.zeros((rows, HD), F32)], axis=1)
    for n, column in enumerate(columns):
        wide = jnp.where(lane == HD + n, column, wide)
    return wide.astype(BF16)


def minus_parts(column):
    high = column.astype(BF16).astype(F32)
    rest = column - high
    middle = rest.astype(BF16).astype(F32)
    return [-high, -middle, middle - rest]


def attend_kernel(heads, step, one_ref, weight_ref, bias_ref, qkv_ref, ctx_ref, lse_ref, keys):
    tokens = qkv_ref.shape[0]
    width = heads * HD
    lane = lax.broadcasted_iota(jnp.int32, (1, 2 * HD), 1)

    def project(n, _):
        rows = pl.ds(pl.multiple_of(n * step, step), step)
        qkv_ref[rows, :] = dot(one_ref[rows, :], weight_ref[...]).astype(BF16)
        return 0

    lax.fori_loop(0, tokens // step, project, 0)
    bias = bias_ref[...].T[:, 0:1]
    for h in range(heads):
        keys[h] = widen(qkv_ref[:, width + h * HD : width + (h + 1) * HD], [bias], lane)

    def block(n, _):
        rows = pl.ds(pl.multiple_of(n * step, step), step)
        outs = []
        stat = jnp.zeros((step, 2 * HD), F32)
        for h in range(heads):
            query = qkv_ref[rows, h * HD : (h + 1) * HD].astype(F32) * HD ** (-0.5)
            scores = dot(widen(query, [jnp.ones((step, 1), F32)], lane), keys[h], NT)
            top = jnp.max(scores, axis=1, keepdims=True)
            weights = jnp.exp(scores - top)
            total = jnp.sum(weights, axis=1, keepdims=True)
            values = qkv_ref[:, 2 * width + h * HD : 2 * width + (h + 1) * HD]
            outs.append((dot(weights.astype(BF16), values) / total).astype(BF16))
            stat = jnp.where(lane == h, top + jnp.log(total), stat)
        ctx_ref[rows, :] = jnp.concatenate(outs, axis=1)
        lse_ref[rows, :] = stat
        return 0

    lax.fori_loop(0, tokens // step, block, 0)


def attend(one, weight, bias, heads, step=1024):
    tokens = one.shape[0]
    return pl.pallas_call(
        functools.partial(attend_kernel, heads, step),
        out_shape=(
            jax.ShapeDtypeStruct((tokens, 3 * heads * HD), BF16),
            jax.ShapeDtypeStruct((tokens, heads * HD), BF16),
            jax.ShapeDtypeStruct((tokens, 2 * HD), F32),
        ),
        in_specs=[VMEM] * 3,
        out_specs=[VMEM] * 3,
        scratch_shapes=[pltpu.VMEM((heads, tokens, 2 * HD), BF16)],
        compiler_params=pltpu.CompilerParams(vmem_limit_bytes=48 * 2**20),
        cost_estimate=pl.CostEstimate(flops=0, bytes_accessed=1, transcendentals=0),
        name="attend",
    )(one, weight, bias)


def attend_back_kernel(
    heads,
    step,
    qkv_ref,
    bias_ref,
    ctx_ref,
    lse_ref,
    own_ref,
    mate_ref,
    weight_ref,
    out_ref,
    keys,
    values,
    dk,
    dv,
    grad_ref,
):
    tokens = qkv_ref.shape[0]
    width = heads * HD
    scale = HD ** (-0.5)
    lane = lax.broadcasted_iota(jnp.int32, (1, 2 * HD), 1)
    one = jnp.ones((tokens, 1), F32)
    bias = bias_ref[...].T[:, 0:1]
    half = tokens // 2
    for n, ref in enumerate((own_ref, mate_ref)):
        grad_ref[n * half : (n + 1) * half, :] = dot(ref[...], weight_ref[...], NT).astype(BF16)
    for h in range(heads):
        key = qkv_ref[:, width + h * HD : width + (h + 1) * HD]
        value = qkv_ref[:, 2 * width + h * HD : 2 * width + (h + 1) * HD]
        keys[h] = widen(key, [bias, one, one, one], lane)
        values[h] = widen(value, [one, one, one], lane)
    dk[...] = jnp.zeros_like(dk)
    dv[...] = jnp.zeros_like(dv)

    def block(n, _):
        rows = pl.ds(pl.multiple_of(n * step, step), step)
        outs = []
        ones = jnp.ones((step, 1), F32)
        for h in range(heads):
            cols = slice(h * HD, (h + 1) * HD)
            query = qkv_ref[rows, cols].astype(F32) * scale
            grad = grad_ref[rows, cols].astype(F32)
            delta = jnp.sum(grad * ctx_ref[rows, cols].astype(F32), axis=1, keepdims=True)
            lse = lse_ref[rows, h : h + 1]
            weights = jnp.exp(dot(widen(query, [ones] + minus_parts(lse), lane), keys[h], NT))
            slopes = dot(widen(grad, minus_parts(delta), lane), values[h], NT)
            slopes = (weights * slopes).astype(BF16)
            weights = weights.astype(BF16)
            key = qkv_ref[:, width + h * HD : width + (h + 1) * HD]
            outs.append((dot(slopes, key) * scale).astype(BF16))
            dk[h] += dot(query.T.astype(BF16), slopes)
            dv[h] += dot(grad.T.astype(BF16), weights)
        out_ref[rows, :width] = jnp.concatenate(outs, axis=1)
        return 0

    lax.fori_loop(0, tokens // step, block, 0)
    for place, total in ((1, dk), (2, dv)):
        turned = jnp.concatenate([total[h].T for h in range(heads)], axis=1)
        out_ref[:, place * width : (place + 1) * width] = turned.astype(BF16)


def attend_back(qkv, bias, ctx, lse, own, mate, weight, heads, step=1024):
    tokens = qkv.shape[0]
    return pl.pallas_call(
        functools.partial(attend_back_kernel, heads, step),
        out_shape=jax.ShapeDtypeStruct((tokens, 3 * heads * HD), BF16),
        in_specs=[VMEM] * 7,
        out_specs=VMEM,
        scratch_shapes=[pltpu.VMEM((heads, tokens, 2 * HD), BF16)] * 2
        + [pltpu.VMEM((heads, HD, tokens), F32)] * 2
        + [pltpu.VMEM((tokens, heads * HD), BF16)],
        compiler_params=pltpu.CompilerParams(vmem_limit_bytes=48 * 2**20),
        cost_estimate=pl.CostEstimate(flops=0, bytes_accessed=1, transcendentals=0),
        name="attend_back",
    )(qkv, bias, ctx, lse, own, mate, weight)


def swap(value, axis, bits):
    size = lax.axis_size(axis)
    return lax.ppermute(value, axis, [(i, i ^ bits) for i in range(size)])


def core_swap(value):
    return swap(value, "tensor", 1)


def side_swap(value):
    return swap(value, "tensor", 2)


def tie(*values):
    return lax.optimization_barrier(values)


def dp_split(size):
    fast = 2 if size < 16 else 4
    return size // fast, fast


def high_swap(value, k):
    return swap(value, "dp", k * dp_split(lax.axis_size("dp"))[1])


def gather_small(shard):
    size = lax.axis_size("dp")
    blocks = shard[None]
    bits = 1
    while bits < size:
        blocks = jnp.concatenate([blocks, swap(blocks, "dp", bits)])
        bits *= 2
    index = lax.axis_index("dp")
    return jnp.stack([blocks[index ^ n] for n in range(size)])


def spread(block):
    _, fast = dp_split(lax.axis_size("dp"))
    return [block] + [swap(block, "dp", j) for j in range(1, fast)]


def entries(k, line, at=None):
    return [(k, j, block, at if j else None) for j, block in enumerate(line)]


def joined_entries(ks, blocks, others):
    return [
        entry
        for n, (k, block) in enumerate(zip(ks, blocks, strict=True))
        for entry in entries(k, [block, *others], n)
    ]


def pack_kernel(qkv_ref, out_ref, packed_ref):
    rows, width = out_ref.shape
    step = width * rows // qkv_ref.shape[1]
    parts = [qkv_ref[n] for n in range(qkv_ref.shape[0])]
    turned = [out_ref[:, n : n + step] for n in range(0, width, step)]
    packed = jnp.concatenate([*parts, jnp.concatenate(turned, axis=0)], axis=1)
    packed_ref[...] = packed.astype(BF16)


def pack_first(qkv, out):
    rows = qkv.shape[1]
    shape = (rows, qkv.shape[0] * qkv.shape[2] + out.size // rows)
    if out.shape[0] % 8:
        step = out.shape[1] * out.shape[0] // rows
        turned = jnp.concatenate([out[:, n : n + step] for n in range(0, out.shape[1], step)])
        return jnp.concatenate([*qkv, turned], axis=1).astype(BF16)
    return pl.pallas_call(
        pack_kernel,
        out_shape=jax.ShapeDtypeStruct(shape, BF16),
        in_specs=[VMEM] * 2,
        out_specs=VMEM,
        compiler_params=pltpu.CompilerParams(vmem_limit_bytes=16 * 2**20),
        cost_estimate=pl.CostEstimate(flops=0, bytes_accessed=1, transcendentals=0),
        name="pack_first",
    )(qkv, out)


def assemble(blocks, cut=None):
    slow, fast = dp_split(lax.axis_size("dp"))
    rows, columns = blocks[0][2].shape[-2:]
    kind = blocks[0][2].dtype
    index = lax.axis_index("dp")
    place = jnp.stack([index // fast, index % fast]).astype(jnp.int32)
    where = [(k, j, at) for k, j, _, at in blocks]
    out_rows = rows * (columns - cut) // columns if cut else 0

    def kernel(place_ref, *refs):
        ins, outs = refs[: len(where)], refs[len(where) : -2]
        whole, sems = refs[-2:] if cut else (outs[0], refs[-1])
        copies = []
        for n, (source, (k, j, at)) in enumerate(zip(ins, where, strict=True)):
            target = (place_ref[0] ^ k) * fast + (place_ref[1] ^ j)
            source = source if at is None else source.at[at]
            copies.append(pltpu.make_async_copy(source, whole.at[target], sems.at[n]))
        for copy in copies:
            copy.start()
        for copy in copies:
            copy.wait()
        if cut:
            outs[0][...] = whole[:, :, :cut]
            if out_rows % 8:
                outs[1][...] = whole[:, :, cut:]
            else:
                turned = []
                for n in range(slow * fast):
                    block = whole[n, :, cut:].astype(F32)
                    parts = [block[m : m + out_rows] for m in range(0, rows, out_rows)]
                    turned.append(jnp.concatenate(parts, axis=1))
                outs[1][...] = jnp.concatenate(turned, axis=0).astype(kind)

    size = slow * fast
    full = (size, rows, columns)
    if not cut:
        shapes = [full]
    elif out_rows % 8:
        shapes = [(size, rows, cut), (size, rows, columns - cut)]
    else:
        shapes = [(size, rows, cut), (size * out_rows, columns)]
    outs = pl.pallas_call(
        kernel,
        out_shape=[jax.ShapeDtypeStruct(shape, kind) for shape in shapes],
        in_specs=[pl.BlockSpec(memory_space=pltpu.SMEM)]
        + [pl.BlockSpec(memory_space=pltpu.HBM)] * len(where),
        out_specs=[VMEM] * len(shapes),
        scratch_shapes=[
            pltpu.VMEM(full if cut else (8, 16, 128), kind),
            pltpu.SemaphoreType.DMA((len(where),)),
        ],
        compiler_params=pltpu.CompilerParams(vmem_limit_bytes=24 * 2**20),
        cost_estimate=pl.CostEstimate(flops=0, bytes_accessed=1, transcendentals=0),
        name="assemble",
    )(place, *[array for _, _, array, _ in blocks])
    outs = list(outs)
    if cut and out_rows % 8:
        turned = outs[1].reshape(size, rows // out_rows, out_rows, columns - cut)
        outs[1] = turned.transpose(0, 2, 1, 3).reshape(size * out_rows, columns)
    return [out.reshape(-1, out.shape[-1]) for out in outs]


def pick(total, k, j):
    slow, fast = dp_split(lax.axis_size("dp"))
    rows = total.shape[0] // (slow * fast)
    index = lax.axis_index("dp")
    start = (((index // fast) ^ k) * fast + ((index % fast) ^ j)) * rows
    return lax.dynamic_slice_in_dim(total, start, rows, 0)


def rows_first(value):
    return with_layout_constraint(value, Layout(tuple(range(value.ndim))))


def scatter_send(total, ks):
    _, fast = dp_split(lax.axis_size("dp"))
    return [
        swap(jnp.concatenate([rows_first(pick(total, k, j)) for k in ks]), "dp", j)
        for j in range(1, fast)
    ]


def scatter_lines(total, ks, received):
    lines = {}
    for n, k in enumerate(ks):
        line = pick(total, k, 0).astype(F32)
        rows = line.shape[0]
        for part in received:
            line = line + part[n * rows : (n + 1) * rows].astype(F32)
        lines[k] = rows_first(line.astype(BF16))
    return lines


def relay_ks():
    slow, _ = dp_split(lax.axis_size("dp"))
    return [1, *range(2, slow, 2)], [*range(3, slow, 2), 0]


def relay_send(lines):
    ks, _ = relay_ks()
    return high_swap(jnp.concatenate([lines[k] for k in ks]), 1)


def relay_split(received):
    ks, _ = relay_ks()
    rows = received.shape[0] // len(ks)
    return {k: received[n * rows : (n + 1) * rows] for n, k in enumerate(ks)}


def relay_last(lines, received):
    _, ks = relay_ks()
    got = relay_split(received)
    parts = [lines[0], got[1]]
    for k in ks[:-1]:
        line = lines[k].astype(F32) + got[k ^ 1].astype(F32)
        parts.append(high_swap(line.astype(BF16), k))
    return parts


def parts_sum(parts):
    return functools.reduce(jnp.add, [part.astype(F32) for part in parts])


def cores_sum(left, right, dims=NN):
    return own_sum(left, right, mates_part(left, right, dims), dims)


def mates_part(left, right, dims=NN):
    return core_swap(dot(left[left.shape[0] // 2 :], right, dims).astype(BF16))


def own_sum(left, right, mate, dims=NN):
    return dot(left[: left.shape[0] // 2], right, dims) + mate.astype(F32)


def side_send(value):
    half = value.shape[0] // 2
    return [side_swap(value[:half]), side_swap(value[half:])]


def join(parts):
    return jnp.concatenate(parts)


def with_mate(own):
    return jnp.concatenate([own, core_swap(own)])


def norm_kernel(step, *refs):
    *pieces, rows_ref, out_ref = refs
    gain, shift = rows_ref[0:1, :], rows_ref[1:2, :]
    at = 0
    for ref in pieces:
        for start in range(0, ref.shape[0], step):
            values = ref[start : start + step, :].astype(F32)
            centered = values - jnp.mean(values, axis=-1, keepdims=True)
            inverse = lax.rsqrt(jnp.mean(centered * centered, axis=-1, keepdims=True) + NORM_EPS)
            out_ref[at : at + step, :] = (centered * inverse * gain + shift).astype(BF16)
            at += step


def norm_tokens(pieces, rows, step=128):
    size, width = sum(v.shape[0] for v in pieces), pieces[0].shape[1]
    return pl.pallas_call(
        functools.partial(norm_kernel, step),
        out_shape=jax.ShapeDtypeStruct((size, width), BF16),
        in_specs=[VMEM] * (len(pieces) + 1),
        out_specs=VMEM,
        compiler_params=pltpu.CompilerParams(vmem_limit_bytes=24 * 2**20),
        cost_estimate=pl.CostEstimate(flops=0, bytes_accessed=1, transcendentals=0),
        name="norm_tokens",
    )(*pieces, rows)


def weight_grad_kernel(count, *refs):
    lefts, rights, out_ref = refs[:count], refs[count:-1], refs[-1]
    total = None
    at = 0
    for left in lefts:
        for start in range(0, left.shape[0], rights[0].shape[0]):
            right = rights[at]
            at += 1
            term = dot(left[start : start + right.shape[0], :], right[...], TN)
            total = term if total is None else total + term
    out_ref[...] = total.astype(BF16)


def weight_grad(lefts, rights, step=256):
    rows, columns = lefts[0].shape[1], rights[0].shape[1]
    return pl.pallas_call(
        functools.partial(weight_grad_kernel, len(lefts)),
        grid=(rows // step,),
        out_shape=jax.ShapeDtypeStruct((rows, columns), BF16),
        in_specs=[pl.BlockSpec((v.shape[0], step), lambda i: (0, i)) for v in lefts]
        + [pl.BlockSpec(v.shape, lambda i: (0, 0)) for v in rights],
        out_specs=pl.BlockSpec((step, columns), lambda i: (i, 0)),
        compiler_params=pltpu.CompilerParams(vmem_limit_bytes=40 * 2**20),
        cost_estimate=pl.CostEstimate(flops=0, bytes_accessed=1, transcendentals=0),
        name="weight_grad",
    )(*lefts, *rights)


def sum_all(value):
    size = lax.axis_size("dp")
    value = value + core_swap(value)
    steps = [("tensor", 2)] + [("dp", 1 << n) for n in range(size.bit_length() - 1)]
    for n in range(0, len(steps), 2):
        first = steps[n]
        if n + 1 == len(steps):
            value = value + swap(value, *first)
            continue
        second = steps[n + 1]
        if first[0] == second[0]:
            both = swap(value, first[0], first[1] | second[1])
        else:
            tensor = lax.axis_size("tensor")
            bits = first[1] | second[1] * tensor
            pairs = [(i, i ^ bits) for i in range(size * tensor)]
            both = lax.ppermute(value, ("dp", "tensor"), pairs)
        value = (value + swap(value, *first)) + (swap(value, *second) + both)
    return value


def layer_norm_parts(values, gain_row, shift_row):
    centered = values - jnp.mean(values, axis=-1, keepdims=True)
    inverse = lax.rsqrt(jnp.mean(centered * centered, axis=-1, keepdims=True) + NORM_EPS)
    normed = centered * inverse
    return (normed * gain_row + shift_row, normed, inverse)


def layer_norm_back(grad_normed, normed, inverse, gain_row):
    scaled = grad_normed * gain_row
    return inverse * (
        scaled
        - jnp.mean(scaled, axis=-1, keepdims=True)
        - normed * jnp.mean(scaled * normed, axis=-1, keepdims=True)
    )


def adam_update(master, grad_sum, moment_one, moment_two, step_rate, clip_factor):
    clipped = grad_sum * clip_factor
    one_new = BETA_FIRST * moment_one + (1.0 - BETA_FIRST) * clipped
    two_new = BETA_SECOND * moment_two + (1.0 - BETA_SECOND) * clipped * clipped
    one_hat = one_new / (1.0 - BETA_FIRST**STEP)
    two_hat = two_new / (1.0 - BETA_SECOND**STEP)
    master_new = master - step_rate * (
        one_hat / (jnp.sqrt(two_hat) + ADAM_EPS) + DECAY_RATE * master
    )
    return (master_new, one_new, two_new)


def first_back_kernel(tokens_ref, near_ref, far_ref, res_ref, rows_ref, out_ref, sums_ref):
    @pl.when(pl.program_id(0) == 0)
    def _():
        sums_ref[...] = jnp.zeros_like(sums_ref)

    values = tokens_ref[...].astype(F32)
    centered = values - jnp.mean(values, axis=-1, keepdims=True)
    inverse = lax.rsqrt(jnp.mean(centered * centered, axis=-1, keepdims=True) + NORM_EPS)
    normed = centered * inverse
    grad = near_ref[...] + far_ref[...].astype(F32)
    back = layer_norm_back(grad, normed, inverse, rows_ref[0:1, :])
    out_ref[...] = (res_ref[...] + back).astype(BF16)
    width = grad.shape[-1]
    sums_ref[0:8, :] += jnp.sum((grad * normed).reshape(-1, 8, width), axis=0)
    sums_ref[8:16, :] += jnp.sum(grad.reshape(-1, 8, width), axis=0)


def first_back(tokens, near, far, res, rows, step=128):
    size, width = tokens.shape
    block = pl.BlockSpec((step, width), lambda i: (i, 0))
    return pl.pallas_call(
        first_back_kernel,
        grid=(size // step,),
        out_shape=(
            jax.ShapeDtypeStruct((size, width), BF16),
            jax.ShapeDtypeStruct((16, width), F32),
        ),
        in_specs=[block] * 4 + [pl.BlockSpec(rows.shape, lambda i: (0, 0))],
        out_specs=[block, pl.BlockSpec((16, width), lambda i: (0, 0))],
        compiler_params=pltpu.CompilerParams(vmem_limit_bytes=60 * 2**20),
        cost_estimate=pl.CostEstimate(flops=0, bytes_accessed=1, transcendentals=0),
        name="first_back",
    )(tokens, near, far, res, rows)


def squares_kernel(counts, sums_ref, two_ref, early_ref, *refs):
    *parts, out_ref = refs
    width = two_ref.shape[1]
    total = early_ref[...]
    for count in counts:
        value = functools.reduce(jnp.add, [part[...].astype(F32) for part in parts[:count]])
        parts = parts[count:]
        total += jnp.sum(jnp.sum(value * value, axis=0, keepdims=True), axis=1, keepdims=True)
    for n in range(2):
        out_ref[n : n + 1, :width] = jnp.sum(
            sums_ref[8 * n : 8 * n + 8, :], axis=0, keepdims=True
        )
    out_ref[2:4, :width] = two_ref[...]
    out_ref[:, width:] = jnp.broadcast_to(total, (4, 128))


def squares_packed(sums, two, early, gradients):
    return pl.pallas_call(
        functools.partial(squares_kernel, [len(parts) for parts in gradients]),
        out_shape=jax.ShapeDtypeStruct((4, two.shape[1] + 128), F32),
        in_specs=[VMEM] * (3 + sum(len(parts) for parts in gradients)),
        out_specs=VMEM,
        compiler_params=pltpu.CompilerParams(vmem_limit_bytes=24 * 2**20),
        cost_estimate=pl.CostEstimate(flops=0, bytes_accessed=1, transcendentals=0),
        name="squares_packed",
    )(sums, two, early.reshape(1, 1), *[part for parts in gradients for part in parts])


def adam_kernel(rates, counts, packed_ref, *refs):
    *refs, norm_ref, shift_ref = refs
    width = packed_ref.shape[1] - 128
    rows = packed_ref[:, :width]
    squares = jnp.sum(jnp.sum(rows * rows, axis=0, keepdims=True), axis=1, keepdims=True)
    grad_norm = jnp.sqrt(packed_ref[0:1, width : width + 1] + squares)
    clip_factor = jnp.minimum(1.0, CLIP_LIMIT / grad_norm)
    norm_ref[...] = grad_norm
    ins, outs = refs[: -3 * len(rates)], refs[-3 * len(rates) :]
    at = 0
    for n, (rate, count) in enumerate(zip(rates, counts, strict=True)):
        master, one, two = ins[at : at + 3]
        parts = ins[at + 3 : at + 3 + count]
        at += 3 + count
        total = functools.reduce(jnp.add, [part[...].astype(F32) for part in parts])
        results = outs[3 * n : 3 * n + 3]
        if n == len(rates) - 1:
            shift_ref[...] = clip_factor * total[3:4, :]
        if master.ndim == 2:
            for out, value in zip(
                results,
                adam_update(master[...], total, one[...], two[...], rate, clip_factor),
                strict=True,
            ):
                out[...] = value
            continue
        width = master.shape[2]
        for c in range(master.shape[0]):
            grad = total[:, c * width : (c + 1) * width]
            values = adam_update(master[c], grad, one[c], two[c], rate, clip_factor)
            for out, value in zip(results, values, strict=True):
                out[c] = value


def adam_all(packed, weights):
    arrays = [v for master, one, two, parts, _ in weights for v in (master, one, two, *parts)]
    shapes = [master.shape for master, *_ in weights for _ in range(3)]
    shapes += [(1, 1), (1, weights[-1][0].shape[1])]
    outs = pl.pallas_call(
        functools.partial(
            adam_kernel, [rate for *_, rate in weights], [len(w[3]) for w in weights]
        ),
        out_shape=[jax.ShapeDtypeStruct(shape, F32) for shape in shapes],
        in_specs=[VMEM] * (len(arrays) + 1),
        out_specs=[VMEM] * len(shapes),
        compiler_params=pltpu.CompilerParams(vmem_limit_bytes=60 * 2**20),
        name="adam_all",
    )(packed, *arrays)
    return outs[-2], outs[-1], [outs[n : n + 3] for n in range(0, len(outs) - 2, 3)]


def gelu_parts(value):
    share = 0.5 + 0.5 * lax.erf(value * 0.5**0.5)
    slope = share + value * jnp.exp(-0.5 * value * value) * (0.5 / jnp.pi) ** 0.5
    return (value * share).astype(BF16), slope.astype(BF16)


def on_device(
    tokens,
    cotangent,
    lengths,
    key_mask,
    qkv_weight,
    out_weight,
    up_weight,
    down_weight,
    norm_params,
    qkv_first,
    qkv_second,
    out_first,
    out_second,
    up_first,
    up_second,
    down_first,
    down_second,
    norm_first,
    norm_second,
):
    own, width = tokens.shape
    cell = 2 * own
    heads = qkv_weight.shape[2] // HD
    dp, tensor = lax.axis_index("dp"), lax.axis_index("tensor")
    side, core = tensor // 2, tensor % 2

    norm_rows = norm_params.shape[1]

    positions = jnp.arange(cell, dtype=jnp.int32)
    key_valid = (positions[None, :] < lengths[:, None]) & (
        (key_mask == 1) | (positions[None, :] == 0)
    )
    bias = jnp.where(key_valid, 0.0, -1e30).astype(F32)
    bias = jnp.where(side == 0, bias, bias[::-1])
    bias = jnp.where(core == 0, bias, jnp.roll(bias, own, axis=1))
    bias_near, bias_far = [jnp.broadcast_to(row, (8, cell)) for row in bias]

    slow, _ = dp_split(lax.axis_size("dp"))
    odds, evens = list(range(1, slow, 2)), list(range(2, slow, 2))
    qkv_width = 3 * heads * HD
    head = own // 4
    first_low = pack_first(qkv_weight.transpose(1, 0, 2), out_weight)
    first = {k: high_swap(first_low, k) for k in odds}
    first_own = spread(first_low)
    top = own // 4
    side_top = side_swap(tokens[:top])
    mate_tokens = core_swap(tokens)
    norm_low, mate_tokens = tie(norm_params.astype(BF16), mate_tokens)
    norm_low = gather_small(norm_low)
    up_low, down_low = up_weight.astype(BF16), down_weight.astype(BF16)
    first, first_own, side_top, tokens, up_low, down_low = tie(
        first, first_own, side_top, tokens, up_low, down_low
    )
    for k in evens:
        first[k] = high_swap(first[k ^ 1], 1)
    first_lines = {k: spread(first[k]) for k in odds}
    side_rest = side_swap(tokens[top:])
    top_mate = core_swap(side_top)
    first, first_lines, up_low, down_low, cotangent, side_rest, top_mate, norm_low = tie(
        first, first_lines, up_low, down_low, cotangent, side_rest, top_mate, norm_low
    )
    for k in evens:
        first_lines[k] = spread(first[k])
    rest_mate = core_swap(side_rest)
    up = {k: high_swap(up_low, k) for k in odds}
    norm_values = jnp.moveaxis(norm_low, 0, 1).reshape(4, width).astype(F32)
    one_near = norm_tokens([tokens, mate_tokens], norm_values[:2])
    one_far = norm_tokens([side_top, side_rest, top_mate, rest_mate], norm_values[:2])
    cot_side = side_swap(cotangent)
    first_lines, one_far, one_near, up_low = tie(first_lines, one_far, one_near, up_low)
    up_own = spread(up_low)[1:]

    qkv_full, out_full = assemble(
        sum([entries(k, line) for k, line in first_lines.items()], entries(0, first_own)),
        qkv_width,
    )
    qkv_far, ctx_far, lse_far = attend(one_far, qkv_full, bias_far, heads)
    ctx_far, up, up_own, cot_side, down_low = tie(ctx_far, up, up_own, cot_side, down_low)
    for k in evens:
        up[k] = high_swap(up[k ^ 1], 1)
    up_others = spread(jnp.stack([up[k] for k in odds] + [down_low]))[1:]
    down = {k: high_swap(down_low, k) for k in odds}
    far_sum = cores_sum(ctx_far, out_full).astype(BF16)
    far_sum, one_near, qkv_full = tie(far_sum, one_near, qkv_full)
    out_far = side_swap(far_sum)
    qkv_near, ctx_near, lse_near = attend(one_near, qkv_full, bias_near, heads)
    ctx_near, out_far, up, up_others, down, cotangent, cot_side = tie(
        ctx_near, out_far, up, up_others, down, cotangent, cot_side
    )
    for k in evens:
        down[k] = high_swap(down[k ^ 1], 1)
    up_even = [spread(up[k])[1:] for k in evens]
    out_near = cores_sum(ctx_near, out_full)
    stream_in = tokens.astype(F32)
    residual = stream_in + (out_near + out_far.astype(F32))

    ln_two, normed_two, inverse_two = layer_norm_parts(residual, norm_values[2], norm_values[3])
    ln_two = ln_two.astype(BF16)
    ln_two, up_even, down = tie(ln_two, up_even, down)
    two_mate = core_swap(ln_two)
    two_side = side_swap(ln_two)
    places = odds + evens
    down_line = jnp.stack([down[k] for k in places])
    down_others = spread(down_line)[1:]
    grad_near = with_mate(cotangent)
    grad_far = with_mate(cot_side)
    two_near = join([ln_two, two_mate])
    two_near, grad_near, grad_far = tie(two_near, grad_near, grad_far)
    (up_full,) = assemble(
        entries(0, [up_low, *up_own])
        + joined_entries(odds, [up[k] for k in odds], up_others)
        + [
            entry
            for k, line in zip(evens, up_even, strict=True)
            for entry in entries(k, [up[k], *line])
        ]
    )
    hid_near, slope_near = gelu_parts(dot(two_near, up_full))
    hid_near, down_line, down_others, two_side = tie(hid_near, down_line, down_others, two_side)
    (down_full,) = assemble(
        [(0, 0, down_low, None)]
        + [(0, j + 1, other, len(odds)) for j, other in enumerate(up_others)]
        + [
            entry
            for n, k in enumerate(places)
            for entry in [(k, 0, down_line, n)]
            + [(k, j + 1, other, n) for j, other in enumerate(down_others)]
        ]
    )
    two_far = with_mate(two_side)
    pre_near = (dot(grad_near, down_full, NT) * slope_near.astype(F32)).astype(BF16)
    two_far, pre_near = tie(two_far, pre_near)
    hid_far, slope_far = gelu_parts(dot(two_far, up_full))
    pre_far = (dot(grad_far, down_full, NT) * slope_far.astype(F32)).astype(BF16)
    far_sum = cores_sum(pre_far, up_full, NT).astype(BF16)
    far_sum, pre_near, pre_far, hid_near, hid_far = tie(
        far_sum, pre_near, pre_far, hid_near, hid_far
    )
    back_far = side_swap(far_sum)
    back_near = cores_sum(pre_near, up_full, NT)
    back_near, hid_near, hid_far, grad_near, grad_far = tie(
        back_near, hid_near, hid_far, grad_near, grad_far
    )
    heavy, light = relay_ks()
    order = heavy + light
    grad_down = dot(join([hid_near, hid_far]), join([grad_near, grad_far]), TN).astype(BF16)
    grad_down, hid_near, hid_far = tie(grad_down, hid_near, hid_far)
    down_received = [scatter_send(grad_down, heavy)]
    last_terms = [dot(v[own:], down_full).astype(BF16) for v in (hid_far, hid_near)]
    last_terms, pre_near, pre_far = tie(last_terms, pre_near, pre_far)
    grad_up = weight_grad([two_near, two_far], [pre_near, pre_far])
    last_terms, grad_down, back_far, grad_up, down_received = tie(
        last_terms, grad_down, back_far, grad_up, down_received
    )
    grad_ln_two = back_near + back_far.astype(F32)
    grad_residual = cotangent.astype(F32) + layer_norm_back(
        grad_ln_two, normed_two, inverse_two, norm_values[2]
    )
    gain_two = jnp.sum(grad_ln_two * normed_two, axis=0)
    shift_two = jnp.sum(grad_ln_two, axis=0)

    res_low = grad_residual.astype(BF16)
    res_side = side_swap(res_low)
    res_mate = core_swap(res_low)
    last_mates = [core_swap(v) for v in last_terms]
    down_lines = scatter_lines(grad_down, heavy, down_received[0])
    res_mate, last_mates, down_lines = tie(res_mate, last_mates, down_lines)
    down_got = relay_send(down_lines)
    up_received = [scatter_send(grad_up, heavy)]
    dqkv_near = attend_back(
        qkv_near, bias_near, ctx_near, lse_near, res_low, res_mate, out_full, heads
    )
    dqkv_near, res_side, up_received, grad_up, down_got, grad_down, last_mates, hid_far = tie(
        dqkv_near, res_side, up_received, grad_up, down_got, grad_down, last_mates, hid_far
    )
    down_received.append(scatter_send(grad_down, light))
    res_side_mate = core_swap(res_side)
    up_lines = scatter_lines(grad_up, heavy, up_received[0])
    last_far = own_sum(hid_far, down_full, last_mates[0]).astype(BF16)
    grad_out = weight_grad(
        [ctx_near, ctx_far], [res_low, res_mate, res_side, res_side_mate], ctx_near.shape[1]
    )
    grad_out, last_far, grad_down, down_received[1] = tie(
        grad_out, last_far, grad_down, down_received[1]
    )
    down_lines.update(scatter_lines(grad_down, light, down_received[1]))
    res_side_mate, grad_out, down_lines, up_lines, last_far = tie(
        res_side_mate, grad_out, down_lines, up_lines, last_far
    )
    up_received.append(scatter_send(grad_up, light))
    out_received = scatter_send(grad_out, order)
    down_parts = relay_last(down_lines, down_got)
    up_got = relay_send(up_lines)
    last_side = side_swap(last_far)
    dqkv_far = attend_back(
        qkv_far, bias_far, ctx_far, lse_far, res_side, res_side_mate, out_full, heads
    )
    dqkv_far, up_got, up_received, grad_up, down_parts, grad_out, out_received, last_side = tie(
        dqkv_far, up_got, up_received, grad_up, down_parts, grad_out, out_received, last_side
    )

    grad_qkv = dot(join([one_near, one_far]), join([dqkv_near, dqkv_far]), TN).astype(BF16)
    grad_qkv, dqkv_far, dqkv_near, grad_up, up_received, grad_out, out_received = tie(
        rows_first(grad_qkv), dqkv_far, dqkv_near, grad_up, up_received, grad_out, out_received
    )
    up_lines.update(scatter_lines(grad_up, light, up_received[1]))
    out_lines = scatter_lines(grad_out, order, out_received)
    up_parts = relay_last(up_lines, up_got)
    out_got = relay_send(out_lines)
    received = [scatter_send(grad_qkv, heavy)]
    first_mates = [mates_part(v, qkv_full, NT) for v in (dqkv_far, dqkv_near)]
    far_sum = own_sum(dqkv_far, qkv_full, first_mates[0], NT).astype(BF16)
    far_sum, first_mates, grad_qkv, dqkv_near, hid_near = tie(
        far_sum, first_mates, grad_qkv, dqkv_near, hid_near
    )
    first_far = side_swap(far_sum)
    received.append(scatter_send(grad_qkv, light))
    first_near = own_sum(dqkv_near, qkv_full, first_mates[1], NT)
    first_near, received[0], grad_qkv, hid_near = tie(first_near, received[0], grad_qkv, hid_near)
    qkv_lines = scatter_lines(grad_qkv, heavy, received[0])
    qkv_got = relay_send(qkv_lines)
    last_near = own_sum(hid_near, down_full, last_mates[1])
    layer_out = (residual + (last_near + last_side.astype(F32))).astype(BF16)
    (
        received[1], qkv_got, qkv_lines, out_got, out_lines, layer_out, up_parts, down_parts,
        grad_qkv,
    ) = tie(
        received[1], qkv_got, qkv_lines, out_got, out_lines, layer_out, up_parts, down_parts,
        grad_qkv,
    )
    qkv_lines.update(scatter_lines(grad_qkv, light, received[1]))
    qkv_parts = relay_last(qkv_lines, qkv_got)
    out_parts = relay_last(out_lines, out_got)
    summed_up, summed_down = parts_sum(up_parts), parts_sum(down_parts)
    early_squares = jnp.sum(summed_up * summed_up) + jnp.sum(summed_down * summed_down)

    input_grad, sums_one = first_back(tokens, first_near, first_far, grad_residual, norm_values)
    rows_two = jnp.stack([gain_two, shift_two])
    qkv_parts, sums_one, input_grad, early_squares = tie(
        qkv_parts, sums_one, input_grad, early_squares
    )
    packed = squares_packed(sums_one, rows_two, early_squares, [qkv_parts, out_parts])
    packed = sum_all(packed)
    summed_norm = lax.dynamic_slice_in_dim(packed, dp * norm_rows, norm_rows, 1)
    grad_norm, shift_grad, results = adam_all(
        packed,
        [
            (*[v.transpose(1, 0, 2) for v in (qkv_weight, qkv_first, qkv_second)], qkv_parts, RATE_QKV),
            (out_weight, out_first, out_second, out_parts, RATE_OUT),
            (up_weight, up_first, up_second, up_parts, RATE_UP),
            (down_weight, down_first, down_second, down_parts, RATE_DOWN),
            (norm_params, norm_first, norm_second, [summed_norm], RATE_NORM),
        ],
    )
    grad_norm, shift_grad = grad_norm[0, 0], shift_grad[0]
    qkv_new, qkv_one, qkv_two = [v.transpose(1, 0, 2) for v in results[0]]
    out_new, out_one, out_two = results[1]
    up_new, up_one, up_two = results[2]
    down_new, down_one, down_two = results[3]
    norm_new, norm_one, norm_two = results[4]
    return (
        layer_out,
        input_grad,
        grad_norm,
        qkv_new,
        qkv_one,
        qkv_two,
        out_new,
        out_one,
        out_two,
        up_new,
        up_one,
        up_two,
        down_new,
        down_one,
        down_two,
        norm_new,
        norm_one,
        norm_two,
        shift_grad,
    )


def solution(mesh):
    tokens = P(("dp", "tensor"), None)
    columns = P("dp", None, "tensor")
    rows = P(("tensor", "dp"), None)
    both = P("dp", "tensor")
    norms = P(None, "dp")
    return jax.shard_map(
        on_device,
        mesh=mesh,
        in_specs=(tokens, tokens, P("dp"), P("dp", None), columns, rows, both, rows, norms)
        + (columns,) * 2
        + (rows,) * 2
        + (both,) * 2
        + (rows,) * 2
        + (norms,) * 2,
        out_specs=(tokens, tokens, P())
        + (columns,) * 3
        + (rows,) * 3
        + (both,) * 3
        + (rows,) * 3
        + (norms,) * 3
        + (P("dp"),),
        check_vma=False,
    )
```
